512 devices in a mesh: gx: 8 (over z), gy: 8 (over y), gz: 8 (over x, core).
Axes of the slice: x: 4, y: 8, z: 8, core: 2. Of those that a mesh axis runs over, the one named last changes fastest.
Arguments:
- fluid_state: float32 [5, 32, 128, 2048], P(None, 'gx', 'gy', 'gz'), may hold values from -4 to 20, as said below
- parcel_data: float32 [24, 24, 24, 8, 64], P('gx', 'gy', 'gz'), may hold values from -2 to 2, as said below
- host_element: int32 [24, 24, 24, 64], P('gx', 'gy', 'gz'), may hold values from 0 to 255
- slot_counts: int32 [24, 24, 24], P('gx', 'gy', 'gz'), may hold values from 0 to 64, as said below
Outputs:
- fluid_next: float32 [5, 32, 128, 2048], P(None, 'gx', 'gy', 'gz')
- parcel_velocity: float32 [24, 24, 24, 3, 64], P('gx', 'gy', 'gz')
The draws below stay inside these ranges and needn't reach their ends.
Inputs may be any that keep to these rules, and one draw needn't show every extreme that they name: `fluid_state`: every node holds the conserved variables of a state with density 0.6 to 2.7, velocity components within 1.2 and pressure 0.6 to 4.5. `parcel_data`: entries 0 to 2 along the fourth dimension are reference coordinates within -1 to 1, entries 3 to 5 velocities, entry 6 a relaxation time of 0.05 to 0.5, entry 7 a parcel mass of 0.01 to 0.1. `host_element`: element numbers (a * 4 + b) * 64 + c of the destination device's block. `slot_counts`: counts toward offsets that leave the grid are 0; in every draw some destination devices receive 64 live slots from each of their neighbouring sources, themselves included.
All inputs are finite; a program needn't handle non-finite values.
Results may differ from the reference program's by a relative error of at most 0.0003.
Values sent between devices are 32-bit elements; how exact they have to be, the bound alone decides.
No kernel may reach another device: no remote copies, remote signals or barrier semaphores. Data moves between devices by JAX's collectives and lax.ppermute only.
A program may use at most 64 MiB of HBM per device.

```python
import math
import jax
import jax.numpy as jnp
import numpy as np
from jax import lax

EX = 1
EY = 4
EZ = 64
CAP = 64
NODX = 32
NODY = 128
NODZ = 2048
SX = 24
SY = 24
SZ = 24
N_GX = 8
N_GY = 8
N_GZ = 8


GAS_GAMMA = 1.4


def draw_fluid_state(key, part):
    key = jax.random.fold_in(key, 11)
    key_list = jax.random.split(key, 4)
    shape_all = (NODX, NODY, NODZ)
    stream_pos = (lax.broadcasted_iota(jnp.int32, shape_all, 0).astype(jnp.float32) + 0.5) / NODX
    behind = stream_pos < 0.3
    rough_density = jnp.clip(0.15 * jax.random.normal(key_list[0], shape_all, jnp.float32), -0.4, 0.4)
    rough_pressure = jnp.clip(0.15 * jax.random.normal(key_list[1], shape_all, jnp.float32), -0.4, 0.4)
    velocity = jnp.clip(0.4 * jax.random.normal(key_list[2], (3,) + shape_all, jnp.float32), -1.2, 1.2)
    density = jnp.where(behind, 1.8, 1.0) * jnp.exp(rough_density)
    pressure = jnp.where(behind, 3.0, 1.0) * jnp.exp(rough_pressure)
    energy = pressure / (GAS_GAMMA - 1.0) + 0.5 * density * jnp.sum(velocity * velocity, axis=0)
    return jnp.concatenate([density[None], density[None] * velocity, energy[None]], axis=0)


def draw_parcel_data(key, part):
    key = jax.random.fold_in(key, 23)
    key_list = jax.random.split(key, 4)
    shape_all = (SX, SY, SZ, 8, CAP)
    channel = lax.broadcasted_iota(jnp.int32, shape_all, 3)
    ref_coord = jax.random.uniform(key_list[0], shape_all, jnp.float32, -1.0, 1.0)
    parcel_vel = jnp.clip(0.5 * jax.random.normal(key_list[1], shape_all, jnp.float32), -2.0, 2.0)
    relax_time = jnp.exp(jax.random.uniform(key_list[2], shape_all, jnp.float32, math.log(0.05), math.log(0.5)))
    parcel_mass = jnp.exp(jax.random.uniform(key_list[3], shape_all, jnp.float32, math.log(0.01), math.log(0.1)))
    return jnp.where(channel < 3, ref_coord, jnp.where(channel < 6, parcel_vel, jnp.where(channel == 6, relax_time, parcel_mass)))


def draw_slot_counts(key, part):
    key = jax.random.fold_in(key, 37)
    key_list = jax.random.split(key, 3)
    shape_all = (SX, SY, SZ)
    curtain_plane = jax.random.randint(key_list[0], (), 0, N_GX)
    index_x = lax.broadcasted_iota(jnp.int32, shape_all, 0)
    index_y = lax.broadcasted_iota(jnp.int32, shape_all, 1)
    index_z = lax.broadcasted_iota(jnp.int32, shape_all, 2)
    dest_x = index_x // 3 + index_x % 3 - 1
    dest_y = index_y // 3 + index_y % 3 - 1
    dest_z = index_z // 3 + index_z % 3 - 1
    outside = (dest_x < 0) | (dest_x >= N_GX) | (dest_y < 0) | (dest_y >= N_GY) | (dest_z < 0) | (dest_z >= N_GZ)
    staying = (index_x % 3 == 1) & (index_y % 3 == 1) & (index_z % 3 == 1)
    base_counts = jax.random.randint(key_list[1], shape_all, 0, max(1, CAP // 8) + 1)
    home_counts = jax.random.randint(key_list[2], shape_all, CAP // 2, CAP + 1)
    counts = jnp.where(staying, home_counts, base_counts)
    counts = jnp.where(dest_x == curtain_plane, CAP, counts)
    return jnp.where(outside, 0, counts).astype(jnp.int32)


def touch_ends(entries, key, smallest, largest):
    longest = entries.shape.index(max(entries.shape))
    spots = []
    for shift in (0, 1):
        where = [jax.random.randint(jax.random.fold_in(key, axis), (), 0, length) for axis, length in enumerate(entries.shape)]
        where[longest] = (where[longest] + shift) % entries.shape[longest]
        spots.append(tuple(where))
    return entries.at[spots[0]].set(smallest).at[spots[1]].set(largest)


def setup_inputs(seed: int = 0) -> dict:
    streams_of = jax.random.split(jax.random.key(seed), 5)
    return {
        "fluid_state": draw_fluid_state(jax.random.fold_in(streams_of[4], 71), 0),
        "parcel_data": draw_parcel_data(jax.random.fold_in(streams_of[4], 71), 0),
        "host_element": touch_ends(jax.random.randint(streams_of[2], (SX, SY, SZ, CAP), 0, EX * EY * EZ), jax.random.fold_in(streams_of[2], 1), 0, (EX * EY * EZ) - 1).astype(jnp.int32),
        "slot_counts": draw_slot_counts(jax.random.fold_in(streams_of[4], 71), 0),
    }


GAS_GAMMA = 1.4
COURANT = 0.5
INV_END = 6.0

def lobatto_tables():
    points = np.array([-1.0, -1.0 / np.sqrt(5.0), 1.0 / np.sqrt(5.0), 1.0])
    weights = np.array([1.0 / 6.0, 5.0 / 6.0, 5.0 / 6.0, 1.0 / 6.0])
    factor = np.array([np.prod([points[row_index] - points[col_index] for col_index in range(4) if col_index != row_index]) for row_index in range(4)])
    derivative = np.zeros((4, 4))
    for row_index in range(4):
        for col_index in range(4):
            if row_index != col_index:
                derivative[row_index, col_index] = factor[row_index] / (factor[col_index] * (points[row_index] - points[col_index]))
        derivative[row_index, row_index] = sum((1.0 / (points[row_index] - points[col_index]) for col_index in range(4) if col_index != row_index))
    return (points, weights, derivative)

def primitive(conserved):
    density = conserved[0]
    velocity = conserved[1:4] / density
    pressure = (GAS_GAMMA - 1.0) * (conserved[4] - 0.5 * density * lax.optimization_barrier(jnp.sum(velocity * velocity, axis=0)))
    sound_speed = jnp.sqrt(GAS_GAMMA * pressure / density)
    return (velocity, pressure, sound_speed)

def normal_flux(conserved, direction):
    velocity, pressure, sound_speed = primitive(conserved)
    normal_speed = velocity[direction]
    momentum = conserved[1:4] * normal_speed
    unit_vec = (jnp.arange(3) == direction).astype(jnp.float32)
    momentum = momentum + unit_vec.reshape((3,) + (1,) * (conserved.ndim - 1)) * pressure
    flux_vec = jnp.concatenate([conserved[direction + 1][None], momentum, ((conserved[4] + pressure) * normal_speed)[None]], axis=0)
    return (flux_vec, jnp.abs(normal_speed) + sound_speed)

def face_flux(left_side, right_side, direction):
    flux_left, speed_left = normal_flux(left_side, direction)
    flux_right, speed_right = normal_flux(right_side, direction)
    spread = jnp.maximum(speed_left, speed_right)
    common = 0.5 * (flux_left + flux_right) - 0.5 * spread * (right_side - left_side)
    return (common, flux_left, flux_right)

def mirror(conserved, direction):
    flip_sign = 1.0 - 2.0 * (jnp.arange(5) == direction + 1).astype(jnp.float32)
    return conserved * flip_sign.reshape((5,) + (1,) * (conserved.ndim - 1))

def surface_term(padded, direction, elem_along):
    axis_pos = direction + 1
    left_side = lax.slice_in_dim(padded, 0, 4 * elem_along + 1, 4, axis_pos)
    right_side = lax.slice_in_dim(padded, 1, 4 * elem_along + 2, 4, axis_pos)
    common, flux_left, flux_right = face_flux(left_side, right_side, direction)
    lower_corr = INV_END * (lax.slice_in_dim(common, 0, elem_along, 1, axis_pos) - lax.slice_in_dim(flux_right, 0, elem_along, 1, axis_pos))
    upper_corr = -INV_END * (lax.slice_in_dim(common, 1, elem_along + 1, 1, axis_pos) - lax.slice_in_dim(flux_left, 1, elem_along + 1, 1, axis_pos))
    zero_fill = jnp.zeros_like(lower_corr)
    stacked = jnp.stack([lower_corr, zero_fill, zero_fill, upper_corr], axis=axis_pos + 1)
    shape_out = list(lower_corr.shape)
    shape_out[axis_pos] = 4 * elem_along
    return stacked.reshape(shape_out)

def along_nodes(field_data, axis_pos, elem_along, derivative):
    dim_sizes = field_data.shape
    split_shape = dim_sizes[:axis_pos] + (elem_along, 4) + dim_sizes[axis_pos + 1:]
    applied = jnp.tensordot(field_data.reshape(split_shape), derivative, axes=([axis_pos + 1], [1]), precision=lax.Precision.HIGHEST)
    return jnp.moveaxis(applied, -1, axis_pos + 1).reshape(dim_sizes)

def fluid_rate(interior, rim_pairs, counts_elem, derivative):
    tendency = jnp.zeros_like(interior)
    for direction in range(3):
        axis_pos = direction + 1
        flux_vec, _ = normal_flux(interior, direction)
        tendency = tendency - along_nodes(flux_vec, axis_pos, counts_elem[direction], derivative)
        padded_dir = jnp.concatenate([rim_pairs[direction][0], interior, rim_pairs[direction][1]], axis=axis_pos)
        tendency = tendency + surface_term(padded_dir, direction, counts_elem[direction])
    return tendency

def lagrange_rows(ref_coord, points):
    basis_rows = []
    for node_index in range(4):
        product_term = jnp.ones_like(ref_coord)
        for other_index in range(4):
            if other_index != node_index:
                product_term = product_term * (ref_coord - float(points[other_index])) / float(points[node_index] - points[other_index])
        basis_rows.append(product_term)
    return jnp.stack(basis_rows, axis=0)

def parcel_forces(payload, gathered, live_mask, time_step, points):
    basis_x = lagrange_rows(payload[0], points)
    basis_y = lagrange_rows(payload[1], points)
    basis_z = lagrange_rows(payload[2], points)
    shape_weight = (basis_x[:, None, None, :] * basis_y[None, :, None, :] * basis_z[None, None, :, :]).reshape(64, payload.shape[1])
    fluid_vel = jnp.einsum('ps,spc->cs', shape_weight, gathered, precision=lax.Precision.HIGHEST)
    parcel_vel = payload[3:6]
    relax_time = jnp.where(live_mask > 0, payload[6], 1.0)
    acceleration = (fluid_vel - parcel_vel) / relax_time
    parcel_mass = payload[7] * live_mask
    source = jnp.concatenate([-parcel_mass * acceleration, (-parcel_mass * lax.optimization_barrier(jnp.sum(acceleration * parcel_vel, axis=0)))[None]], axis=0)
    new_velocity = (parcel_vel + time_step * acceleration) * live_mask
    return (shape_weight, source, new_velocity)

def mirror_pad(field_data, direction):
    axis_pos = direction + 1
    extent = field_data.shape[axis_pos]
    first_layer = lax.slice_in_dim(field_data, 0, 1, 1, axis_pos)
    last_layer = lax.slice_in_dim(field_data, extent - 1, extent, 1, axis_pos)
    return jnp.concatenate([mirror(first_layer, direction), field_data, mirror(last_layer, direction)], axis=axis_pos)

def top_speed(x_plane):
    velocity, pressure, sound_speed = primitive(x_plane)
    return jnp.max(jnp.sqrt(lax.optimization_barrier(jnp.sum(velocity * velocity, axis=0))) + sound_speed)

def reference(fluid_state, parcel_data, host_element, slot_counts):
    points, weights, derivative_np = lobatto_tables()
    derivative = jnp.asarray(derivative_np, dtype=jnp.float32)
    cube_weights = weights[:, None, None] * weights[None, :, None] * weights[None, None, :]
    inv_mass = jnp.asarray((1.0 / cube_weights).reshape(64), dtype=jnp.float32)
    plane_tops = lax.map(top_speed, jnp.moveaxis(fluid_state, 1, 0))
    time_step = COURANT * 2.0 / (7.0 * jnp.max(plane_tops))
    padded = mirror_pad(mirror_pad(mirror_pad(fluid_state, 0), 1), 2)
    device_count = N_GX * N_GY * N_GZ
    slot_total = 27 * CAP
    elem_count = EX * EY * EZ
    slot_index = lax.broadcasted_iota(jnp.int32, (SX, SY, SZ, CAP), 3)
    live_sent = slot_index < slot_counts[:, :, :, None]
    host_code = jnp.where(live_sent, host_element + 1, 0).astype(jnp.float32)
    packet = jnp.concatenate([parcel_data, host_code[:, :, :, None, :]], axis=3)
    packet = packet.reshape(N_GX, 3, N_GY, 3, N_GZ, 3, 9, CAP)
    packet = jnp.pad(packet, ((1, 1), (0, 0), (1, 1), (0, 0), (1, 1), (0, 0), (0, 0), (0, 0)))
    received_list = []
    for off_a in range(3):
        for off_b in range(3):
            for off_c in range(3):
                received_list.append(packet[off_a:off_a + N_GX, 2 - off_a, off_b:off_b + N_GY, 2 - off_b, off_c:off_c + N_GZ, 2 - off_c])
    received = jnp.stack(received_list, axis=3).reshape(device_count, 27, 9, CAP)
    payload_all = received.transpose(0, 2, 1, 3).reshape(device_count, 9, slot_total)

    def per_device(device_items):
        dev_index, payload_full = device_items
        block_x = (dev_index // (N_GY * N_GZ)).astype(jnp.int32)
        block_y = (dev_index // N_GZ % N_GY).astype(jnp.int32)
        block_z = (dev_index % N_GZ).astype(jnp.int32)
        starts = (jnp.zeros((), jnp.int32), block_x * (4 * EX), block_y * (4 * EY), block_z * (4 * EZ))
        block_data = lax.dynamic_slice(padded, starts, (5, 4 * EX + 2, 4 * EY + 2, 4 * EZ + 2))
        interior = block_data[:, 1:-1, 1:-1, 1:-1]
        rim_pairs = ((block_data[:, :1, 1:-1, 1:-1], block_data[:, -1:, 1:-1, 1:-1]), (block_data[:, 1:-1, :1, 1:-1], block_data[:, 1:-1, -1:, 1:-1]), (block_data[:, 1:-1, 1:-1, :1], block_data[:, 1:-1, 1:-1, -1:]))
        tendency = fluid_rate(interior, rim_pairs, (EX, EY, EZ), derivative)
        velocity, pressure, sound_speed = primitive(interior)
        node_vel = velocity.reshape(3, EX, 4, EY, 4, EZ, 4).transpose(1, 3, 5, 2, 4, 6, 0).reshape(elem_count, 64, 3)
        payload = payload_full[:8]
        host_ids = payload_full[8].astype(jnp.int32) - 1
        live_mask = (host_ids >= 0).astype(jnp.float32)
        host_safe = jnp.maximum(host_ids, 0).astype(jnp.int32)
        gathered = jnp.take(node_vel, host_safe, axis=0)
        shape_weight, source, new_velocity = parcel_forces(payload, gathered, live_mask, time_step, points)
        contrib = (source[:, None, :] * shape_weight[None, :, :] * inv_mass[None, :, None] * live_mask[None, None, :]).transpose(2, 1, 0)
        deposit = jax.ops.segment_sum(contrib, host_safe, num_segments=elem_count)
        deposit = deposit.reshape(EX, EY, EZ, 4, 4, 4, 4).transpose(6, 0, 3, 1, 4, 2, 5).reshape(4, 4 * EX, 4 * EY, 4 * EZ)
        tendency = tendency + jnp.concatenate([jnp.zeros_like(deposit[:1]), deposit], axis=0)
        velocity_block = new_velocity.reshape(3, 3, 3, 3, CAP).transpose(1, 2, 3, 0, 4)
        return (interior + time_step * tendency, velocity_block)
    fluid_blocks, velocity_blocks = lax.map(per_device, (jnp.arange(device_count, dtype=jnp.int32), payload_all))
    fluid_next = fluid_blocks.reshape(N_GX, N_GY, N_GZ, 5, 4 * EX, 4 * EY, 4 * EZ).transpose(3, 0, 4, 1, 5, 2, 6).reshape(5, NODX, NODY, NODZ)
    parcel_velocity = velocity_blocks.reshape(N_GX, N_GY, N_GZ, 3, 3, 3, 3, CAP).transpose(0, 3, 1, 4, 2, 5, 6, 7).reshape(SX, SY, SZ, 3, CAP)
    return (fluid_next, parcel_velocity)
```

```python
import jax
import jax.numpy as jnp
import numpy as np
from jax import lax
from jax.experimental import pallas as pl
from jax.experimental.pallas import tpu as pltpu
from jax.sharding import PartitionSpec as P

F32 = jnp.float32
BF16 = jnp.bfloat16
AXES = ("gx", "gy", "gz")
VMEM_BYTES = 24 * 1024 * 1024

NODES = np.array([-1.0, -1.0 / np.sqrt(5.0), 1.0 / np.sqrt(5.0), 1.0])
WEIGHTS = np.array([1.0 / 6.0, 5.0 / 6.0, 5.0 / 6.0, 1.0 / 6.0])


def derivative_table():
    factor = [np.prod([NODES[i] - NODES[j] for j in range(4) if j != i]) for i in range(4)]
    table = np.zeros((4, 4))
    for i in range(4):
        for j in range(4):
            if i != j:
                table[i, j] = factor[i] / (factor[j] * (NODES[i] - NODES[j]))
    return table


DERIV = derivative_table()
SCALE = [1.0 / np.prod([NODES[i] - NODES[j] for j in range(4) if j != i]) for i in range(4)]

GROUPS, TOP, FACE = 0, 9, 10


def by_pos(pos, values):
    out = jnp.full(pos.shape, float(values[3]), F32)
    for k in range(3):
        out = jnp.where(pos == k, float(values[k]), out)
    return out


def primitives(state):
    inverse = 1.0 / state[0]
    vel = [state[d + 1] * inverse for d in range(3)]
    square = vel[0] * vel[0] + vel[1] * vel[1] + vel[2] * vel[2]
    pressure = 0.4 * (state[4] - 0.5 * state[0] * square)
    sound = jnp.sqrt(1.4 * pressure * inverse)
    return vel, pressure, sound, square


def flux(state, vel, pressure, d):
    normal = vel[d]
    out = [state[d + 1]]
    for k in range(3):
        term = state[k + 1] * normal
        out.append(term + pressure if k == d else term)
    out.append((state[4] + pressure) * normal)
    return out


def side(state, d):
    vel, pressure, sound, _ = primitives(state)
    return flux(state, vel, pressure, d), jnp.abs(vel[d]) + sound


def pack_kernel(u_ref, data_ref, host_ref, count_ref, up_ref, down_ref, keep_ref, face_ref):
    slot = lax.broadcasted_iota(jnp.int32, (1, 64), 1)
    for a, out in ((2, up_ref), (0, down_ref), (1, keep_ref)):
        for b in range(3):
            for c in range(3):
                count = count_ref[a, b : b + 1, c : c + 1]
                host = host_ref[a, b, c : c + 1, :]
                code = jnp.where(slot < count, host + 1, 0).astype(F32)
                out[3 * b + c, :, 0:64] = data_ref[a, b, c]
                out[3 * b + c, :, 64:128] = jnp.broadcast_to(code, (8, 64))
    top = None
    for i in range(4):
        _, _, sound, square = primitives([u_ref[v, i] for v in range(5)])
        speed = jnp.sqrt(square) + sound
        top = speed if top is None else jnp.maximum(top, speed)
    top = jnp.maximum(top[:, :128], top[:, 128:])
    top = jnp.maximum(top[:8], top[8:])
    up_ref[TOP] = top
    down_ref[TOP] = top
    for v in range(5):
        for yh in range(2):
            for zh in range(2):
                tile = FACE + 4 * v + 2 * yh + zh
                ys, zs = slice(8 * yh, 8 * yh + 8), slice(128 * zh, 128 * zh + 128)
                up_ref[tile] = u_ref[v, 3, ys, zs]
                down_ref[tile] = u_ref[v, 0, ys, zs]
        for i in range(4):
            for zh in range(2):
                zs = slice(128 * zh, 128 * zh + 128)
                row = 4 * zh + i
                face_ref[v, row : row + 1, :] = u_ref[v, i, 15:16, zs]
                face_ref[5 + v, row : row + 1, :] = u_ref[v, i, 0:1, zs]
    lane = lax.broadcasted_iota(jnp.int32, (16, 128), 1)
    high = jnp.zeros((16, 128), F32)
    low = jnp.zeros((16, 128), F32)
    for v in range(5):
        for i in range(4):
            here = lane == 4 * v + i
            high = jnp.where(here, u_ref[v, i, :, 255:256], high)
            low = jnp.where(here, u_ref[v, i, :, 0:1], low)
    for yh in range(2):
        face_ref[10 + yh] = high[8 * yh : 8 * yh + 8]
        face_ref[12 + yh] = low[8 * yh : 8 * yh + 8]


def turn_y_kernel(lo_ref, hi_ref, own_ref, face_ref, mine_ref, up_ref, down_ref, keep_ref):
    for a, source in enumerate((lo_ref, own_ref, hi_ref)):
        for c in range(3):
            up_ref[3 * a + c] = source[6 + c]
            down_ref[3 * a + c] = source[c]
            keep_ref[3 * a + c] = source[3 + c]
    top = jnp.maximum(jnp.maximum(lo_ref[TOP], hi_ref[TOP]), mine_ref[TOP])
    up_ref[TOP] = top
    down_ref[TOP] = top
    for v in range(5):
        up_ref[FACE + v] = face_ref[v]
        down_ref[FACE + v] = face_ref[5 + v]


def turn_z_kernel(lo_ref, hi_ref, own_ref, face_ref, mine_ref, up_ref, down_ref, keep_ref):
    for b, source in enumerate((lo_ref, own_ref, hi_ref)):
        for a in range(3):
            up_ref[3 * a + b] = source[3 * a + 2]
            down_ref[3 * a + b] = source[3 * a]
            keep_ref[3 * a + b] = source[3 * a + 1]
    top = jnp.maximum(jnp.maximum(lo_ref[TOP], hi_ref[TOP]), mine_ref[TOP])
    up_ref[TOP] = top
    down_ref[TOP] = top
    for yh in range(2):
        up_ref[FACE + yh] = face_ref[10 + yh]
        down_ref[FACE + yh] = face_ref[12 + yh]


def wall(axis, last, own, received, sign_of):
    at = lax.axis_index(axis) == (lax.axis_size(axis) - 1 if last else 0)
    pick = jnp.full(received[0].shape, at.astype(jnp.int32), jnp.int32) == 1
    return [jnp.where(pick, sign_of(v) * own[v], received[v]) for v in range(5)]


def shift_rate(state, fluxes, speed, low, high, axis, pos, first, last, coef):
    count = state[0].shape[axis]
    low_state, low_flux, low_speed = low
    high_state, high_flux, high_speed = high
    at_low = pos == 0
    ends = at_low | (pos == 3)

    def beside(here, below, above):
        near = jnp.where(at_low, pltpu.roll(here, 1, axis), pltpu.roll(here, count - 1, axis))
        return jnp.where(first, below, jnp.where(last, above, near))

    spread = jnp.maximum(speed, beside(speed, low_speed, high_speed))
    spread = jnp.where(ends, 3.0 * spread, 0.0)
    out = []
    for v in range(5):
        value = fluxes[v]
        above = jnp.where(last, high_flux[v], pltpu.roll(value, count - 1, axis))
        below = jnp.where(first, low_flux[v], pltpu.roll(value, 1, axis))
        total = coef[1] * above + coef[-1] * below
        for d in (-3, -2, 2, 3):
            total = total + coef[d] * pltpu.roll(value, -d % count, axis)
        out.append(spread * (beside(state[v], low_state[v], high_state[v]) - state[v]) - total)
    return out


def rate_kernel(u_ref, xl_ref, xh_ref, yl_ref, yh_ref, zl_ref, zh_ref, face_ref, rate_ref, fx_ref, sx_ref):
    shape = (16, 256)
    row = lax.broadcasted_iota(jnp.int32, shape, 0)
    lane = lax.broadcasted_iota(jnp.int32, shape, 1)
    ypos, zpos = row & 3, lane & 3

    def coefs(pos):
        out = {}
        for d in (-3, -2, -1, 1, 2, 3):
            values = [DERIV[k, k + d] if 0 <= k + d < 4 else 0.0 for k in range(4)]
            if d == 1:
                values[3] = 3.0
            if d == -1:
                values[0] = -3.0
            out[d] = by_pos(pos, values)
        return out

    ycoef, zcoef = coefs(ypos), coefs(zpos)
    yfirst, ylast = row == 0, row == 15
    zfirst, zlast = lane == 0, lane == 255

    yflip = lambda v: -1.0 if v == 2 else 1.0
    ylow = wall("gy", False, [face_ref[5 + v] for v in range(5)], [yl_ref[FACE + v] for v in range(5)], yflip)
    yhigh = wall("gy", True, [face_ref[v] for v in range(5)], [yh_ref[FACE + v] for v in range(5)], yflip)
    ylow_flux, ylow_speed = side(ylow, 1)
    yhigh_flux, yhigh_speed = side(yhigh, 1)

    def columns(first_tile, ref):
        both = jnp.concatenate([ref[first_tile], ref[first_tile + 1]], axis=0)
        return [both if v == 0 else pltpu.roll(both, 128 - 4 * v, 1) for v in range(5)]

    zflip = lambda v: -1.0 if v == 3 else 1.0
    zlow = wall("gz", False, columns(12, face_ref), columns(FACE, zl_ref), zflip)
    zhigh = wall("gz", True, columns(10, face_ref), columns(FACE, zh_ref), zflip)
    zlow_flux, zlow_speed = side(zlow, 2)
    zhigh_flux, zhigh_speed = side(zhigh, 2)

    def pick_row(tile, i):
        return jnp.concatenate([tile[i : i + 1], tile[4 + i : 5 + i]], axis=1)

    for i in range(4):
        state = [u_ref[v, i] for v in range(5)]
        vel, pressure, sound, _ = primitives(state)
        xflux = flux(state, vel, pressure, 0)
        for v in range(5):
            fx_ref[v, i] = xflux[v]
        if i in (0, 3):
            sx_ref[i // 3] = jnp.abs(vel[0]) + sound
        low = ([pick_row(t, i) for t in ylow], [pick_row(t, i) for t in ylow_flux], pick_row(ylow_speed, i))
        high = ([pick_row(t, i) for t in yhigh], [pick_row(t, i) for t in yhigh_flux], pick_row(yhigh_speed, i))
        yrate = shift_rate(
            state, flux(state, vel, pressure, 1), jnp.abs(vel[1]) + sound,
            low, high, 0, ypos, yfirst, ylast, ycoef,
        )
        pick = lambda t: t[:, i : i + 1]
        low = ([pick(t) for t in zlow], [pick(t) for t in zlow_flux], pick(zlow_speed))
        high = ([pick(t) for t in zhigh], [pick(t) for t in zhigh_flux], pick(zhigh_speed))
        zrate = shift_rate(
            state, flux(state, vel, pressure, 2), jnp.abs(vel[2]) + sound,
            low, high, 1, zpos, zfirst, zlast, zcoef,
        )
        for v in range(5):
            rate_ref[v, i] = yrate[v] + zrate[v]

    xflip = lambda v: -1.0 if v == 1 else 1.0
    for half in range(2):
        for part in range(2):
            ys, zs = slice(8 * half, 8 * half + 8), slice(128 * part, 128 * part + 128)
            tile = FACE + 2 * half + part
            ends = []
            for last, i, ref in ((False, 0, xl_ref), (True, 3, xh_ref)):
                own = [u_ref[v, i, ys, zs] for v in range(5)]
                beyond = wall("gx", last, own, [ref[tile + 4 * v] for v in range(5)], xflip)
                far_flux, far_speed = side(beyond, 0)
                spread = 3.0 * jnp.maximum(sx_ref[i // 3, ys, zs], far_speed)
                sign = -3.0 if last else 3.0
                ends.append([sign * far_flux[v] + spread * (beyond[v] - own[v]) for v in range(5)])
            for v in range(5):
                f = [fx_ref[v, i, ys, zs] for i in range(4)]
                for j in range(4):
                    total = rate_ref[v, j, ys, zs]
                    for i in range(4):
                        if i != j:
                            total = total - float(DERIV[j, i]) * f[i]
                    if j == 0:
                        total = total + ends[0][v]
                    if j == 3:
                        total = total + ends[1][v]
                    rate_ref[v, j, ys, zs] = total


def split(value):
    high = value.astype(BF16)
    return high, (value - high.astype(F32)).astype(BF16)


def parcel_kernel(u_ref, zl_ref, zh_ref, own_ref, dep_ref, base_ref, acc_ref, tiles, vel_hi, vel_lo, z_hi, z_lo, a_hi, a_lo, total):
    for c, source in enumerate((zl_ref, own_ref, zh_ref)):
        for ab in range(9):
            tiles[3 * ab + c] = source[ab]
    tiles[27] = jnp.zeros((8, 128), F32)
    for i in range(4):
        inverse = 1.0 / u_ref[0, i]
        for d in range(3):
            high, low = split(u_ref[d + 1, i] * inverse)
            start = 16 * (4 * d + i)
            vel_hi[start : start + 16, :] = high
            vel_lo[start : start + 16, :] = low
    total[...] = jnp.zeros((256, 256), F32)
    left = lax.broadcasted_iota(jnp.int32, (8, 128), 1) < 64
    sub8 = lax.broadcasted_iota(jnp.int32, (8, 256), 0)
    sub16 = lax.broadcasted_iota(jnp.int32, (16, 256), 0)
    pos, block = sub16 & 3, sub16 >> 2
    weight_y = by_pos(pos, 1.0 / WEIGHTS)
    inner = float(NODES[2])

    def chunk(j, carry):
        fields, codes = [], []
        for p in range(2):
            first, second = tiles[4 * j + 2 * p], tiles[4 * j + 2 * p + 1]
            fields.append(jnp.where(left, first, pltpu.roll(second, 64, 1)))
            codes.append(jnp.where(left, pltpu.roll(first, 64, 1), second))
        field = jnp.concatenate(fields, axis=1)
        code = jnp.concatenate(codes, axis=1)
        live = code > 0.5
        host = code.astype(jnp.int32) - 1
        host = jnp.concatenate([host, host], axis=0)
        row_y, col_z = host >> 6, host & 63
        outer = (field + 1.0) * (field - 1.0)
        middle = (field + inner) * (field - inner)
        basis = [
            float(SCALE[0]) * middle * (field - 1.0),
            float(SCALE[1]) * outer * (field - inner),
            float(SCALE[2]) * outer * (field + inner),
            float(SCALE[3]) * middle * (field + 1.0),
        ]

        def spread(r):
            rows = [jnp.broadcast_to(basis[k][r : r + 1], (16, 256)) for k in range(4)]
            return jnp.where(pos == 0, rows[0], jnp.where(pos == 1, rows[1], jnp.where(pos == 2, rows[2], rows[3])))

        in_y = jnp.where(row_y == block, spread(1), 0.0)
        in_z = spread(2)
        in_z_hi = in_z.astype(BF16).astype(F32)
        in_z_lo = in_z - in_z_hi
        offset = col_z - block
        for t in range(16):
            here = offset == 4 * t
            z_hi[16 * t : 16 * t + 16, :] = jnp.where(here, in_z_hi, 0.0).astype(BF16)
            z_lo[16 * t : 16 * t + 16, :] = jnp.where(here, in_z_lo, 0.0).astype(BF16)
        wide = jnp.dot(vel_hi[...], z_hi[...], preferred_element_type=F32)
        wide += jnp.dot(vel_lo[...], z_hi[...], preferred_element_type=F32)
        wide += jnp.dot(vel_hi[...], z_lo[...], preferred_element_type=F32)
        in_xy = [basis[i][0:1] * in_y for i in range(4)]
        seen = []
        for d in range(3):
            mixed = None
            for i in range(4):
                start = 16 * (4 * d + i)
                term = in_xy[i] * wide[start : start + 16]
                mixed = term if mixed is None else mixed + term
            seen.append(jnp.sum(mixed, axis=0, keepdims=True))
        fluid = jnp.where(sub8 == 0, seen[0], jnp.where(sub8 == 1, seen[1], seen[2]))
        speed = pltpu.roll(field, 5, 0)
        keep = live & (sub8 < 3)
        relax = jnp.where(live[0:1], field[6:7], 1.0)
        force = jnp.where(keep, (fluid - speed) / relax, 0.0)
        base = jnp.where(keep, speed, 0.0)
        for p in range(2):
            base_ref[2 * j + p] = base[:, 128 * p : 128 * p + 128]
            acc_ref[2 * j + p] = force[:, 128 * p : 128 * p + 128]
        mass = field[7:8]
        push = -mass * force
        work = -mass * jnp.sum(force * base, axis=0, keepdims=True)
        sources = [push[0:1], push[1:2], push[2:3], work]
        for i in range(4):
            scaled = in_xy[i] * (weight_y * float(1.0 / WEIGHTS[i]))
            for d in range(4):
                high, low = split(sources[d] * scaled)
                start = 16 * (4 * d + i)
                a_hi[start : start + 16, :] = high
                a_lo[start : start + 16, :] = low
        lanes = (((1,), (1,)), ((), ()))
        out = lax.dot_general(a_hi[...], z_hi[...], lanes, preferred_element_type=F32)
        out += lax.dot_general(a_lo[...], z_hi[...], lanes, preferred_element_type=F32)
        out += lax.dot_general(a_hi[...], z_lo[...], lanes, preferred_element_type=F32)
        total[...] += out
        return carry

    lax.fori_loop(0, 7, chunk, 0)
    zpos = lax.broadcasted_iota(jnp.int32, (16, 256), 1) & 3
    weight_z = by_pos(zpos, 1.0 / WEIGHTS)
    for d in range(4):
        for i in range(4):
            start = 16 * (4 * d + i)
            dep_ref[d, i] = total[start : start + 16, :] * weight_z


def finish_kernel(u_ref, rate_ref, dep_ref, top_ref, base_ref, acc_ref, next_ref, vel_ref):
    top = jnp.max(jnp.max(top_ref[...], axis=0, keepdims=True), axis=1, keepdims=True)
    step = 1.0 / (7.0 * jnp.broadcast_to(top, (8, 256)))
    step16 = jnp.concatenate([step, step], axis=0)
    for v in range(5):
        for i in range(4):
            rate = rate_ref[v, i]
            if v > 0:
                rate = rate + dep_ref[v - 1, i]
            next_ref[v, i] = u_ref[v, i] + step16 * rate
    small = step[:, :128]
    for pair in range(14):
        value = base_ref[pair] + small * acc_ref[pair]
        for h in range(2):
            g = 2 * pair + h
            if g < 27:
                vel_ref[g // 9, g // 3 % 3, g % 3] = value[0:3, 64 * h : 64 * h + 64]


def shifted(value, axis, by):
    count = lax.axis_size(axis)
    return lax.ppermute(value, axis, [(i, (i + by) % count) for i in range(count)])


def call(kernel, outs, scratch=(), flops=10**6, nbytes=10**6):
    return pl.pallas_call(
        kernel,
        out_shape=outs,
        scratch_shapes=list(scratch),
        compiler_params=pltpu.CompilerParams(vmem_limit_bytes=VMEM_BYTES),
        cost_estimate=pl.CostEstimate(flops=flops, bytes_accessed=nbytes, transcendentals=0),
    )


def tiles_of(n):
    return jax.ShapeDtypeStruct((n, 8, 128), F32)


def local(fluid_state, parcel_data, host_element, slot_counts):
    x_up, x_down, keep_x, faces = call(pack_kernel, (tiles_of(30), tiles_of(30), tiles_of(9), tiles_of(14)))(
        fluid_state, parcel_data, host_element, slot_counts
    )
    x_low, x_high = shifted(x_up, "gx", 1), shifted(x_down, "gx", -1)
    y_up, y_down, keep_y = call(turn_y_kernel, (tiles_of(15), tiles_of(15), tiles_of(9)))(
        x_low, x_high, keep_x, faces, x_up
    )
    y_low, y_high = shifted(y_up, "gy", 1), shifted(y_down, "gy", -1)
    z_up, z_down, keep_z = call(turn_z_kernel, (tiles_of(12), tiles_of(12), tiles_of(9)))(
        y_low, y_high, keep_y, faces, y_up
    )
    z_low, z_high = shifted(z_up, "gz", 1), shifted(z_down, "gz", -1)
    top = jnp.maximum(jnp.maximum(z_low[TOP], z_high[TOP]), z_up[TOP])
    for axis in AXES:
        top = jnp.maximum(jnp.maximum(shifted(top, axis, 3), shifted(top, axis, -3)), top)
    field = jax.ShapeDtypeStruct((5, 4, 16, 256), F32)
    rate = call(
        rate_kernel, field, [pltpu.VMEM((5, 4, 16, 256), F32), pltpu.VMEM((2, 16, 256), F32)],
    )(fluid_state, x_low, x_high, y_low, y_high, z_low, z_high, faces)
    deposit, base, acc = call(
        parcel_kernel,
        (jax.ShapeDtypeStruct((4, 4, 16, 256), F32), tiles_of(14), tiles_of(14)),
        [
            pltpu.VMEM((28, 8, 128), F32),
            pltpu.VMEM((192, 256), BF16),
            pltpu.VMEM((192, 256), BF16),
            pltpu.VMEM((256, 256), BF16),
            pltpu.VMEM((256, 256), BF16),
            pltpu.VMEM((256, 256), BF16),
            pltpu.VMEM((256, 256), BF16),
            pltpu.VMEM((256, 256), F32),
        ],
    )(fluid_state, z_low, z_high, keep_z)
    return call(finish_kernel, (field, jax.ShapeDtypeStruct((3, 3, 3, 3, 64), F32)))(
        fluid_state, rate, deposit, top, base, acc
    )


def solution(mesh):
    placed = (
        P(None, "gx", "gy", "gz"),
        P("gx", "gy", "gz", None, None),
        P("gx", "gy", "gz", None),
        P("gx", "gy", "gz"),
    )
    return jax.shard_map(
        local,
        mesh=mesh,
        in_specs=placed,
        out_specs=(P(None, "gx", "gy", "gz"), P("gx", "gy", "gz", None, None)),
        check_vma=False,
    )
```

```python
import jax
import jax.numpy as jnp
import numpy as np
from jax import lax
from jax.experimental import pallas as pl
from jax.experimental.pallas import tpu as pltpu
from jax.sharding import PartitionSpec as P

F32 = jnp.float32
BF16 = jnp.bfloat16
VMEM_BYTES = 24 * 1024 * 1024

NODES = np.array([-1.0, -1.0 / np.sqrt(5.0), 1.0 / np.sqrt(5.0), 1.0])
WEIGHTS = np.array([1.0 / 6.0, 5.0 / 6.0, 5.0 / 6.0, 1.0 / 6.0])


def derivative_table():
    factor = [np.prod([NODES[i] - NODES[j] for j in range(4) if j != i]) for i in range(4)]
    table = np.zeros((4, 4))
    for i in range(4):
        for j in range(4):
            if i != j:
                table[i, j] = factor[i] / (factor[j] * (NODES[i] - NODES[j]))
    return table


DERIV = derivative_table()
SCALE = [1.0 / np.prod([NODES[i] - NODES[j] for j in range(4) if j != i]) for i in range(4)]

FACE = 9


def by_pos(pos, values):
    out = jnp.full(pos.shape, float(values[3]), F32)
    for k in range(3):
        out = jnp.where(pos == k, float(values[k]), out)
    return out


def primitives(state):
    inverse = 1.0 / state[0]
    vel = [state[d + 1] * inverse for d in range(3)]
    square = vel[0] * vel[0] + vel[1] * vel[1] + vel[2] * vel[2]
    pressure = 0.4 * (state[4] - 0.5 * state[0] * square)
    sound = jnp.sqrt(1.4 * pressure * inverse)
    return vel, pressure, sound, square


def flux(state, vel, pressure, d):
    normal = vel[d]
    out = [state[d + 1]]
    for k in range(3):
        term = state[k + 1] * normal
        out.append(term + pressure if k == d else term)
    out.append((state[4] + pressure) * normal)
    return out


def side(state, d):
    vel, pressure, sound, _ = primitives(state)
    return flux(state, vel, pressure, d), jnp.abs(vel[d]) + sound


def parity(axis):
    return lax.axis_index(axis) & 1


def lows_highs(axis, first_ref, second_ref):
    odd = jnp.full((8, 128), parity(axis), jnp.int32) == 1

    def low(tile):
        return jnp.where(odd, first_ref[tile], second_ref[tile])

    def high(tile):
        return jnp.where(odd, second_ref[tile], first_ref[tile])

    return low, high


def pack_kernel(u_hbm, data_hbm, host_hbm, count_hbm, first_ref, second_ref, keep_ref, face_ref, top_ref, u_ref, data_ref, host_ref, count_ref, sems):
    copies = [
        pltpu.make_async_copy(source, target, sems.at[k])
        for k, (source, target) in enumerate(
            ((u_hbm, u_ref), (data_hbm, data_ref), (host_hbm, host_ref), (count_hbm, count_ref))
        )
    ]
    for copy in copies:
        copy.start()
    for copy in copies:
        copy.wait()
    top = None
    for i in range(4):
        _, _, sound, square = primitives([u_ref[v, i] for v in range(5)])
        speed = jnp.sqrt(square) + sound
        top = speed if top is None else jnp.maximum(top, speed)
    top = jnp.maximum(top[:, :128], top[:, 128:])
    top_ref[...] = jnp.broadcast_to(jnp.max(top, axis=0, keepdims=True), (8, 128))
    slot = lax.broadcasted_iota(jnp.int32, (1, 64), 1)
    odd = parity("gx")
    for a, out in ((2 - 2 * odd, first_ref), (2 * odd, second_ref), (1, keep_ref)):
        for b in range(3):
            for c in range(3):
                count = count_ref[a, b : b + 1, c : c + 1]
                host = host_ref[a, b, c : c + 1, :]
                code = jnp.where(slot < count, host + 1, 0).astype(F32)
                out[3 * b + c, :, 0:64] = data_ref[a, b, c]
                out[3 * b + c, :, 64:128] = jnp.broadcast_to(code, (8, 64))
    for v in range(5):
        for yh in range(2):
            for zh in range(2):
                tile = FACE + 4 * v + 2 * yh + zh
                ys, zs = slice(8 * yh, 8 * yh + 8), slice(128 * zh, 128 * zh + 128)
                first_ref[tile] = u_ref[v, 3 - 3 * odd, ys, zs]
                second_ref[tile] = u_ref[v, 3 * odd, ys, zs]
        for i in range(4):
            for zh in range(2):
                zs = slice(128 * zh, 128 * zh + 128)
                row = 4 * zh + i
                face_ref[v, row : row + 1, :] = u_ref[v, i, 15:16, zs]
                face_ref[5 + v, row : row + 1, :] = u_ref[v, i, 0:1, zs]
    lane = lax.broadcasted_iota(jnp.int32, (16, 128), 1)
    high = jnp.zeros((16, 128), F32)
    low = jnp.zeros((16, 128), F32)
    for v in range(5):
        for i in range(4):
            here = lane == 4 * v + i
            high = jnp.where(here, u_ref[v, i, :, 255:256], high)
            low = jnp.where(here, u_ref[v, i, :, 0:1], low)
    for yh in range(2):
        face_ref[10 + yh] = high[8 * yh : 8 * yh + 8]
        face_ref[12 + yh] = low[8 * yh : 8 * yh + 8]


def turn_y_kernel(x1_ref, x2_ref, own_ref, face_ref, tops_ref, first_ref, second_ref, keep_ref, top_ref):
    top_ref[...] = jnp.max(tops_ref[...], axis=0, keepdims=True)
    low, high = lows_highs("gx", x1_ref, x2_ref)
    odd = parity("gy")
    for a, source in enumerate((low, lambda t: own_ref[t], high)):
        for c in range(3):
            first_ref[3 * a + c] = source(6 - 6 * odd + c)
            second_ref[3 * a + c] = source(6 * odd + c)
            keep_ref[3 * a + c] = source(3 + c)
    for v in range(5):
        first_ref[FACE + v] = face_ref[v + 5 * odd]
        second_ref[FACE + v] = face_ref[v + 5 - 5 * odd]


def turn_z_kernel(y1_ref, y2_ref, own_ref, face_ref, tops_ref, first_ref, second_ref, keep_ref, top_ref):
    top_ref[...] = jnp.max(tops_ref[...], axis=0, keepdims=True)
    low, high = lows_highs("gy", y1_ref, y2_ref)
    odd = parity("gz")
    for b, source in enumerate((low, lambda t: own_ref[t], high)):
        for a in range(3):
            first_ref[3 * a + b] = source(3 * a + 2 - 2 * odd)
            second_ref[3 * a + b] = source(3 * a + 2 * odd)
            keep_ref[3 * a + b] = source(3 * a + 1)
    for yh in range(2):
        first_ref[FACE + yh] = face_ref[10 + 2 * odd + yh]
        second_ref[FACE + yh] = face_ref[12 - 2 * odd + yh]


def wall(axis, last, own, received, sign_of):
    at = lax.axis_index(axis) == (lax.axis_size(axis) - 1 if last else 0)
    pick = jnp.full(received[0].shape, at.astype(jnp.int32), jnp.int32) == 1
    return [jnp.where(pick, sign_of(v) * own[v], received[v]) for v in range(5)]


def shift_rate(state, fluxes, speed, low, high, axis, pos, first, last, coef):
    count = state[0].shape[axis]
    low_state, low_flux, low_speed = low
    high_state, high_flux, high_speed = high
    at_low = pos == 0
    ends = at_low | (pos == 3)

    def beside(here, below, above):
        near = jnp.where(at_low, pltpu.roll(here, 1, axis), pltpu.roll(here, count - 1, axis))
        return jnp.where(first, below, jnp.where(last, above, near))

    spread = jnp.maximum(speed, beside(speed, low_speed, high_speed))
    spread = jnp.where(ends, 3.0 * spread, 0.0)
    out = []
    for v in range(5):
        value = fluxes[v]
        above = jnp.where(last, high_flux[v], pltpu.roll(value, count - 1, axis))
        below = jnp.where(first, low_flux[v], pltpu.roll(value, 1, axis))
        total = coef[1] * above + coef[-1] * below
        for d in (-3, -2, 2, 3):
            total = total + coef[d] * pltpu.roll(value, -d % count, axis)
        out.append(spread * (beside(state[v], low_state[v], high_state[v]) - state[v]) - total)
    return out


def rate_kernel(u_ref, x1_ref, x2_ref, y1_ref, y2_ref, z1_ref, z2_ref, face_ref, rate_ref, fx_ref, sx_ref):
    x_side = lows_highs("gx", x1_ref, x2_ref)
    y_side = lows_highs("gy", y1_ref, y2_ref)
    z_side = lows_highs("gz", z1_ref, z2_ref)
    shape = (16, 256)
    row = lax.broadcasted_iota(jnp.int32, shape, 0)
    lane = lax.broadcasted_iota(jnp.int32, shape, 1)
    ypos, zpos = row & 3, lane & 3

    def coefs(pos):
        out = {}
        for d in (-3, -2, -1, 1, 2, 3):
            values = [DERIV[k, k + d] if 0 <= k + d < 4 else 0.0 for k in range(4)]
            if d == 1:
                values[3] = 3.0
            if d == -1:
                values[0] = -3.0
            out[d] = by_pos(pos, values)
        return out

    ycoef, zcoef = coefs(ypos), coefs(zpos)
    yfirst, ylast = row == 0, row == 15
    zfirst, zlast = lane == 0, lane == 255

    yflip = lambda v: -1.0 if v == 2 else 1.0
    ylow = wall("gy", False, [face_ref[5 + v] for v in range(5)], [y_side[0](FACE + v) for v in range(5)], yflip)
    yhigh = wall("gy", True, [face_ref[v] for v in range(5)], [y_side[1](FACE + v) for v in range(5)], yflip)
    ylow_flux, ylow_speed = side(ylow, 1)
    yhigh_flux, yhigh_speed = side(yhigh, 1)

    def columns(first_tile, source):
        both = jnp.concatenate([source(first_tile), source(first_tile + 1)], axis=0)
        return [both if v == 0 else pltpu.roll(both, 128 - 4 * v, 1) for v in range(5)]

    own = lambda t: face_ref[t]
    zflip = lambda v: -1.0 if v == 3 else 1.0
    zlow = wall("gz", False, columns(12, own), columns(FACE, z_side[0]), zflip)
    zhigh = wall("gz", True, columns(10, own), columns(FACE, z_side[1]), zflip)
    zlow_flux, zlow_speed = side(zlow, 2)
    zhigh_flux, zhigh_speed = side(zhigh, 2)

    def pick_row(tile, i):
        return jnp.concatenate([tile[i : i + 1], tile[4 + i : 5 + i]], axis=1)

    for i in range(4):
        state = [u_ref[v, i] for v in range(5)]
        vel, pressure, sound, _ = primitives(state)
        xflux = flux(state, vel, pressure, 0)
        for v in range(5):
            fx_ref[v, i] = xflux[v]
        if i in (0, 3):
            sx_ref[i // 3] = jnp.abs(vel[0]) + sound
        low = ([pick_row(t, i) for t in ylow], [pick_row(t, i) for t in ylow_flux], pick_row(ylow_speed, i))
        high = ([pick_row(t, i) for t in yhigh], [pick_row(t, i) for t in yhigh_flux], pick_row(yhigh_speed, i))
        yrate = shift_rate(
            state, flux(state, vel, pressure, 1), jnp.abs(vel[1]) + sound,
            low, high, 0, ypos, yfirst, ylast, ycoef,
        )
        pick = lambda t: t[:, i : i + 1]
        low = ([pick(t) for t in zlow], [pick(t) for t in zlow_flux], pick(zlow_speed))
        high = ([pick(t) for t in zhigh], [pick(t) for t in zhigh_flux], pick(zhigh_speed))
        zrate = shift_rate(
            state, flux(state, vel, pressure, 2), jnp.abs(vel[2]) + sound,
            low, high, 1, zpos, zfirst, zlast, zcoef,
        )
        for v in range(5):
            rate_ref[v, i] = yrate[v] + zrate[v]

    xflip = lambda v: -1.0 if v == 1 else 1.0
    for half in range(2):
        for part in range(2):
            ys, zs = slice(8 * half, 8 * half + 8), slice(128 * part, 128 * part + 128)
            tile = FACE + 2 * half + part
            ends = []
            for last, i, source in ((False, 0, x_side[0]), (True, 3, x_side[1])):
                mine = [u_ref[v, i, ys, zs] for v in range(5)]
                beyond = wall("gx", last, mine, [source(tile + 4 * v) for v in range(5)], xflip)
                far_flux, far_speed = side(beyond, 0)
                spread = 3.0 * jnp.maximum(sx_ref[i // 3, ys, zs], far_speed)
                sign = -3.0 if last else 3.0
                ends.append([sign * far_flux[v] + spread * (beyond[v] - mine[v]) for v in range(5)])
            for v in range(5):
                f = [fx_ref[v, i, ys, zs] for i in range(4)]
                for j in range(4):
                    total = rate_ref[v, j, ys, zs]
                    for i in range(4):
                        if i != j:
                            total = total - float(DERIV[j, i]) * f[i]
                    if j == 0:
                        total = total + ends[0][v]
                    if j == 3:
                        total = total + ends[1][v]
                    rate_ref[v, j, ys, zs] = total


def split(value):
    high = value.astype(BF16)
    return high, (value - high.astype(F32)).astype(BF16)


def parcel_kernel(u_ref, z1_ref, z2_ref, own_ref, dep_ref, base_ref, acc_ref, vel_hi, vel_lo, z_hi, z_lo, a_hi, a_lo):
    low, high = lows_highs("gz", z1_ref, z2_ref)
    sides = (low, lambda t: own_ref[t], high)
    tiles = [sides[g % 3](g // 3) for g in range(27)] + [jnp.zeros((8, 128), F32)]
    for i in range(4):
        inverse = 1.0 / u_ref[0, i]
        for d in range(3):
            hi, lo = split(u_ref[d + 1, i] * inverse)
            start = 16 * (4 * d + i)
            vel_hi[start : start + 16, :] = hi
            vel_lo[start : start + 16, :] = lo
    left = lax.broadcasted_iota(jnp.int32, (8, 128), 1) < 64
    sub8 = lax.broadcasted_iota(jnp.int32, (8, 128), 0)
    sub16 = lax.broadcasted_iota(jnp.int32, (16, 128), 0)
    pos, block = sub16 & 3, sub16 >> 2
    weight_y = by_pos(pos, 1.0 / WEIGHTS)
    weight_xy = [weight_y * float(1.0 / WEIGHTS[i]) for i in range(4)]
    inner = float(NODES[2])
    kept = []
    for p in range(14):
        first, second = tiles[2 * p], tiles[2 * p + 1]
        field = jnp.where(left, first, pltpu.roll(second, 64, 1))
        code = jnp.where(left, pltpu.roll(first, 64, 1), second)
        host = code.astype(jnp.int32) - 1
        host = jnp.concatenate([host, host], axis=0)
        outer = (field + 1.0) * (field - 1.0)
        middle = (field + inner) * (field - inner)
        basis = [
            float(SCALE[0]) * middle * (field - 1.0),
            float(SCALE[1]) * outer * (field - inner),
            float(SCALE[2]) * outer * (field + inner),
            float(SCALE[3]) * middle * (field + 1.0),
        ]

        def spread(r):
            rows = [jnp.broadcast_to(basis[k][r : r + 1], (16, 128)) for k in range(4)]
            return jnp.where(pos == 0, rows[0], jnp.where(pos == 1, rows[1], jnp.where(pos == 2, rows[2], rows[3])))

        in_y = jnp.where((host >> 6) == block, spread(1), 0.0)
        in_z = spread(2)
        in_z_hi = in_z.astype(BF16).astype(F32)
        in_z_lo = in_z - in_z_hi
        offset = (host & 63) - block
        cols = slice(128 * p, 128 * p + 128)
        for t in range(16):
            here = offset == 4 * t
            z_hi[16 * t : 16 * t + 16, cols] = jnp.where(here, in_z_hi, 0.0).astype(BF16)
            z_lo[16 * t : 16 * t + 16, cols] = jnp.where(here, in_z_lo, 0.0).astype(BF16)
        kept.append((field, code, [basis[i][0:1] for i in range(4)], in_y))
    wide = jnp.dot(vel_hi[...], z_hi[...], preferred_element_type=F32)
    wide += jnp.dot(vel_lo[...], z_hi[...], preferred_element_type=F32)
    wide += jnp.dot(vel_hi[...], z_lo[...], preferred_element_type=F32)
    for p in range(14):
        field, code, in_x, in_y = kept[p]
        cols = slice(128 * p, 128 * p + 128)
        live = code > 0.5
        in_xy = [in_x[i] * in_y for i in range(4)]
        seen = []
        for d in range(3):
            mixed = None
            for i in range(4):
                start = 16 * (4 * d + i)
                term = in_xy[i] * wide[start : start + 16, cols]
                mixed = term if mixed is None else mixed + term
            seen.append(jnp.sum(mixed, axis=0, keepdims=True))
        fluid = jnp.where(sub8 == 0, seen[0], jnp.where(sub8 == 1, seen[1], seen[2]))
        speed = pltpu.roll(field, 5, 0)
        keep = live & (sub8 < 3)
        relax = jnp.where(live[0:1], field[6:7], 1.0)
        force = jnp.where(keep, (fluid - speed) / relax, 0.0)
        base = jnp.where(keep, speed, 0.0)
        base_ref[p] = base
        acc_ref[p] = force
        mass = field[7:8]
        push = -mass * force
        work = -mass * jnp.sum(force * base, axis=0, keepdims=True)
        sources = [push[0:1], push[1:2], push[2:3], work]
        for i in range(4):
            scaled = in_xy[i] * weight_xy[i]
            for d in range(4):
                hi, lo = split(sources[d] * scaled)
                start = 16 * (4 * d + i)
                a_hi[start : start + 16, cols] = hi
                a_lo[start : start + 16, cols] = lo
    lanes = (((1,), (1,)), ((), ()))
    total = lax.dot_general(a_hi[...], z_hi[...], lanes, preferred_element_type=F32)
    total += lax.dot_general(a_lo[...], z_hi[...], lanes, preferred_element_type=F32)
    total += lax.dot_general(a_hi[...], z_lo[...], lanes, preferred_element_type=F32)
    zpos = lax.broadcasted_iota(jnp.int32, (16, 256), 1) & 3
    weight_z = by_pos(zpos, 1.0 / WEIGHTS)
    for d in range(4):
        for i in range(4):
            start = 16 * (4 * d + i)
            dep_ref[d, i] = total[start : start + 16, :] * weight_z


def finish_kernel(u_ref, rate_ref, dep_ref, top_ref, base_ref, acc_ref, next_ref, vel_ref):
    top = jnp.max(jnp.max(top_ref[...], axis=0, keepdims=True), axis=1, keepdims=True)
    step = 1.0 / (7.0 * jnp.broadcast_to(top, (8, 256)))
    step16 = jnp.concatenate([step, step], axis=0)
    for v in range(5):
        for i in range(4):
            rate = rate_ref[v, i]
            if v > 0:
                rate = rate + dep_ref[v - 1, i]
            next_ref[v, i] = u_ref[v, i] + step16 * rate
    small = step[:, :128]
    for pair in range(14):
        value = base_ref[pair] + small * acc_ref[pair]
        for h in range(2):
            g = 2 * pair + h
            if g < 27:
                vel_ref[g // 9, g // 3 % 3, g % 3] = value[0:3, 64 * h : 64 * h + 64]


def exchanged(first, second, axis):
    count = lax.axis_size(axis)
    out = []
    for start, value in ((0, first), (1, second)):
        pairs = [(i, i + 1) for i in range(start, count - 1, 2)]
        pairs = pairs + [(j, i) for i, j in pairs]
        out.append(lax.ppermute(value, axis, pairs) if pairs else jnp.zeros_like(value))
    return out


def call(kernel, outs, scratch=(), inputs=None):
    return pl.pallas_call(
        kernel,
        out_shape=outs,
        scratch_shapes=list(scratch),
        compiler_params=pltpu.CompilerParams(vmem_limit_bytes=VMEM_BYTES),
        **({} if inputs is None else {"in_specs": inputs}),
    )


def tiles_of(n):
    return jax.ShapeDtypeStruct((n, 8, 128), F32)


def local(fluid_state, parcel_data, host_element, slot_counts):
    tile = jax.ShapeDtypeStruct((8, 128), F32)
    row = jax.ShapeDtypeStruct((1, 128), F32)
    args = (fluid_state, parcel_data, host_element, slot_counts)
    x_first, x_second, keep_x, faces, top = call(
        pack_kernel,
        (tiles_of(29), tiles_of(29), tiles_of(9), tiles_of(14), tile),
        [pltpu.VMEM(arg.shape, arg.dtype) for arg in args] + [pltpu.SemaphoreType.DMA((4,))],
        [pl.BlockSpec(memory_space=pltpu.HBM)] * 4,
    )(*args)
    top = lax.all_to_all(top, "gx", 0, 0, tiled=True)
    x1, x2 = exchanged(x_first, x_second, "gx")
    y_first, y_second, keep_y, top = call(turn_y_kernel, (tiles_of(14), tiles_of(14), tiles_of(9), row))(
        x1, x2, keep_x, faces, top
    )
    top = lax.pmax(top, "gy")
    y1, y2 = exchanged(y_first, y_second, "gy")
    z_first, z_second, keep_z, top = call(turn_z_kernel, (tiles_of(11), tiles_of(11), tiles_of(9), row))(
        y1, y2, keep_y, faces, top
    )
    top = lax.all_gather(top, "gz", axis=0, tiled=True)
    z1, z2 = exchanged(z_first, z_second, "gz")
    field = jax.ShapeDtypeStruct((5, 4, 16, 256), F32)
    rate = call(
        rate_kernel, field, [pltpu.VMEM((5, 4, 16, 256), F32), pltpu.VMEM((2, 16, 256), F32)],
    )(fluid_state, x1, x2, y1, y2, z1, z2, faces)
    deposit, base, acc = call(
        parcel_kernel,
        (jax.ShapeDtypeStruct((4, 4, 16, 256), F32), tiles_of(14), tiles_of(14)),
        [
            pltpu.VMEM((192, 256), BF16),
            pltpu.VMEM((192, 256), BF16),
            pltpu.VMEM((256, 1792), BF16),
            pltpu.VMEM((256, 1792), BF16),
            pltpu.VMEM((256, 1792), BF16),
            pltpu.VMEM((256, 1792), BF16),
        ],
    )(fluid_state, z1, z2, keep_z)
    return call(finish_kernel, (field, jax.ShapeDtypeStruct((3, 3, 3, 3, 64), F32)))(
        fluid_state, rate, deposit, top, base, acc
    )


def solution(mesh):
    placed = (
        P(None, "gx", "gy", "gz"),
        P("gx", "gy", "gz", None, None),
        P("gx", "gy", "gz", None),
        P("gx", "gy", "gz"),
    )
    return jax.shard_map(
        local,
        mesh=mesh,
        in_specs=placed,
        out_specs=(P(None, "gx", "gy", "gz"), P("gx", "gy", "gz", None, None)),
        check_vma=False,
    )
```

```python
import jax
import jax.numpy as jnp
import numpy as np
from jax import lax
from jax.experimental import pallas as pl
from jax.experimental.pallas import tpu as pltpu
from jax.sharding import PartitionSpec as P

F32 = jnp.float32
BF16 = jnp.bfloat16
VMEM_BYTES = 24 * 1024 * 1024

NODES = np.array([-1.0, -1.0 / np.sqrt(5.0), 1.0 / np.sqrt(5.0), 1.0])
WEIGHTS = np.array([1.0 / 6.0, 5.0 / 6.0, 5.0 / 6.0, 1.0 / 6.0])


def derivative_table():
    factor = [np.prod([NODES[i] - NODES[j] for j in range(4) if j != i]) for i in range(4)]
    table = np.zeros((4, 4))
    for i in range(4):
        for j in range(4):
            if i != j:
                table[i, j] = factor[i] / (factor[j] * (NODES[i] - NODES[j]))
    return table


DERIV = derivative_table()
SCALE = [1.0 / np.prod([NODES[i] - NODES[j] for j in range(4) if j != i]) for i in range(4)]

FACE = 9

PIECES = (8, 32, 2)


def by_pos(pos, values):
    out = jnp.full(pos.shape, float(values[3]), F32)
    for k in range(3):
        out = jnp.where(pos == k, float(values[k]), out)
    return out


def primitives(state):
    inverse = 1.0 / state[0]
    vel = [state[d + 1] * inverse for d in range(3)]
    square = vel[0] * vel[0] + vel[1] * vel[1] + vel[2] * vel[2]
    pressure = 0.4 * (state[4] - 0.5 * state[0] * square)
    sound = jnp.sqrt(1.4 * pressure * inverse)
    return vel, pressure, sound, square


def flux(state, vel, pressure, d):
    normal = vel[d]
    out = [state[d + 1]]
    for k in range(3):
        term = state[k + 1] * normal
        out.append(term + pressure if k == d else term)
    out.append((state[4] + pressure) * normal)
    return out


def side(state, d):
    vel, pressure, sound, _ = primitives(state)
    return flux(state, vel, pressure, d), jnp.abs(vel[d]) + sound


def parity(axis):
    return lax.axis_index(axis) & 1


def lows_highs(axis, first_ref, second_ref):
    odd = jnp.full((8, 128), parity(axis), jnp.int32) == 1

    def low(tile):
        return jnp.where(odd, first_ref[tile], second_ref[tile])

    def high(tile):
        return jnp.where(odd, second_ref[tile], first_ref[tile])

    return low, high


def pack_kernel(u_hbm, data_hbm, host_hbm, count_hbm, first_ref, second_ref, keep_ref, face_ref, top_ref, u_ref, data_ref, host_ref, count_ref, sems):
    copies = [
        pltpu.make_async_copy(source, target, sems.at[k])
        for k, (source, target) in enumerate(
            ((u_hbm, u_ref), (data_hbm, data_ref), (host_hbm, host_ref), (count_hbm, count_ref))
        )
    ]
    for copy in copies:
        copy.start()
    for copy in copies:
        copy.wait()
    top = None
    for i in range(4):
        _, _, sound, square = primitives([u_ref[v, i] for v in range(5)])
        speed = jnp.sqrt(square) + sound
        top = speed if top is None else jnp.maximum(top, speed)
    top = jnp.maximum(top[:, :128], top[:, 128:])
    top = jnp.broadcast_to(jnp.max(top, axis=0, keepdims=True), (8, 128))
    for t in range(PIECES[0]):
        top_ref[t] = top
    slot = lax.broadcasted_iota(jnp.int32, (1, 64), 1)
    odd = parity("gx")
    for a, out in ((2 - 2 * odd, first_ref), (2 * odd, second_ref), (1, keep_ref)):
        for b in range(3):
            for c in range(3):
                count = count_ref[a, b : b + 1, c : c + 1]
                host = host_ref[a, b, c : c + 1, :]
                code = jnp.where(slot < count, host + 1, 0).astype(F32)
                out[3 * b + c, :, 0:64] = data_ref[a, b, c]
                out[3 * b + c, :, 64:128] = jnp.broadcast_to(code, (8, 64))
    for v in range(5):
        for yh in range(2):
            for zh in range(2):
                tile = FACE + 4 * v + 2 * yh + zh
                ys, zs = slice(8 * yh, 8 * yh + 8), slice(128 * zh, 128 * zh + 128)
                first_ref[tile] = u_ref[v, 3 - 3 * odd, ys, zs]
                second_ref[tile] = u_ref[v, 3 * odd, ys, zs]
        for i in range(4):
            for zh in range(2):
                zs = slice(128 * zh, 128 * zh + 128)
                row = 4 * zh + i
                face_ref[v, row : row + 1, :] = u_ref[v, i, 15:16, zs]
                face_ref[5 + v, row : row + 1, :] = u_ref[v, i, 0:1, zs]
    lane = lax.broadcasted_iota(jnp.int32, (16, 128), 1)
    high = jnp.zeros((16, 128), F32)
    low = jnp.zeros((16, 128), F32)
    for v in range(5):
        for i in range(4):
            here = lane == 4 * v + i
            high = jnp.where(here, u_ref[v, i, :, 255:256], high)
            low = jnp.where(here, u_ref[v, i, :, 0:1], low)
    for yh in range(2):
        face_ref[10 + yh] = high[8 * yh : 8 * yh + 8]
        face_ref[12 + yh] = low[8 * yh : 8 * yh + 8]


def folded(tops_ref, pieces):
    top = tops_ref[0]
    for t in range(pieces, tops_ref.shape[0], pieces):
        top = jnp.maximum(top, tops_ref[t])
    return top


def fold(tops_ref, top_ref, pieces):
    top = folded(tops_ref, pieces)
    for t in range(top_ref.shape[0]):
        top_ref[t] = top


def turn_y_kernel(x1_ref, x2_ref, own_ref, face_ref, tops_ref, first_ref, second_ref, keep_ref, top_ref):
    fold(tops_ref, top_ref, PIECES[0])
    low, high = lows_highs("gx", x1_ref, x2_ref)
    odd = parity("gy")
    for a, source in enumerate((low, lambda t: own_ref[t], high)):
        for c in range(3):
            first_ref[3 * a + c] = source(6 - 6 * odd + c)
            second_ref[3 * a + c] = source(6 * odd + c)
            keep_ref[3 * a + c] = source(3 + c)
    for v in range(5):
        first_ref[FACE + v] = face_ref[v + 5 * odd]
        second_ref[FACE + v] = face_ref[v + 5 - 5 * odd]


def turn_z_kernel(y1_ref, y2_ref, own_ref, face_ref, tops_ref, first_ref, second_ref, keep_ref, top_ref):
    fold(tops_ref, top_ref, PIECES[1])
    low, high = lows_highs("gy", y1_ref, y2_ref)
    odd = parity("gz")
    for b, source in enumerate((low, lambda t: own_ref[t], high)):
        for a in range(3):
            first_ref[3 * a + b] = source(3 * a + 2 - 2 * odd)
            second_ref[3 * a + b] = source(3 * a + 2 * odd)
            keep_ref[3 * a + b] = source(3 * a + 1)
    for yh in range(2):
        first_ref[FACE + yh] = face_ref[10 + 2 * odd + yh]
        second_ref[FACE + yh] = face_ref[12 - 2 * odd + yh]


def wall(axis, last, own, received, sign_of):
    at = lax.axis_index(axis) == (lax.axis_size(axis) - 1 if last else 0)
    pick = jnp.full(received[0].shape, at.astype(jnp.int32), jnp.int32) == 1
    return [jnp.where(pick, sign_of(v) * own[v], received[v]) for v in range(5)]


def shift_rate(state, fluxes, speed, low, high, axis, pos, first, last, coef):
    count = state[0].shape[axis]
    low_state, low_flux, low_speed = low
    high_state, high_flux, high_speed = high
    at_low = pos == 0
    ends = at_low | (pos == 3)

    def beside(here, below, above):
        near = jnp.where(at_low, pltpu.roll(here, 1, axis), pltpu.roll(here, count - 1, axis))
        return jnp.where(first, below, jnp.where(last, above, near))

    spread = jnp.maximum(speed, beside(speed, low_speed, high_speed))
    spread = jnp.where(ends, 3.0 * spread, 0.0)
    out = []
    for v in range(5):
        value = fluxes[v]
        above = jnp.where(last, high_flux[v], pltpu.roll(value, count - 1, axis))
        below = jnp.where(first, low_flux[v], pltpu.roll(value, 1, axis))
        total = coef[1] * above + coef[-1] * below
        for d in (-3, -2, 2, 3):
            total = total + coef[d] * pltpu.roll(value, -d % count, axis)
        out.append(spread * (beside(state[v], low_state[v], high_state[v]) - state[v]) - total)
    return out


def rate_kernel(u_ref, x1_ref, x2_ref, y1_ref, y2_ref, z1_ref, z2_ref, face_ref, rate_ref, fx_ref, sx_ref):
    x_side = lows_highs("gx", x1_ref, x2_ref)
    y_side = lows_highs("gy", y1_ref, y2_ref)
    z_side = lows_highs("gz", z1_ref, z2_ref)
    shape = (16, 256)
    row = lax.broadcasted_iota(jnp.int32, shape, 0)
    lane = lax.broadcasted_iota(jnp.int32, shape, 1)
    ypos, zpos = row & 3, lane & 3

    def coefs(pos):
        out = {}
        for d in (-3, -2, -1, 1, 2, 3):
            values = [DERIV[k, k + d] if 0 <= k + d < 4 else 0.0 for k in range(4)]
            if d == 1:
                values[3] = 3.0
            if d == -1:
                values[0] = -3.0
            out[d] = by_pos(pos, values)
        return out

    ycoef, zcoef = coefs(ypos), coefs(zpos)
    yfirst, ylast = row == 0, row == 15
    zfirst, zlast = lane == 0, lane == 255

    yflip = lambda v: -1.0 if v == 2 else 1.0
    ylow = wall("gy", False, [face_ref[5 + v] for v in range(5)], [y_side[0](FACE + v) for v in range(5)], yflip)
    yhigh = wall("gy", True, [face_ref[v] for v in range(5)], [y_side[1](FACE + v) for v in range(5)], yflip)
    ylow_flux, ylow_speed = side(ylow, 1)
    yhigh_flux, yhigh_speed = side(yhigh, 1)

    def columns(first_tile, source):
        both = jnp.concatenate([source(first_tile), source(first_tile + 1)], axis=0)
        return [both if v == 0 else pltpu.roll(both, 128 - 4 * v, 1) for v in range(5)]

    own = lambda t: face_ref[t]
    zflip = lambda v: -1.0 if v == 3 else 1.0
    zlow = wall("gz", False, columns(12, own), columns(FACE, z_side[0]), zflip)
    zhigh = wall("gz", True, columns(10, own), columns(FACE, z_side[1]), zflip)
    zlow_flux, zlow_speed = side(zlow, 2)
    zhigh_flux, zhigh_speed = side(zhigh, 2)

    def pick_row(tile, i):
        return jnp.concatenate([tile[i : i + 1], tile[4 + i : 5 + i]], axis=1)

    for i in range(4):
        state = [u_ref[v, i] for v in range(5)]
        vel, pressure, sound, _ = primitives(state)
        xflux = flux(state, vel, pressure, 0)
        for v in range(5):
            fx_ref[v, i] = xflux[v]
        if i in (0, 3):
            sx_ref[i // 3] = jnp.abs(vel[0]) + sound
        low = ([pick_row(t, i) for t in ylow], [pick_row(t, i) for t in ylow_flux], pick_row(ylow_speed, i))
        high = ([pick_row(t, i) for t in yhigh], [pick_row(t, i) for t in yhigh_flux], pick_row(yhigh_speed, i))
        yrate = shift_rate(
            state, flux(state, vel, pressure, 1), jnp.abs(vel[1]) + sound,
            low, high, 0, ypos, yfirst, ylast, ycoef,
        )
        pick = lambda t: t[:, i : i + 1]
        low = ([pick(t) for t in zlow], [pick(t) for t in zlow_flux], pick(zlow_speed))
        high = ([pick(t) for t in zhigh], [pick(t) for t in zhigh_flux], pick(zhigh_speed))
        zrate = shift_rate(
            state, flux(state, vel, pressure, 2), jnp.abs(vel[2]) + sound,
            low, high, 1, zpos, zfirst, zlast, zcoef,
        )
        for v in range(5):
            rate_ref[v, i] = yrate[v] + zrate[v]

    xflip = lambda v: -1.0 if v == 1 else 1.0
    for half in range(2):
        for part in range(2):
            ys, zs = slice(8 * half, 8 * half + 8), slice(128 * part, 128 * part + 128)
            tile = FACE + 2 * half + part
            ends = []
            for last, i, source in ((False, 0, x_side[0]), (True, 3, x_side[1])):
                mine = [u_ref[v, i, ys, zs] for v in range(5)]
                beyond = wall("gx", last, mine, [source(tile + 4 * v) for v in range(5)], xflip)
                far_flux, far_speed = side(beyond, 0)
                spread = 3.0 * jnp.maximum(sx_ref[i // 3, ys, zs], far_speed)
                sign = -3.0 if last else 3.0
                ends.append([sign * far_flux[v] + spread * (beyond[v] - mine[v]) for v in range(5)])
            for v in range(5):
                f = [fx_ref[v, i, ys, zs] for i in range(4)]
                for j in range(4):
                    total = rate_ref[v, j, ys, zs]
                    for i in range(4):
                        if i != j:
                            total = total - float(DERIV[j, i]) * f[i]
                    if j == 0:
                        total = total + ends[0][v]
                    if j == 3:
                        total = total + ends[1][v]
                    rate_ref[v, j, ys, zs] = total


def split(value):
    high = value.astype(BF16)
    return high, (value - high.astype(F32)).astype(BF16)


def parcel_kernel(u_ref, z1_ref, z2_ref, own_ref, dep_ref, base_ref, acc_ref, vel_hi, vel_lo, z_hi, z_lo, a_hi, a_lo):
    low, high = lows_highs("gz", z1_ref, z2_ref)
    sides = (low, lambda t: own_ref[t], high)
    tiles = [sides[g % 3](g // 3) for g in range(27)] + [jnp.zeros((8, 128), F32)]
    for i in range(4):
        inverse = 1.0 / u_ref[0, i]
        for d in range(3):
            hi, lo = split(u_ref[d + 1, i] * inverse)
            start = 16 * (4 * d + i)
            vel_hi[start : start + 16, :] = hi
            vel_lo[start : start + 16, :] = lo
    left = lax.broadcasted_iota(jnp.int32, (8, 128), 1) < 64
    sub8 = lax.broadcasted_iota(jnp.int32, (8, 128), 0)
    sub16 = lax.broadcasted_iota(jnp.int32, (16, 128), 0)
    pos, block = sub16 & 3, sub16 >> 2
    weight_y = by_pos(pos, 1.0 / WEIGHTS)
    weight_xy = [weight_y * float(1.0 / WEIGHTS[i]) for i in range(4)]
    inner = float(NODES[2])
    kept = []
    for p in range(14):
        first, second = tiles[2 * p], tiles[2 * p + 1]
        field = jnp.where(left, first, pltpu.roll(second, 64, 1))
        code = jnp.where(left, pltpu.roll(first, 64, 1), second)
        host = code.astype(jnp.int32) - 1
        host = jnp.concatenate([host, host], axis=0)
        outer = (field + 1.0) * (field - 1.0)
        middle = (field + inner) * (field - inner)
        basis = [
            float(SCALE[0]) * middle * (field - 1.0),
            float(SCALE[1]) * outer * (field - inner),
            float(SCALE[2]) * outer * (field + inner),
            float(SCALE[3]) * middle * (field + 1.0),
        ]

        def spread(r):
            rows = [jnp.broadcast_to(basis[k][r : r + 1], (16, 128)) for k in range(4)]
            return jnp.where(pos == 0, rows[0], jnp.where(pos == 1, rows[1], jnp.where(pos == 2, rows[2], rows[3])))

        in_y = jnp.where((host >> 6) == block, spread(1), 0.0)
        in_z = spread(2)
        in_z_hi = in_z.astype(BF16).astype(F32)
        in_z_lo = in_z - in_z_hi
        offset = (host & 63) - block
        cols = slice(128 * p, 128 * p + 128)
        for t in range(16):
            here = offset == 4 * t
            z_hi[16 * t : 16 * t + 16, cols] = jnp.where(here, in_z_hi, 0.0).astype(BF16)
            z_lo[16 * t : 16 * t + 16, cols] = jnp.where(here, in_z_lo, 0.0).astype(BF16)
        kept.append((field, code, [basis[i][0:1] for i in range(4)], in_y))
    wide = jnp.dot(vel_hi[...], z_hi[...], preferred_element_type=F32)
    wide += jnp.dot(vel_lo[...], z_hi[...], preferred_element_type=F32)
    wide += jnp.dot(vel_hi[...], z_lo[...], preferred_element_type=F32)
    for p in range(14):
        field, code, in_x, in_y = kept[p]
        cols = slice(128 * p, 128 * p + 128)
        live = code > 0.5
        in_xy = [in_x[i] * in_y for i in range(4)]
        seen = []
        for d in range(3):
            mixed = None
            for i in range(4):
                start = 16 * (4 * d + i)
                term = in_xy[i] * wide[start : start + 16, cols]
                mixed = term if mixed is None else mixed + term
            seen.append(jnp.sum(mixed, axis=0, keepdims=True))
        fluid = jnp.where(sub8 == 0, seen[0], jnp.where(sub8 == 1, seen[1], seen[2]))
        speed = pltpu.roll(field, 5, 0)
        keep = live & (sub8 < 3)
        relax = jnp.where(live[0:1], field[6:7], 1.0)
        force = jnp.where(keep, (fluid - speed) / relax, 0.0)
        base = jnp.where(keep, speed, 0.0)
        base_ref[p] = base
        acc_ref[p] = force
        mass = field[7:8]
        push = -mass * force
        work = -mass * jnp.sum(force * base, axis=0, keepdims=True)
        sources = [push[0:1], push[1:2], push[2:3], work]
        for i in range(4):
            scaled = in_xy[i] * weight_xy[i]
            for d in range(4):
                hi, lo = split(sources[d] * scaled)
                start = 16 * (4 * d + i)
                a_hi[start : start + 16, cols] = hi
                a_lo[start : start + 16, cols] = lo
    lanes = (((1,), (1,)), ((), ()))
    total = lax.dot_general(a_hi[...], z_hi[...], lanes, preferred_element_type=F32)
    total += lax.dot_general(a_lo[...], z_hi[...], lanes, preferred_element_type=F32)
    total += lax.dot_general(a_hi[...], z_lo[...], lanes, preferred_element_type=F32)
    zpos = lax.broadcasted_iota(jnp.int32, (16, 256), 1) & 3
    weight_z = by_pos(zpos, 1.0 / WEIGHTS)
    for d in range(4):
        for i in range(4):
            start = 16 * (4 * d + i)
            dep_ref[d, i] = total[start : start + 16, :] * weight_z


def finish_kernel(u_ref, rate_ref, dep_ref, top_ref, base_ref, acc_ref, next_ref, vel_ref):
    top = jnp.max(jnp.max(folded(top_ref, PIECES[2]), axis=0, keepdims=True), axis=1, keepdims=True)
    step = 1.0 / (7.0 * jnp.broadcast_to(top, (8, 256)))
    step16 = jnp.concatenate([step, step], axis=0)
    for v in range(5):
        for i in range(4):
            rate = rate_ref[v, i]
            if v > 0:
                rate = rate + dep_ref[v - 1, i]
            next_ref[v, i] = u_ref[v, i] + step16 * rate
    small = step[:, :128]
    for pair in range(14):
        value = base_ref[pair] + small * acc_ref[pair]
        for h in range(2):
            g = 2 * pair + h
            if g < 27:
                vel_ref[g // 9, g // 3 % 3, g % 3] = value[0:3, 64 * h : 64 * h + 64]


def exchanged(first, second, axis):
    count = lax.axis_size(axis)
    out = []
    for start, value in ((0, first), (1, second)):
        pairs = [(i, i + 1) for i in range(start, count - 1, 2)]
        pairs = pairs + [(j, i) for i, j in pairs]
        out.append(lax.ppermute(value, axis, pairs) if pairs else jnp.zeros_like(value))
    return out


def call(kernel, outs, scratch=(), inputs=None):
    return pl.pallas_call(
        kernel,
        out_shape=outs,
        scratch_shapes=list(scratch),
        compiler_params=pltpu.CompilerParams(vmem_limit_bytes=VMEM_BYTES),
        **({} if inputs is None else {"in_specs": inputs}),
    )


def tiles_of(n):
    return jax.ShapeDtypeStruct((n, 8, 128), F32)


def local(fluid_state, parcel_data, host_element, slot_counts):
    args = (fluid_state, parcel_data, host_element, slot_counts)
    x_first, x_second, keep_x, faces, top = call(
        pack_kernel,
        (tiles_of(29), tiles_of(29), tiles_of(9), tiles_of(14), tiles_of(PIECES[0])),
        [pltpu.VMEM(arg.shape, arg.dtype) for arg in args] + [pltpu.SemaphoreType.DMA((4,))],
        [pl.BlockSpec(memory_space=pltpu.HBM)] * 4,
    )(*args)
    top = lax.all_gather(top, "gx", axis=0, tiled=True)
    x1, x2 = exchanged(x_first, x_second, "gx")
    y_first, y_second, keep_y, top = call(turn_y_kernel, (tiles_of(14), tiles_of(14), tiles_of(9), tiles_of(PIECES[1])))(
        x1, x2, keep_x, faces, top
    )
    top = lax.all_gather(top, "gy", axis=0, tiled=True)
    y1, y2 = exchanged(y_first, y_second, "gy")
    z_first, z_second, keep_z, top = call(turn_z_kernel, (tiles_of(11), tiles_of(11), tiles_of(9), tiles_of(PIECES[2])))(
        y1, y2, keep_y, faces, top
    )
    top = lax.all_gather(top, "gz", axis=0, tiled=True)
    z1, z2 = exchanged(z_first, z_second, "gz")
    field = jax.ShapeDtypeStruct((5, 4, 16, 256), F32)
    rate = call(
        rate_kernel, field, [pltpu.VMEM((5, 4, 16, 256), F32), pltpu.VMEM((2, 16, 256), F32)],
    )(fluid_state, x1, x2, y1, y2, z1, z2, faces)
    deposit, base, acc = call(
        parcel_kernel,
        (jax.ShapeDtypeStruct((4, 4, 16, 256), F32), tiles_of(14), tiles_of(14)),
        [
            pltpu.VMEM((192, 256), BF16),
            pltpu.VMEM((192, 256), BF16),
            pltpu.VMEM((256, 1792), BF16),
            pltpu.VMEM((256, 1792), BF16),
            pltpu.VMEM((256, 1792), BF16),
            pltpu.VMEM((256, 1792), BF16),
        ],
    )(fluid_state, z1, z2, keep_z)
    return call(finish_kernel, (field, jax.ShapeDtypeStruct((3, 3, 3, 3, 64), F32)))(
        fluid_state, rate, deposit, top, base, acc
    )


def solution(mesh):
    placed = (
        P(None, "gx", "gy", "gz"),
        P("gx", "gy", "gz", None, None),
        P("gx", "gy", "gz", None),
        P("gx", "gy", "gz"),
    )
    return jax.shard_map(
        local,
        mesh=mesh,
        in_specs=placed,
        out_specs=(P(None, "gx", "gy", "gz"), P("gx", "gy", "gz", None, None)),
        check_vma=False,
    )
```

```python
import jax
import jax.numpy as jnp
import numpy as np
from jax import lax
from jax.experimental import pallas as pl
from jax.experimental.pallas import tpu as pltpu
from jax.sharding import PartitionSpec as P

F32 = jnp.float32
BF16 = jnp.bfloat16
VMEM_BYTES = 24 * 1024 * 1024

NODES = np.array([-1.0, -1.0 / np.sqrt(5.0), 1.0 / np.sqrt(5.0), 1.0])
WEIGHTS = np.array([1.0 / 6.0, 5.0 / 6.0, 5.0 / 6.0, 1.0 / 6.0])


def derivative_table():
    factor = [np.prod([NODES[i] - NODES[j] for j in range(4) if j != i]) for i in range(4)]
    table = np.zeros((4, 4))
    for i in range(4):
        for j in range(4):
            if i != j:
                table[i, j] = factor[i] / (factor[j] * (NODES[i] - NODES[j]))
    return table


DERIV = derivative_table()
SCALE = [1.0 / np.prod([NODES[i] - NODES[j] for j in range(4) if j != i]) for i in range(4)]

TOP, FACE = 9, 10


def by_pos(pos, values):
    out = jnp.full(pos.shape, float(values[3]), F32)
    for k in range(3):
        out = jnp.where(pos == k, float(values[k]), out)
    return out


def primitives(state):
    inverse = 1.0 / state[0]
    vel = [state[d + 1] * inverse for d in range(3)]
    square = vel[0] * vel[0] + vel[1] * vel[1] + vel[2] * vel[2]
    pressure = 0.4 * (state[4] - 0.5 * state[0] * square)
    sound = jnp.sqrt(1.4 * pressure * inverse)
    return vel, pressure, sound, square


def flux(state, vel, pressure, d):
    normal = vel[d]
    out = [state[d + 1]]
    for k in range(3):
        term = state[k + 1] * normal
        out.append(term + pressure if k == d else term)
    out.append((state[4] + pressure) * normal)
    return out


def side(state, d):
    vel, pressure, sound, _ = primitives(state)
    return flux(state, vel, pressure, d), jnp.abs(vel[d]) + sound


def tile_of(ref):
    return lambda tile: ref[tile]


def face_kernel(u_ref, up_ref, down_ref, face_ref):
    top = None
    for i in range(4):
        _, _, sound, square = primitives([u_ref[v, i] for v in range(5)])
        speed = jnp.sqrt(square) + sound
        top = speed if top is None else jnp.maximum(top, speed)
    top = jnp.maximum(top[:, :128], top[:, 128:])
    top = jnp.maximum(top[:8], top[8:])
    up_ref[0] = top
    down_ref[0] = top
    for v in range(5):
        for yh in range(2):
            for zh in range(2):
                tile = 1 + 4 * v + 2 * yh + zh
                ys, zs = slice(8 * yh, 8 * yh + 8), slice(128 * zh, 128 * zh + 128)
                up_ref[tile] = u_ref[v, 3, ys, zs]
                down_ref[tile] = u_ref[v, 0, ys, zs]
        for i in range(4):
            for zh in range(2):
                zs = slice(128 * zh, 128 * zh + 128)
                row = 4 * zh + i
                face_ref[v, row : row + 1, :] = u_ref[v, i, 15:16, zs]
                face_ref[5 + v, row : row + 1, :] = u_ref[v, i, 0:1, zs]
    lane = lax.broadcasted_iota(jnp.int32, (16, 128), 1)
    high = jnp.zeros((16, 128), F32)
    low = jnp.zeros((16, 128), F32)
    for v in range(5):
        for i in range(4):
            here = lane == 4 * v + i
            high = jnp.where(here, u_ref[v, i, :, 255:256], high)
            low = jnp.where(here, u_ref[v, i, :, 0:1], low)
    for yh in range(2):
        face_ref[10 + yh] = high[8 * yh : 8 * yh + 8]
        face_ref[12 + yh] = low[8 * yh : 8 * yh + 8]


def pack_kernel(data_ref, host_ref, count_ref, face_up_ref, face_down_ref, up_ref, down_ref, keep_ref):
    slot = lax.broadcasted_iota(jnp.int32, (1, 64), 1)
    for a, out in ((2, up_ref), (0, down_ref), (1, keep_ref)):
        for b in range(3):
            for c in range(3):
                count = count_ref[a, b : b + 1, c : c + 1]
                host = host_ref[a, b, c : c + 1, :]
                code = jnp.where(slot < count, host + 1, 0).astype(F32)
                out[3 * b + c, :, 0:64] = data_ref[a, b, c]
                out[3 * b + c, :, 64:128] = jnp.broadcast_to(code, (8, 64))
    for t in range(21):
        up_ref[TOP + t] = face_up_ref[t]
        down_ref[TOP + t] = face_down_ref[t]


def turn_y_kernel(low_ref, high_ref, own_ref, face_ref, mine_ref, up_ref, down_ref, keep_ref):
    for a, source in enumerate((low_ref, own_ref, high_ref)):
        for c in range(3):
            up_ref[3 * a + c] = source[6 + c]
            down_ref[3 * a + c] = source[c]
            keep_ref[3 * a + c] = source[3 + c]
    top = jnp.maximum(jnp.maximum(low_ref[TOP], high_ref[TOP]), mine_ref[TOP])
    up_ref[TOP] = top
    down_ref[TOP] = top
    for v in range(5):
        up_ref[FACE + v] = face_ref[v]
        down_ref[FACE + v] = face_ref[5 + v]


def turn_z_kernel(low_ref, high_ref, own_ref, face_ref, mine_ref, up_ref, down_ref, keep_ref):
    for b, source in enumerate((low_ref, own_ref, high_ref)):
        for a in range(3):
            up_ref[3 * a + b] = source[3 * a + 2]
            down_ref[3 * a + b] = source[3 * a]
            keep_ref[3 * a + b] = source[3 * a + 1]
    top = jnp.maximum(jnp.maximum(low_ref[TOP], high_ref[TOP]), mine_ref[TOP])
    up_ref[TOP] = top
    down_ref[TOP] = top
    for yh in range(2):
        up_ref[FACE + yh] = face_ref[10 + yh]
        down_ref[FACE + yh] = face_ref[12 + yh]


def top_kernel(low_ref, high_ref, mine_ref, top_ref):
    top = jnp.maximum(jnp.maximum(low_ref[TOP], high_ref[TOP]), mine_ref[TOP])
    top_ref[...] = jnp.broadcast_to(jnp.max(top, axis=0, keepdims=True), top_ref.shape)


def fold_kernel(tops_ref, top_ref):
    top_ref[...] = jnp.broadcast_to(jnp.max(tops_ref[...], axis=0, keepdims=True), top_ref.shape)


def wall(axis, last, own, received, sign_of):
    at = lax.axis_index(axis) == (lax.axis_size(axis) - 1 if last else 0)
    pick = jnp.full(received[0].shape, at.astype(jnp.int32), jnp.int32) == 1
    return [jnp.where(pick, sign_of(v) * own[v], received[v]) for v in range(5)]


def shift_rate(state, fluxes, speed, low, high, axis, pos, first, last, coef):
    count = state[0].shape[axis]
    low_state, low_flux, low_speed = low
    high_state, high_flux, high_speed = high
    at_low = pos == 0
    ends = at_low | (pos == 3)

    def beside(here, below, above):
        near = jnp.where(at_low, pltpu.roll(here, 1, axis), pltpu.roll(here, count - 1, axis))
        return jnp.where(first, below, jnp.where(last, above, near))

    spread = jnp.maximum(speed, beside(speed, low_speed, high_speed))
    spread = jnp.where(ends, 3.0 * spread, 0.0)
    out = []
    for v in range(5):
        value = fluxes[v]
        above = jnp.where(last, high_flux[v], pltpu.roll(value, count - 1, axis))
        below = jnp.where(first, low_flux[v], pltpu.roll(value, 1, axis))
        total = coef[1] * above + coef[-1] * below
        for d in (-3, -2, 2, 3):
            total = total + coef[d] * pltpu.roll(value, -d % count, axis)
        out.append(spread * (beside(state[v], low_state[v], high_state[v]) - state[v]) - total)
    return out


def rate_kernel(u_ref, x1_ref, x2_ref, y1_ref, y2_ref, z1_ref, z2_ref, face_ref, rate_ref, fx_ref, sx_ref):
    x_side = tile_of(x1_ref), tile_of(x2_ref)
    y_side = tile_of(y1_ref), tile_of(y2_ref)
    z_side = tile_of(z1_ref), tile_of(z2_ref)
    shape = (16, 256)
    row = lax.broadcasted_iota(jnp.int32, shape, 0)
    lane = lax.broadcasted_iota(jnp.int32, shape, 1)
    ypos, zpos = row & 3, lane & 3

    def coefs(pos):
        out = {}
        for d in (-3, -2, -1, 1, 2, 3):
            values = [DERIV[k, k + d] if 0 <= k + d < 4 else 0.0 for k in range(4)]
            if d == 1:
                values[3] = 3.0
            if d == -1:
                values[0] = -3.0
            out[d] = by_pos(pos, values)
        return out

    ycoef, zcoef = coefs(ypos), coefs(zpos)
    yfirst, ylast = row == 0, row == 15
    zfirst, zlast = lane == 0, lane == 255

    yflip = lambda v: -1.0 if v == 2 else 1.0
    ylow = wall("gy", False, [face_ref[5 + v] for v in range(5)], [y_side[0](FACE + v) for v in range(5)], yflip)
    yhigh = wall("gy", True, [face_ref[v] for v in range(5)], [y_side[1](FACE + v) for v in range(5)], yflip)
    ylow_flux, ylow_speed = side(ylow, 1)
    yhigh_flux, yhigh_speed = side(yhigh, 1)

    def columns(first_tile, source):
        both = jnp.concatenate([source(first_tile), source(first_tile + 1)], axis=0)
        return [both if v == 0 else pltpu.roll(both, 128 - 4 * v, 1) for v in range(5)]

    own = tile_of(face_ref)
    zflip = lambda v: -1.0 if v == 3 else 1.0
    zlow = wall("gz", False, columns(12, own), columns(FACE, z_side[0]), zflip)
    zhigh = wall("gz", True, columns(10, own), columns(FACE, z_side[1]), zflip)
    zlow_flux, zlow_speed = side(zlow, 2)
    zhigh_flux, zhigh_speed = side(zhigh, 2)

    def pick_row(tile, i):
        return jnp.concatenate([tile[i : i + 1], tile[4 + i : 5 + i]], axis=1)

    for i in range(4):
        state = [u_ref[v, i] for v in range(5)]
        vel, pressure, sound, _ = primitives(state)
        xflux = flux(state, vel, pressure, 0)
        for v in range(5):
            fx_ref[v, i] = xflux[v]
        if i in (0, 3):
            sx_ref[i // 3] = jnp.abs(vel[0]) + sound
        low = ([pick_row(t, i) for t in ylow], [pick_row(t, i) for t in ylow_flux], pick_row(ylow_speed, i))
        high = ([pick_row(t, i) for t in yhigh], [pick_row(t, i) for t in yhigh_flux], pick_row(yhigh_speed, i))
        yrate = shift_rate(
            state, flux(state, vel, pressure, 1), jnp.abs(vel[1]) + sound,
            low, high, 0, ypos, yfirst, ylast, ycoef,
        )
        pick = lambda t: t[:, i : i + 1]
        low = ([pick(t) for t in zlow], [pick(t) for t in zlow_flux], pick(zlow_speed))
        high = ([pick(t) for t in zhigh], [pick(t) for t in zhigh_flux], pick(zhigh_speed))
        zrate = shift_rate(
            state, flux(state, vel, pressure, 2), jnp.abs(vel[2]) + sound,
            low, high, 1, zpos, zfirst, zlast, zcoef,
        )
        for v in range(5):
            rate_ref[v, i] = yrate[v] + zrate[v]

    xflip = lambda v: -1.0 if v == 1 else 1.0
    for half in range(2):
        for part in range(2):
            ys, zs = slice(8 * half, 8 * half + 8), slice(128 * part, 128 * part + 128)
            tile = FACE + 2 * half + part
            ends = []
            for last, i, source in ((False, 0, x_side[0]), (True, 3, x_side[1])):
                mine = [u_ref[v, i, ys, zs] for v in range(5)]
                beyond = wall("gx", last, mine, [source(tile + 4 * v) for v in range(5)], xflip)
                far_flux, far_speed = side(beyond, 0)
                spread = 3.0 * jnp.maximum(sx_ref[i // 3, ys, zs], far_speed)
                sign = -3.0 if last else 3.0
                ends.append([sign * far_flux[v] + spread * (beyond[v] - mine[v]) for v in range(5)])
            for v in range(5):
                f = [fx_ref[v, i, ys, zs] for i in range(4)]
                for j in range(4):
                    total = rate_ref[v, j, ys, zs]
                    for i in range(4):
                        if i != j:
                            total = total - float(DERIV[j, i]) * f[i]
                    if j == 0:
                        total = total + ends[0][v]
                    if j == 3:
                        total = total + ends[1][v]
                    rate_ref[v, j, ys, zs] = total


def split(value):
    high = value.astype(BF16)
    return high, (value - high.astype(F32)).astype(BF16)


def parcel_kernel(u_ref, z1_ref, z2_ref, own_ref, dep_ref, base_ref, acc_ref, vel_hi, vel_lo, z_hi, z_lo, a_hi, a_lo):
    sides = (z1_ref, own_ref, z2_ref)
    tiles = [sides[g % 3][g // 3] for g in range(27)] + [jnp.zeros((8, 128), F32)]
    for i in range(4):
        inverse = 1.0 / u_ref[0, i]
        for d in range(3):
            hi, lo = split(u_ref[d + 1, i] * inverse)
            start = 16 * (4 * d + i)
            vel_hi[start : start + 16, :] = hi
            vel_lo[start : start + 16, :] = lo
    left = lax.broadcasted_iota(jnp.int32, (8, 128), 1) < 64
    sub8 = lax.broadcasted_iota(jnp.int32, (8, 128), 0)
    sub16 = lax.broadcasted_iota(jnp.int32, (16, 128), 0)
    pos, block = sub16 & 3, sub16 >> 2
    weight_y = by_pos(pos, 1.0 / WEIGHTS)
    weight_xy = [weight_y * float(1.0 / WEIGHTS[i]) for i in range(4)]
    inner = float(NODES[2])
    kept = []
    for p in range(14):
        first, second = tiles[2 * p], tiles[2 * p + 1]
        field = jnp.where(left, first, pltpu.roll(second, 64, 1))
        code = jnp.where(left, pltpu.roll(first, 64, 1), second)
        host = code.astype(jnp.int32) - 1
        host = jnp.concatenate([host, host], axis=0)
        outer = (field + 1.0) * (field - 1.0)
        middle = (field + inner) * (field - inner)
        basis = [
            float(SCALE[0]) * middle * (field - 1.0),
            float(SCALE[1]) * outer * (field - inner),
            float(SCALE[2]) * outer * (field + inner),
            float(SCALE[3]) * middle * (field + 1.0),
        ]

        def spread(r):
            rows = [jnp.broadcast_to(basis[k][r : r + 1], (16, 128)) for k in range(4)]
            return jnp.where(pos == 0, rows[0], jnp.where(pos == 1, rows[1], jnp.where(pos == 2, rows[2], rows[3])))

        in_y = jnp.where((host >> 6) == block, spread(1), 0.0)
        in_z = spread(2)
        in_z_hi = in_z.astype(BF16).astype(F32)
        in_z_lo = in_z - in_z_hi
        offset = (host & 63) - block
        cols = slice(128 * p, 128 * p + 128)
        for t in range(16):
            here = offset == 4 * t
            z_hi[16 * t : 16 * t + 16, cols] = jnp.where(here, in_z_hi, 0.0).astype(BF16)
            z_lo[16 * t : 16 * t + 16, cols] = jnp.where(here, in_z_lo, 0.0).astype(BF16)
        kept.append((field, code, [basis[i][0:1] for i in range(4)], in_y))
    wide = jnp.dot(vel_hi[...], z_hi[...], preferred_element_type=F32)
    wide += jnp.dot(vel_lo[...], z_hi[...], preferred_element_type=F32)
    wide += jnp.dot(vel_hi[...], z_lo[...], preferred_element_type=F32)
    for p in range(14):
        field, code, in_x, in_y = kept[p]
        cols = slice(128 * p, 128 * p + 128)
        live = code > 0.5
        in_xy = [in_x[i] * in_y for i in range(4)]
        seen = []
        for d in range(3):
            mixed = None
            for i in range(4):
                start = 16 * (4 * d + i)
                term = in_xy[i] * wide[start : start + 16, cols]
                mixed = term if mixed is None else mixed + term
            seen.append(jnp.sum(mixed, axis=0, keepdims=True))
        fluid = jnp.where(sub8 == 0, seen[0], jnp.where(sub8 == 1, seen[1], seen[2]))
        speed = pltpu.roll(field, 5, 0)
        keep = live & (sub8 < 3)
        relax = jnp.where(live[0:1], field[6:7], 1.0)
        force = jnp.where(keep, (fluid - speed) / relax, 0.0)
        base = jnp.where(keep, speed, 0.0)
        base_ref[p] = base
        acc_ref[p] = force
        mass = field[7:8]
        push = -mass * force
        work = -mass * jnp.sum(force * base, axis=0, keepdims=True)
        sources = [push[0:1], push[1:2], push[2:3], work]
        for i in range(4):
            scaled = in_xy[i] * weight_xy[i]
            for d in range(4):
                hi, lo = split(sources[d] * scaled)
                start = 16 * (4 * d + i)
                a_hi[start : start + 16, cols] = hi
                a_lo[start : start + 16, cols] = lo
    lanes = (((1,), (1,)), ((), ()))
    total = lax.dot_general(a_hi[...], z_hi[...], lanes, preferred_element_type=F32)
    total += lax.dot_general(a_lo[...], z_hi[...], lanes, preferred_element_type=F32)
    total += lax.dot_general(a_hi[...], z_lo[...], lanes, preferred_element_type=F32)
    zpos = lax.broadcasted_iota(jnp.int32, (16, 256), 1) & 3
    weight_z = by_pos(zpos, 1.0 / WEIGHTS)
    for d in range(4):
        for i in range(4):
            start = 16 * (4 * d + i)
            dep_ref[d, i] = total[start : start + 16, :] * weight_z


def finish_kernel(u_ref, rate_ref, dep_ref, top_ref, base_ref, acc_ref, next_ref, vel_ref):
    top = jnp.max(jnp.max(top_ref[...], axis=0, keepdims=True), axis=1, keepdims=True)
    step = 1.0 / (7.0 * jnp.broadcast_to(top, (8, 256)))
    step16 = jnp.concatenate([step, step], axis=0)
    for v in range(5):
        for i in range(4):
            rate = rate_ref[v, i]
            if v > 0:
                rate = rate + dep_ref[v - 1, i]
            next_ref[v, i] = u_ref[v, i] + step16 * rate
    small = step[:, :128]
    for pair in range(14):
        value = base_ref[pair] + small * acc_ref[pair]
        for h in range(2):
            g = 2 * pair + h
            if g < 27:
                vel_ref[g // 9, g // 3 % 3, g % 3] = value[0:3, 64 * h : 64 * h + 64]


def exchanged(up, down, axis):
    count = lax.axis_size(axis)
    return (
        lax.ppermute(up, axis, [(i, (i + 1) % count) for i in range(count)]),
        lax.ppermute(down, axis, [((i + 1) % count, i) for i in range(count)]),
    )


def spread_top(top, axis):
    count = lax.axis_size(axis)
    groups = [list(range(0, count, 2)), list(range(1, count, 2))]
    return lax.all_to_all(top, axis, 0, 0, axis_index_groups=groups, tiled=True)


def call(kernel, outs, scratch=()):
    return pl.pallas_call(
        kernel,
        out_shape=outs,
        scratch_shapes=list(scratch),
        compiler_params=pltpu.CompilerParams(vmem_limit_bytes=VMEM_BYTES),
    )


def tiles_of(n):
    return jax.ShapeDtypeStruct((n, 8, 128), F32)


def local(fluid_state, parcel_data, host_element, slot_counts):
    face_up, face_down, faces = call(face_kernel, (tiles_of(21), tiles_of(21), tiles_of(14)))(fluid_state)
    x_up, x_down, keep_x = call(pack_kernel, (tiles_of(30), tiles_of(30), tiles_of(9)))(
        parcel_data, host_element, slot_counts, face_up, face_down
    )
    x1, x2 = exchanged(x_up, x_down, "gx")
    y_up, y_down, keep_y = call(turn_y_kernel, (tiles_of(15), tiles_of(15), tiles_of(9)))(x1, x2, keep_x, faces, x_up)
    y1, y2 = exchanged(y_up, y_down, "gy")
    z_up, z_down, keep_z = call(turn_z_kernel, (tiles_of(12), tiles_of(12), tiles_of(9)))(y1, y2, keep_y, faces, y_up)
    z1, z2 = exchanged(z_up, z_down, "gz")
    rows = [jax.ShapeDtypeStruct((max(1, lax.axis_size(axis) // 2), 128), F32) for axis in ("gx", "gy", "gz")]
    top = spread_top(call(top_kernel, rows[0])(z1, z2, z_up), "gx")
    top = spread_top(call(fold_kernel, rows[1])(top), "gy")
    top = spread_top(call(fold_kernel, rows[2])(top), "gz")
    field = jax.ShapeDtypeStruct((5, 4, 16, 256), F32)
    rate = call(
        rate_kernel, field, [pltpu.VMEM((5, 4, 16, 256), F32), pltpu.VMEM((2, 16, 256), F32)],
    )(fluid_state, x1, x2, y1, y2, z1, z2, faces)
    deposit, base, acc = call(
        parcel_kernel,
        (jax.ShapeDtypeStruct((4, 4, 16, 256), F32), tiles_of(14), tiles_of(14)),
        [
            pltpu.VMEM((192, 256), BF16),
            pltpu.VMEM((192, 256), BF16),
            pltpu.VMEM((256, 1792), BF16),
            pltpu.VMEM((256, 1792), BF16),
            pltpu.VMEM((256, 1792), BF16),
            pltpu.VMEM((256, 1792), BF16),
        ],
    )(fluid_state, z1, z2, keep_z)
    return call(finish_kernel, (field, jax.ShapeDtypeStruct((3, 3, 3, 3, 64), F32)))(
        fluid_state, rate, deposit, top, base, acc
    )


def solution(mesh):
    placed = (
        P(None, "gx", "gy", "gz"),
        P("gx", "gy", "gz", None, None),
        P("gx", "gy", "gz", None),
        P("gx", "gy", "gz"),
    )
    return jax.shard_map(
        local,
        mesh=mesh,
        in_specs=placed,
        out_specs=(P(None, "gx", "gy", "gz"), P("gx", "gy", "gz", None, None)),
        check_vma=False,
    )
```

```python
import jax
import jax.numpy as jnp
import numpy as np
from jax import lax
from jax.experimental import pallas as pl
from jax.experimental.pallas import tpu as pltpu
from jax.sharding import PartitionSpec as P

F32 = jnp.float32
BF16 = jnp.bfloat16
VMEM_BYTES = 24 * 1024 * 1024
TURN_BYTES = 16 * 1024 * 1024

NODES = np.array([-1.0, -1.0 / np.sqrt(5.0), 1.0 / np.sqrt(5.0), 1.0])
WEIGHTS = np.array([1.0 / 6.0, 5.0 / 6.0, 5.0 / 6.0, 1.0 / 6.0])


def derivative_table():
    factor = [np.prod([NODES[i] - NODES[j] for j in range(4) if j != i]) for i in range(4)]
    table = np.zeros((4, 4))
    for i in range(4):
        for j in range(4):
            if i != j:
                table[i, j] = factor[i] / (factor[j] * (NODES[i] - NODES[j]))
    return table


DERIV = derivative_table()
SCALE = [1.0 / np.prod([NODES[i] - NODES[j] for j in range(4) if j != i]) for i in range(4)]

FACE = 9


def by_pos(pos, values):
    out = jnp.full(pos.shape, float(values[3]), F32)
    for k in range(3):
        out = jnp.where(pos == k, float(values[k]), out)
    return out


def primitives(state):
    inverse = 1.0 / state[0]
    vel = [state[d + 1] * inverse for d in range(3)]
    square = vel[0] * vel[0] + vel[1] * vel[1] + vel[2] * vel[2]
    pressure = 0.4 * (state[4] - 0.5 * state[0] * square)
    sound = jnp.sqrt(1.4 * pressure * inverse)
    return vel, pressure, sound, square


def flux(state, vel, pressure, d):
    normal = vel[d]
    out = [state[d + 1]]
    for k in range(3):
        term = state[k + 1] * normal
        out.append(term + pressure if k == d else term)
    out.append((state[4] + pressure) * normal)
    return out


def side(state, d):
    vel, pressure, sound, _ = primitives(state)
    return flux(state, vel, pressure, d), jnp.abs(vel[d]) + sound


def tile_of(ref):
    return lambda tile: ref[tile]


def face_kernel(u_ref, up_ref, down_ref, face_ref, top_ref):
    top = None
    for i in range(4):
        _, _, sound, square = primitives([u_ref[v, i] for v in range(5)])
        speed = jnp.sqrt(square) + sound
        top = speed if top is None else jnp.maximum(top, speed)
    top = jnp.maximum(top[:, :128], top[:, 128:])
    top_ref[...] = jnp.broadcast_to(jnp.max(top, axis=0, keepdims=True), top_ref.shape)
    for v in range(5):
        for yh in range(2):
            for zh in range(2):
                tile = 4 * v + 2 * yh + zh
                ys, zs = slice(8 * yh, 8 * yh + 8), slice(128 * zh, 128 * zh + 128)
                up_ref[tile] = u_ref[v, 3, ys, zs]
                down_ref[tile] = u_ref[v, 0, ys, zs]
        for i in range(4):
            for zh in range(2):
                zs = slice(128 * zh, 128 * zh + 128)
                row = 4 * zh + i
                face_ref[v, row : row + 1, :] = u_ref[v, i, 15:16, zs]
                face_ref[5 + v, row : row + 1, :] = u_ref[v, i, 0:1, zs]
    lane = lax.broadcasted_iota(jnp.int32, (16, 128), 1)
    high = jnp.zeros((16, 128), F32)
    low = jnp.zeros((16, 128), F32)
    for v in range(5):
        for i in range(4):
            here = lane == 4 * v + i
            high = jnp.where(here, u_ref[v, i, :, 255:256], high)
            low = jnp.where(here, u_ref[v, i, :, 0:1], low)
    for yh in range(2):
        face_ref[10 + yh] = high[8 * yh : 8 * yh + 8]
        face_ref[12 + yh] = low[8 * yh : 8 * yh + 8]


def pack_kernel(data_ref, host_ref, count_ref, face_up_ref, face_down_ref, up_ref, down_ref, keep_ref):
    slot = lax.broadcasted_iota(jnp.int32, (1, 64), 1)
    for a, out in ((2, up_ref), (0, down_ref), (1, keep_ref)):
        for b in range(3):
            for c in range(3):
                count = count_ref[a, b : b + 1, c : c + 1]
                host = host_ref[a, b, c : c + 1, :]
                code = jnp.where(slot < count, host + 1, 0).astype(F32)
                out[3 * b + c, :, 0:64] = data_ref[a, b, c]
                out[3 * b + c, :, 64:128] = jnp.broadcast_to(code, (8, 64))
    for t in range(20):
        up_ref[FACE + t] = face_up_ref[t]
        down_ref[FACE + t] = face_down_ref[t]


def turn_y_kernel(low_ref, high_ref, own_ref, face_ref, up_ref, down_ref, keep_ref):
    for a, source in enumerate((low_ref, own_ref, high_ref)):
        for c in range(3):
            up_ref[3 * a + c] = source[6 + c]
            down_ref[3 * a + c] = source[c]
            keep_ref[3 * a + c] = source[3 + c]
    for v in range(5):
        up_ref[FACE + v] = face_ref[v]
        down_ref[FACE + v] = face_ref[5 + v]


def turn_z_kernel(low_ref, high_ref, own_ref, face_ref, up_ref, down_ref, keep_ref):
    for b, source in enumerate((low_ref, own_ref, high_ref)):
        for a in range(3):
            up_ref[3 * a + b] = source[3 * a + 2]
            down_ref[3 * a + b] = source[3 * a]
            keep_ref[3 * a + b] = source[3 * a + 1]
    for yh in range(2):
        up_ref[FACE + yh] = face_ref[10 + yh]
        down_ref[FACE + yh] = face_ref[12 + yh]


def fold_kernel(tops_ref, turned_ref, top_ref):
    top_ref[...] = jnp.broadcast_to(jnp.max(tops_ref[...], axis=0, keepdims=True), top_ref.shape)


def wall(axis, last, own, received, sign_of):
    at = lax.axis_index(axis) == (lax.axis_size(axis) - 1 if last else 0)
    pick = jnp.full(received[0].shape, at.astype(jnp.int32), jnp.int32) == 1
    return [jnp.where(pick, sign_of(v) * own[v], received[v]) for v in range(5)]


def shift_rate(state, fluxes, speed, low, high, axis, pos, first, last, coef):
    count = state[0].shape[axis]
    low_state, low_flux, low_speed = low
    high_state, high_flux, high_speed = high
    at_low = pos == 0
    ends = at_low | (pos == 3)

    def beside(here, below, above):
        near = jnp.where(at_low, pltpu.roll(here, 1, axis), pltpu.roll(here, count - 1, axis))
        return jnp.where(first, below, jnp.where(last, above, near))

    spread = jnp.maximum(speed, beside(speed, low_speed, high_speed))
    spread = jnp.where(ends, 3.0 * spread, 0.0)
    out = []
    for v in range(5):
        value = fluxes[v]
        above = jnp.where(last, high_flux[v], pltpu.roll(value, count - 1, axis))
        below = jnp.where(first, low_flux[v], pltpu.roll(value, 1, axis))
        total = coef[1] * above + coef[-1] * below
        for d in (-3, -2, 2, 3):
            total = total + coef[d] * pltpu.roll(value, -d % count, axis)
        out.append(spread * (beside(state[v], low_state[v], high_state[v]) - state[v]) - total)
    return out


def rate_kernel(u_ref, x1_ref, x2_ref, y1_ref, y2_ref, z1_ref, z2_ref, face_ref, rate_ref, fx_ref, sx_ref):
    x_side = tile_of(x1_ref), tile_of(x2_ref)
    y_side = tile_of(y1_ref), tile_of(y2_ref)
    z_side = tile_of(z1_ref), tile_of(z2_ref)
    shape = (16, 256)
    row = lax.broadcasted_iota(jnp.int32, shape, 0)
    lane = lax.broadcasted_iota(jnp.int32, shape, 1)
    ypos, zpos = row & 3, lane & 3

    def coefs(pos):
        out = {}
        for d in (-3, -2, -1, 1, 2, 3):
            values = [DERIV[k, k + d] if 0 <= k + d < 4 else 0.0 for k in range(4)]
            if d == 1:
                values[3] = 3.0
            if d == -1:
                values[0] = -3.0
            out[d] = by_pos(pos, values)
        return out

    ycoef, zcoef = coefs(ypos), coefs(zpos)
    yfirst, ylast = row == 0, row == 15
    zfirst, zlast = lane == 0, lane == 255

    yflip = lambda v: -1.0 if v == 2 else 1.0
    ylow = wall("gy", False, [face_ref[5 + v] for v in range(5)], [y_side[0](FACE + v) for v in range(5)], yflip)
    yhigh = wall("gy", True, [face_ref[v] for v in range(5)], [y_side[1](FACE + v) for v in range(5)], yflip)
    ylow_flux, ylow_speed = side(ylow, 1)
    yhigh_flux, yhigh_speed = side(yhigh, 1)

    def columns(first_tile, source):
        both = jnp.concatenate([source(first_tile), source(first_tile + 1)], axis=0)
        return [both if v == 0 else pltpu.roll(both, 128 - 4 * v, 1) for v in range(5)]

    own = tile_of(face_ref)
    zflip = lambda v: -1.0 if v == 3 else 1.0
    zlow = wall("gz", False, columns(12, own), columns(FACE, z_side[0]), zflip)
    zhigh = wall("gz", True, columns(10, own), columns(FACE, z_side[1]), zflip)
    zlow_flux, zlow_speed = side(zlow, 2)
    zhigh_flux, zhigh_speed = side(zhigh, 2)

    def pick_row(tile, i):
        return jnp.concatenate([tile[i : i + 1], tile[4 + i : 5 + i]], axis=1)

    for i in range(4):
        state = [u_ref[v, i] for v in range(5)]
        vel, pressure, sound, _ = primitives(state)
        xflux = flux(state, vel, pressure, 0)
        for v in range(5):
            fx_ref[v, i] = xflux[v]
        if i in (0, 3):
            sx_ref[i // 3] = jnp.abs(vel[0]) + sound
        low = ([pick_row(t, i) for t in ylow], [pick_row(t, i) for t in ylow_flux], pick_row(ylow_speed, i))
        high = ([pick_row(t, i) for t in yhigh], [pick_row(t, i) for t in yhigh_flux], pick_row(yhigh_speed, i))
        yrate = shift_rate(
            state, flux(state, vel, pressure, 1), jnp.abs(vel[1]) + sound,
            low, high, 0, ypos, yfirst, ylast, ycoef,
        )
        pick = lambda t: t[:, i : i + 1]
        low = ([pick(t) for t in zlow], [pick(t) for t in zlow_flux], pick(zlow_speed))
        high = ([pick(t) for t in zhigh], [pick(t) for t in zhigh_flux], pick(zhigh_speed))
        zrate = shift_rate(
            state, flux(state, vel, pressure, 2), jnp.abs(vel[2]) + sound,
            low, high, 1, zpos, zfirst, zlast, zcoef,
        )
        for v in range(5):
            rate_ref[v, i] = yrate[v] + zrate[v]

    xflip = lambda v: -1.0 if v == 1 else 1.0
    for half in range(2):
        for part in range(2):
            ys, zs = slice(8 * half, 8 * half + 8), slice(128 * part, 128 * part + 128)
            tile = FACE + 2 * half + part
            ends = []
            for last, i, source in ((False, 0, x_side[0]), (True, 3, x_side[1])):
                mine = [u_ref[v, i, ys, zs] for v in range(5)]
                beyond = wall("gx", last, mine, [source(tile + 4 * v) for v in range(5)], xflip)
                far_flux, far_speed = side(beyond, 0)
                spread = 3.0 * jnp.maximum(sx_ref[i // 3, ys, zs], far_speed)
                sign = -3.0 if last else 3.0
                ends.append([sign * far_flux[v] + spread * (beyond[v] - mine[v]) for v in range(5)])
            for v in range(5):
                f = [fx_ref[v, i, ys, zs] for i in range(4)]
                for j in range(4):
                    total = rate_ref[v, j, ys, zs]
                    for i in range(4):
                        if i != j:
                            total = total - float(DERIV[j, i]) * f[i]
                    if j == 0:
                        total = total + ends[0][v]
                    if j == 3:
                        total = total + ends[1][v]
                    rate_ref[v, j, ys, zs] = total


def split(value):
    high = value.astype(BF16)
    return high, (value - high.astype(F32)).astype(BF16)


def parcel_kernel(u_ref, z1_ref, z2_ref, own_ref, dep_ref, base_ref, acc_ref, vel_hi, vel_lo, z_hi, z_lo, a_hi, a_lo):
    sides = (z1_ref, own_ref, z2_ref)
    tiles = [sides[g % 3][g // 3] for g in range(27)] + [jnp.zeros((8, 128), F32)]
    for i in range(4):
        inverse = 1.0 / u_ref[0, i]
        for d in range(3):
            hi, lo = split(u_ref[d + 1, i] * inverse)
            start = 16 * (4 * d + i)
            vel_hi[start : start + 16, :] = hi
            vel_lo[start : start + 16, :] = lo
    left = lax.broadcasted_iota(jnp.int32, (8, 128), 1) < 64
    sub8 = lax.broadcasted_iota(jnp.int32, (8, 128), 0)
    sub16 = lax.broadcasted_iota(jnp.int32, (16, 128), 0)
    pos, block = sub16 & 3, sub16 >> 2
    weight_y = by_pos(pos, 1.0 / WEIGHTS)
    weight_xy = [weight_y * float(1.0 / WEIGHTS[i]) for i in range(4)]
    inner = float(NODES[2])
    kept = []
    for p in range(14):
        first, second = tiles[2 * p], tiles[2 * p + 1]
        field = jnp.where(left, first, pltpu.roll(second, 64, 1))
        code = jnp.where(left, pltpu.roll(first, 64, 1), second)
        host = code.astype(jnp.int32) - 1
        host = jnp.concatenate([host, host], axis=0)
        outer = (field + 1.0) * (field - 1.0)
        middle = (field + inner) * (field - inner)
        basis = [
            float(SCALE[0]) * middle * (field - 1.0),
            float(SCALE[1]) * outer * (field - inner),
            float(SCALE[2]) * outer * (field + inner),
            float(SCALE[3]) * middle * (field + 1.0),
        ]

        def spread(r):
            rows = [jnp.broadcast_to(basis[k][r : r + 1], (16, 128)) for k in range(4)]
            return jnp.where(pos == 0, rows[0], jnp.where(pos == 1, rows[1], jnp.where(pos == 2, rows[2], rows[3])))

        in_y = jnp.where((host >> 6) == block, spread(1), 0.0)
        in_z = spread(2)
        in_z_hi = in_z.astype(BF16).astype(F32)
        in_z_lo = in_z - in_z_hi
        offset = (host & 63) - block
        cols = slice(128 * p, 128 * p + 128)
        for t in range(16):
            here = offset == 4 * t
            z_hi[16 * t : 16 * t + 16, cols] = jnp.where(here, in_z_hi, 0.0).astype(BF16)
            z_lo[16 * t : 16 * t + 16, cols] = jnp.where(here, in_z_lo, 0.0).astype(BF16)
        kept.append((field, code, [basis[i][0:1] for i in range(4)], in_y))
    wide = jnp.dot(vel_hi[...], z_hi[...], preferred_element_type=F32)
    wide += jnp.dot(vel_lo[...], z_hi[...], preferred_element_type=F32)
    wide += jnp.dot(vel_hi[...], z_lo[...], preferred_element_type=F32)
    for p in range(14):
        field, code, in_x, in_y = kept[p]
        cols = slice(128 * p, 128 * p + 128)
        live = code > 0.5
        in_xy = [in_x[i] * in_y for i in range(4)]
        seen = []
        for d in range(3):
            mixed = None
            for i in range(4):
                start = 16 * (4 * d + i)
                term = in_xy[i] * wide[start : start + 16, cols]
                mixed = term if mixed is None else mixed + term
            seen.append(jnp.sum(mixed, axis=0, keepdims=True))
        fluid = jnp.where(sub8 == 0, seen[0], jnp.where(sub8 == 1, seen[1], seen[2]))
        speed = pltpu.roll(field, 5, 0)
        keep = live & (sub8 < 3)
        relax = jnp.where(live[0:1], field[6:7], 1.0)
        force = jnp.where(keep, (fluid - speed) / relax, 0.0)
        base = jnp.where(keep, speed, 0.0)
        base_ref[p] = base
        acc_ref[p] = force
        mass = field[7:8]
        push = -mass * force
        work = -mass * jnp.sum(force * base, axis=0, keepdims=True)
        sources = [push[0:1], push[1:2], push[2:3], work]
        for i in range(4):
            scaled = in_xy[i] * weight_xy[i]
            for d in range(4):
                hi, lo = split(sources[d] * scaled)
                start = 16 * (4 * d + i)
                a_hi[start : start + 16, cols] = hi
                a_lo[start : start + 16, cols] = lo
    lanes = (((1,), (1,)), ((), ()))
    total = lax.dot_general(a_hi[...], z_hi[...], lanes, preferred_element_type=F32)
    total += lax.dot_general(a_lo[...], z_hi[...], lanes, preferred_element_type=F32)
    total += lax.dot_general(a_hi[...], z_lo[...], lanes, preferred_element_type=F32)
    zpos = lax.broadcasted_iota(jnp.int32, (16, 256), 1) & 3
    weight_z = by_pos(zpos, 1.0 / WEIGHTS)
    for d in range(4):
        for i in range(4):
            start = 16 * (4 * d + i)
            dep_ref[d, i] = total[start : start + 16, :] * weight_z


def finish_kernel(u_ref, rate_ref, dep_ref, top_ref, base_ref, acc_ref, next_ref, vel_ref):
    top = jnp.max(jnp.max(top_ref[...], axis=0, keepdims=True), axis=1, keepdims=True)
    step = 1.0 / (7.0 * jnp.broadcast_to(top, (8, 256)))
    step16 = jnp.concatenate([step, step], axis=0)
    for v in range(5):
        for i in range(4):
            rate = rate_ref[v, i]
            if v > 0:
                rate = rate + dep_ref[v - 1, i]
            next_ref[v, i] = u_ref[v, i] + step16 * rate
    small = step[:, :128]
    for pair in range(14):
        value = base_ref[pair] + small * acc_ref[pair]
        for h in range(2):
            g = 2 * pair + h
            if g < 27:
                vel_ref[g // 9, g // 3 % 3, g % 3] = value[0:3, 64 * h : 64 * h + 64]


def exchanged(up, down, axis, wrap):
    count = lax.axis_size(axis)
    pairs = [(i, (i + 1) % count) for i in range(count if wrap else count - 1)]
    return (
        lax.ppermute(up, axis, pairs),
        lax.ppermute(down, axis, [(j, i) for i, j in pairs]),
    )


def all_tops(top, axis):
    return lax.all_to_all(top, axis, 0, 0, tiled=True)


def call(kernel, outs, scratch=(), nbytes=None):
    cost = None if nbytes is None else pl.CostEstimate(flops=0, bytes_accessed=nbytes, transcendentals=0)
    return pl.pallas_call(
        kernel,
        out_shape=outs,
        scratch_shapes=list(scratch),
        compiler_params=pltpu.CompilerParams(vmem_limit_bytes=VMEM_BYTES),
        cost_estimate=cost,
    )


def tiles_of(n):
    return jax.ShapeDtypeStruct((n, 8, 128), F32)


def local(fluid_state, parcel_data, host_element, slot_counts):
    rows = [jax.ShapeDtypeStruct((lax.axis_size(axis), 128), F32) for axis in ("gx", "gy", "gz")]
    face_up, face_down, faces, top = call(face_kernel, (tiles_of(20), tiles_of(20), tiles_of(14), rows[0]))(fluid_state)
    x_up, x_down, keep_x = call(pack_kernel, (tiles_of(29), tiles_of(29), tiles_of(9)))(
        parcel_data, host_element, slot_counts, face_up, face_down
    )
    x1, x2 = exchanged(x_up, x_down, "gx", False)
    tops = all_tops(top, "gx")
    y_up, y_down, keep_y = call(turn_y_kernel, (tiles_of(14), tiles_of(14), tiles_of(9)), nbytes=TURN_BYTES)(
        x1, x2, keep_x, faces
    )
    y1, y2 = exchanged(y_up, y_down, "gy", False)
    tops = all_tops(call(fold_kernel, rows[1])(tops, keep_y), "gy")
    z_up, z_down, keep_z = call(turn_z_kernel, (tiles_of(11), tiles_of(11), tiles_of(9)), nbytes=TURN_BYTES)(
        y1, y2, keep_y, faces
    )
    z1, z2 = exchanged(z_up, z_down, "gz", True)
    top = all_tops(call(fold_kernel, rows[2])(tops, keep_z), "gz")
    field = jax.ShapeDtypeStruct((5, 4, 16, 256), F32)
    rate = call(
        rate_kernel, field, [pltpu.VMEM((5, 4, 16, 256), F32), pltpu.VMEM((2, 16, 256), F32)],
    )(fluid_state, x1, x2, y1, y2, z1, z2, faces)
    deposit, base, acc = call(
        parcel_kernel,
        (jax.ShapeDtypeStruct((4, 4, 16, 256), F32), tiles_of(14), tiles_of(14)),
        [
            pltpu.VMEM((192, 256), BF16),
            pltpu.VMEM((192, 256), BF16),
            pltpu.VMEM((256, 1792), BF16),
            pltpu.VMEM((256, 1792), BF16),
            pltpu.VMEM((256, 1792), BF16),
            pltpu.VMEM((256, 1792), BF16),
        ],
    )(fluid_state, z1, z2, keep_z)
    return call(finish_kernel, (field, jax.ShapeDtypeStruct((3, 3, 3, 3, 64), F32)))(
        fluid_state, rate, deposit, top, base, acc
    )


def solution(mesh):
    placed = (
        P(None, "gx", "gy", "gz"),
        P("gx", "gy", "gz", None, None),
        P("gx", "gy", "gz", None),
        P("gx", "gy", "gz"),
    )
    return jax.shard_map(
        local,
        mesh=mesh,
        in_specs=placed,
        out_specs=(P(None, "gx", "gy", "gz"), P("gx", "gy", "gz", None, None)),
        check_vma=False,
    )
```

```python
import jax
import jax.numpy as jnp
import numpy as np
from jax import lax
from jax.experimental import pallas as pl
from jax.experimental.pallas import tpu as pltpu
from jax.sharding import PartitionSpec as P

F32 = jnp.float32
BF16 = jnp.bfloat16
VMEM_BYTES = 24 * 1024 * 1024
TURN_BYTES = 64 * 1024 * 1024

NODES = np.array([-1.0, -1.0 / np.sqrt(5.0), 1.0 / np.sqrt(5.0), 1.0])
WEIGHTS = np.array([1.0 / 6.0, 5.0 / 6.0, 5.0 / 6.0, 1.0 / 6.0])


def derivative_table():
    factor = [np.prod([NODES[i] - NODES[j] for j in range(4) if j != i]) for i in range(4)]
    table = np.zeros((4, 4))
    for i in range(4):
        for j in range(4):
            if i != j:
                table[i, j] = factor[i] / (factor[j] * (NODES[i] - NODES[j]))
    return table


DERIV = derivative_table()
SCALE = [1.0 / np.prod([NODES[i] - NODES[j] for j in range(4) if j != i]) for i in range(4)]

FACE = 9


def by_pos(pos, values):
    out = jnp.full(pos.shape, float(values[3]), F32)
    for k in range(3):
        out = jnp.where(pos == k, float(values[k]), out)
    return out


def primitives(state):
    inverse = 1.0 / state[0]
    vel = [state[d + 1] * inverse for d in range(3)]
    square = vel[0] * vel[0] + vel[1] * vel[1] + vel[2] * vel[2]
    pressure = 0.4 * (state[4] - 0.5 * state[0] * square)
    sound = jnp.sqrt(1.4 * pressure * inverse)
    return vel, pressure, sound, square


def flux(state, vel, pressure, d):
    normal = vel[d]
    out = [state[d + 1]]
    for k in range(3):
        term = state[k + 1] * normal
        out.append(term + pressure if k == d else term)
    out.append((state[4] + pressure) * normal)
    return out


def side(state, d):
    vel, pressure, sound, _ = primitives(state)
    return flux(state, vel, pressure, d), jnp.abs(vel[d]) + sound


def tile_of(ref):
    return lambda tile: ref[tile]


def face_kernel(u_ref, up_ref, down_ref, face_ref, top_ref):
    top = None
    for i in range(4):
        _, _, sound, square = primitives([u_ref[v, i] for v in range(5)])
        speed = jnp.sqrt(square) + sound
        top = speed if top is None else jnp.maximum(top, speed)
    top = jnp.maximum(top[:, :128], top[:, 128:])
    top_ref[...] = jnp.broadcast_to(jnp.max(top, axis=0, keepdims=True), top_ref.shape)
    for v in range(5):
        for yh in range(2):
            for zh in range(2):
                tile = 4 * v + 2 * yh + zh
                ys, zs = slice(8 * yh, 8 * yh + 8), slice(128 * zh, 128 * zh + 128)
                up_ref[tile] = u_ref[v, 3, ys, zs]
                down_ref[tile] = u_ref[v, 0, ys, zs]
        for i in range(4):
            for zh in range(2):
                zs = slice(128 * zh, 128 * zh + 128)
                row = 4 * zh + i
                face_ref[v, row : row + 1, :] = u_ref[v, i, 15:16, zs]
                face_ref[5 + v, row : row + 1, :] = u_ref[v, i, 0:1, zs]
    lane = lax.broadcasted_iota(jnp.int32, (16, 128), 1)
    high = jnp.zeros((16, 128), F32)
    low = jnp.zeros((16, 128), F32)
    for v in range(5):
        for i in range(4):
            here = lane == 4 * v + i
            high = jnp.where(here, u_ref[v, i, :, 255:256], high)
            low = jnp.where(here, u_ref[v, i, :, 0:1], low)
    for yh in range(2):
        face_ref[10 + yh] = high[8 * yh : 8 * yh + 8]
        face_ref[12 + yh] = low[8 * yh : 8 * yh + 8]


def pack_kernel(data_ref, host_ref, count_ref, face_up_ref, face_down_ref, up_ref, down_ref, keep_ref):
    slot = lax.broadcasted_iota(jnp.int32, (1, 64), 1)
    for a, out in ((2, up_ref), (0, down_ref), (1, keep_ref)):
        for b in range(3):
            for c in range(3):
                count = count_ref[a, b : b + 1, c : c + 1]
                host = host_ref[a, b, c : c + 1, :]
                code = jnp.where(slot < count, host + 1, 0).astype(F32)
                out[3 * b + c, :, 0:64] = data_ref[a, b, c]
                out[3 * b + c, :, 64:128] = jnp.broadcast_to(code, (8, 64))
    for t in range(20):
        up_ref[FACE + t] = face_up_ref[t]
        down_ref[FACE + t] = face_down_ref[t]


def turn_y_kernel(low_ref, high_ref, own_ref, face_ref, up_ref, down_ref, keep_ref):
    for a, source in enumerate((low_ref, own_ref, high_ref)):
        for c in range(3):
            up_ref[3 * a + c] = source[6 + c]
            down_ref[3 * a + c] = source[c]
            keep_ref[3 * a + c] = source[3 + c]
    for v in range(5):
        up_ref[FACE + v] = face_ref[v]
        down_ref[FACE + v] = face_ref[5 + v]


def turn_z_kernel(low_ref, high_ref, own_ref, face_ref, folded_ref, up_ref, down_ref, keep_ref):
    for b, source in enumerate((low_ref, own_ref, high_ref)):
        for a in range(3):
            up_ref[3 * a + b] = source[3 * a + 2]
            down_ref[3 * a + b] = source[3 * a]
            keep_ref[3 * a + b] = source[3 * a + 1]
    for yh in range(2):
        up_ref[FACE + yh] = face_ref[10 + yh]
        down_ref[FACE + yh] = face_ref[12 + yh]


def fold_kernel(tops_ref, turned_ref, top_ref):
    top_ref[...] = jnp.broadcast_to(jnp.max(tops_ref[...], axis=0, keepdims=True), top_ref.shape)


def wall(axis, last, own, received, sign_of):
    at = lax.axis_index(axis) == (lax.axis_size(axis) - 1 if last else 0)
    pick = jnp.full(received[0].shape, at.astype(jnp.int32), jnp.int32) == 1
    return [jnp.where(pick, sign_of(v) * own[v], received[v]) for v in range(5)]


def shift_rate(state, fluxes, speed, low, high, axis, pos, first, last, coef):
    count = state[0].shape[axis]
    low_state, low_flux, low_speed = low
    high_state, high_flux, high_speed = high
    at_low = pos == 0
    ends = at_low | (pos == 3)

    def beside(here, below, above):
        near = jnp.where(at_low, pltpu.roll(here, 1, axis), pltpu.roll(here, count - 1, axis))
        return jnp.where(first, below, jnp.where(last, above, near))

    spread = jnp.maximum(speed, beside(speed, low_speed, high_speed))
    spread = jnp.where(ends, 3.0 * spread, 0.0)
    out = []
    for v in range(5):
        value = fluxes[v]
        above = jnp.where(last, high_flux[v], pltpu.roll(value, count - 1, axis))
        below = jnp.where(first, low_flux[v], pltpu.roll(value, 1, axis))
        total = coef[1] * above + coef[-1] * below
        for d in (-3, -2, 2, 3):
            total = total + coef[d] * pltpu.roll(value, -d % count, axis)
        out.append(spread * (beside(state[v], low_state[v], high_state[v]) - state[v]) - total)
    return out


def rate_kernel(u_ref, x1_ref, x2_ref, y1_ref, y2_ref, z1_ref, z2_ref, face_ref, folded_ref, rate_ref, fx_ref, sx_ref):
    x_side = tile_of(x1_ref), tile_of(x2_ref)
    y_side = tile_of(y1_ref), tile_of(y2_ref)
    z_side = tile_of(z1_ref), tile_of(z2_ref)
    shape = (16, 256)
    row = lax.broadcasted_iota(jnp.int32, shape, 0)
    lane = lax.broadcasted_iota(jnp.int32, shape, 1)
    ypos, zpos = row & 3, lane & 3

    def coefs(pos):
        out = {}
        for d in (-3, -2, -1, 1, 2, 3):
            values = [DERIV[k, k + d] if 0 <= k + d < 4 else 0.0 for k in range(4)]
            if d == 1:
                values[3] = 3.0
            if d == -1:
                values[0] = -3.0
            out[d] = by_pos(pos, values)
        return out

    ycoef, zcoef = coefs(ypos), coefs(zpos)
    yfirst, ylast = row == 0, row == 15
    zfirst, zlast = lane == 0, lane == 255

    yflip = lambda v: -1.0 if v == 2 else 1.0
    ylow = wall("gy", False, [face_ref[5 + v] for v in range(5)], [y_side[0](FACE + v) for v in range(5)], yflip)
    yhigh = wall("gy", True, [face_ref[v] for v in range(5)], [y_side[1](FACE + v) for v in range(5)], yflip)
    ylow_flux, ylow_speed = side(ylow, 1)
    yhigh_flux, yhigh_speed = side(yhigh, 1)

    def columns(first_tile, source):
        both = jnp.concatenate([source(first_tile), source(first_tile + 1)], axis=0)
        return [both if v == 0 else pltpu.roll(both, 128 - 4 * v, 1) for v in range(5)]

    own = tile_of(face_ref)
    zflip = lambda v: -1.0 if v == 3 else 1.0
    zlow = wall("gz", False, columns(12, own), columns(FACE, z_side[0]), zflip)
    zhigh = wall("gz", True, columns(10, own), columns(FACE, z_side[1]), zflip)
    zlow_flux, zlow_speed = side(zlow, 2)
    zhigh_flux, zhigh_speed = side(zhigh, 2)

    def pick_row(tile, i):
        return jnp.concatenate([tile[i : i + 1], tile[4 + i : 5 + i]], axis=1)

    for i in range(4):
        state = [u_ref[v, i] for v in range(5)]
        vel, pressure, sound, _ = primitives(state)
        xflux = flux(state, vel, pressure, 0)
        for v in range(5):
            fx_ref[v, i] = xflux[v]
        if i in (0, 3):
            sx_ref[i // 3] = jnp.abs(vel[0]) + sound
        low = ([pick_row(t, i) for t in ylow], [pick_row(t, i) for t in ylow_flux], pick_row(ylow_speed, i))
        high = ([pick_row(t, i) for t in yhigh], [pick_row(t, i) for t in yhigh_flux], pick_row(yhigh_speed, i))
        yrate = shift_rate(
            state, flux(state, vel, pressure, 1), jnp.abs(vel[1]) + sound,
            low, high, 0, ypos, yfirst, ylast, ycoef,
        )
        pick = lambda t: t[:, i : i + 1]
        low = ([pick(t) for t in zlow], [pick(t) for t in zlow_flux], pick(zlow_speed))
        high = ([pick(t) for t in zhigh], [pick(t) for t in zhigh_flux], pick(zhigh_speed))
        zrate = shift_rate(
            state, flux(state, vel, pressure, 2), jnp.abs(vel[2]) + sound,
            low, high, 1, zpos, zfirst, zlast, zcoef,
        )
        for v in range(5):
            rate_ref[v, i] = yrate[v] + zrate[v]

    xflip = lambda v: -1.0 if v == 1 else 1.0
    for half in range(2):
        for part in range(2):
            ys, zs = slice(8 * half, 8 * half + 8), slice(128 * part, 128 * part + 128)
            tile = FACE + 2 * half + part
            ends = []
            for last, i, source in ((False, 0, x_side[0]), (True, 3, x_side[1])):
                mine = [u_ref[v, i, ys, zs] for v in range(5)]
                beyond = wall("gx", last, mine, [source(tile + 4 * v) for v in range(5)], xflip)
                far_flux, far_speed = side(beyond, 0)
                spread = 3.0 * jnp.maximum(sx_ref[i // 3, ys, zs], far_speed)
                sign = -3.0 if last else 3.0
                ends.append([sign * far_flux[v] + spread * (beyond[v] - mine[v]) for v in range(5)])
            for v in range(5):
                f = [fx_ref[v, i, ys, zs] for i in range(4)]
                for j in range(4):
                    total = rate_ref[v, j, ys, zs]
                    for i in range(4):
                        if i != j:
                            total = total - float(DERIV[j, i]) * f[i]
                    if j == 0:
                        total = total + ends[0][v]
                    if j == 3:
                        total = total + ends[1][v]
                    rate_ref[v, j, ys, zs] = total


def split(value):
    high = value.astype(BF16)
    return high, (value - high.astype(F32)).astype(BF16)


def parcel_kernel(u_ref, z1_ref, z2_ref, own_ref, dep_ref, base_ref, acc_ref, vel_hi, vel_lo, z_hi, z_lo, a_hi, a_lo):
    sides = (z1_ref, own_ref, z2_ref)
    tiles = [sides[g % 3][g // 3] for g in range(27)] + [jnp.zeros((8, 128), F32)]
    for i in range(4):
        inverse = 1.0 / u_ref[0, i]
        for d in range(3):
            hi, lo = split(u_ref[d + 1, i] * inverse)
            start = 16 * (4 * d + i)
            vel_hi[start : start + 16, :] = hi
            vel_lo[start : start + 16, :] = lo
    left = lax.broadcasted_iota(jnp.int32, (8, 128), 1) < 64
    sub8 = lax.broadcasted_iota(jnp.int32, (8, 128), 0)
    sub16 = lax.broadcasted_iota(jnp.int32, (16, 128), 0)
    pos, block = sub16 & 3, sub16 >> 2
    weight_y = by_pos(pos, 1.0 / WEIGHTS)
    weight_xy = [weight_y * float(1.0 / WEIGHTS[i]) for i in range(4)]
    inner = float(NODES[2])
    kept = []
    for p in range(14):
        first, second = tiles[2 * p], tiles[2 * p + 1]
        field = jnp.where(left, first, pltpu.roll(second, 64, 1))
        code = jnp.where(left, pltpu.roll(first, 64, 1), second)
        host = code.astype(jnp.int32) - 1
        host = jnp.concatenate([host, host], axis=0)
        outer = (field + 1.0) * (field - 1.0)
        middle = (field + inner) * (field - inner)
        basis = [
            float(SCALE[0]) * middle * (field - 1.0),
            float(SCALE[1]) * outer * (field - inner),
            float(SCALE[2]) * outer * (field + inner),
            float(SCALE[3]) * middle * (field + 1.0),
        ]

        def spread(r):
            rows = [jnp.broadcast_to(basis[k][r : r + 1], (16, 128)) for k in range(4)]
            return jnp.where(pos == 0, rows[0], jnp.where(pos == 1, rows[1], jnp.where(pos == 2, rows[2], rows[3])))

        in_y = jnp.where((host >> 6) == block, spread(1), 0.0)
        in_z = spread(2)
        in_z_hi = in_z.astype(BF16).astype(F32)
        in_z_lo = in_z - in_z_hi
        offset = (host & 63) - block
        cols = slice(128 * p, 128 * p + 128)
        for t in range(16):
            here = offset == 4 * t
            z_hi[16 * t : 16 * t + 16, cols] = jnp.where(here, in_z_hi, 0.0).astype(BF16)
            z_lo[16 * t : 16 * t + 16, cols] = jnp.where(here, in_z_lo, 0.0).astype(BF16)
        kept.append((field, code, [basis[i][0:1] for i in range(4)], in_y))
    wide = jnp.dot(vel_hi[...], z_hi[...], preferred_element_type=F32)
    wide += jnp.dot(vel_lo[...], z_hi[...], preferred_element_type=F32)
    wide += jnp.dot(vel_hi[...], z_lo[...], preferred_element_type=F32)
    for p in range(14):
        field, code, in_x, in_y = kept[p]
        cols = slice(128 * p, 128 * p + 128)
        live = code > 0.5
        in_xy = [in_x[i] * in_y for i in range(4)]
        seen = []
        for d in range(3):
            mixed = None
            for i in range(4):
                start = 16 * (4 * d + i)
                term = in_xy[i] * wide[start : start + 16, cols]
                mixed = term if mixed is None else mixed + term
            seen.append(jnp.sum(mixed, axis=0, keepdims=True))
        fluid = jnp.where(sub8 == 0, seen[0], jnp.where(sub8 == 1, seen[1], seen[2]))
        speed = pltpu.roll(field, 5, 0)
        keep = live & (sub8 < 3)
        relax = jnp.where(live[0:1], field[6:7], 1.0)
        force = jnp.where(keep, (fluid - speed) / relax, 0.0)
        base = jnp.where(keep, speed, 0.0)
        base_ref[p] = base
        acc_ref[p] = force
        mass = field[7:8]
        push = -mass * force
        work = -mass * jnp.sum(force * base, axis=0, keepdims=True)
        sources = [push[0:1], push[1:2], push[2:3], work]
        for i in range(4):
            scaled = in_xy[i] * weight_xy[i]
            for d in range(4):
                hi, lo = split(sources[d] * scaled)
                start = 16 * (4 * d + i)
                a_hi[start : start + 16, cols] = hi
                a_lo[start : start + 16, cols] = lo
    lanes = (((1,), (1,)), ((), ()))
    total = lax.dot_general(a_hi[...], z_hi[...], lanes, preferred_element_type=F32)
    total += lax.dot_general(a_lo[...], z_hi[...], lanes, preferred_element_type=F32)
    total += lax.dot_general(a_hi[...], z_lo[...], lanes, preferred_element_type=F32)
    zpos = lax.broadcasted_iota(jnp.int32, (16, 256), 1) & 3
    weight_z = by_pos(zpos, 1.0 / WEIGHTS)
    for d in range(4):
        for i in range(4):
            start = 16 * (4 * d + i)
            dep_ref[d, i] = total[start : start + 16, :] * weight_z


def finish_kernel(u_ref, rate_ref, dep_ref, top_ref, base_ref, acc_ref, next_ref, vel_ref):
    top = jnp.max(jnp.max(top_ref[...], axis=0, keepdims=True), axis=1, keepdims=True)
    step = 1.0 / (7.0 * jnp.broadcast_to(top, (8, 256)))
    step16 = jnp.concatenate([step, step], axis=0)
    for v in range(5):
        for i in range(4):
            rate = rate_ref[v, i]
            if v > 0:
                rate = rate + dep_ref[v - 1, i]
            next_ref[v, i] = u_ref[v, i] + step16 * rate
    small = step[:, :128]
    for pair in range(14):
        value = base_ref[pair] + small * acc_ref[pair]
        for h in range(2):
            g = 2 * pair + h
            if g < 27:
                vel_ref[g // 9, g // 3 % 3, g % 3] = value[0:3, 64 * h : 64 * h + 64]


def exchanged(up, down, axis, wrap):
    count = lax.axis_size(axis)
    pairs = [(i, (i + 1) % count) for i in range(count if wrap else count - 1)]
    return (
        lax.ppermute(up, axis, pairs),
        lax.ppermute(down, axis, [(j, i) for i, j in pairs]),
    )


def all_tops(top, axis):
    return lax.all_to_all(top, axis, 0, 0, tiled=True)


def call(kernel, outs, scratch=(), nbytes=None):
    cost = None if nbytes is None else pl.CostEstimate(flops=0, bytes_accessed=nbytes, transcendentals=0)
    return pl.pallas_call(
        kernel,
        out_shape=outs,
        scratch_shapes=list(scratch),
        compiler_params=pltpu.CompilerParams(vmem_limit_bytes=VMEM_BYTES),
        cost_estimate=cost,
    )


def tiles_of(n):
    return jax.ShapeDtypeStruct((n, 8, 128), F32)


def local(fluid_state, parcel_data, host_element, slot_counts):
    rows = [jax.ShapeDtypeStruct((lax.axis_size(axis), 128), F32) for axis in ("gx", "gy", "gz")]
    face_up, face_down, faces, top = call(face_kernel, (tiles_of(20), tiles_of(20), tiles_of(14), rows[0]))(fluid_state)
    x_up, x_down, keep_x = call(pack_kernel, (tiles_of(29), tiles_of(29), tiles_of(9)))(
        parcel_data, host_element, slot_counts, face_up, face_down
    )
    x1, x2 = exchanged(x_up, x_down, "gx", False)
    tops = all_tops(top, "gx")
    y_up, y_down, keep_y = call(turn_y_kernel, (tiles_of(14), tiles_of(14), tiles_of(9)), nbytes=TURN_BYTES)(
        x1, x2, keep_x, faces
    )
    y1, y2 = exchanged(y_up, y_down, "gy", False)
    fold = call(fold_kernel, rows[1])(tops, keep_y)
    tops = all_tops(fold, "gy")
    z_up, z_down, keep_z = call(turn_z_kernel, (tiles_of(11), tiles_of(11), tiles_of(9)), nbytes=TURN_BYTES)(
        y1, y2, keep_y, faces, fold
    )
    z1, z2 = exchanged(z_up, z_down, "gz", True)
    fold = call(fold_kernel, rows[2])(tops, keep_z)
    top = all_tops(fold, "gz")
    field = jax.ShapeDtypeStruct((5, 4, 16, 256), F32)
    rate = call(
        rate_kernel, field, [pltpu.VMEM((5, 4, 16, 256), F32), pltpu.VMEM((2, 16, 256), F32)],
    )(fluid_state, x1, x2, y1, y2, z1, z2, faces, fold)
    deposit, base, acc = call(
        parcel_kernel,
        (jax.ShapeDtypeStruct((4, 4, 16, 256), F32), tiles_of(14), tiles_of(14)),
        [
            pltpu.VMEM((192, 256), BF16),
            pltpu.VMEM((192, 256), BF16),
            pltpu.VMEM((256, 1792), BF16),
            pltpu.VMEM((256, 1792), BF16),
            pltpu.VMEM((256, 1792), BF16),
            pltpu.VMEM((256, 1792), BF16),
        ],
    )(fluid_state, z1, z2, keep_z)
    return call(finish_kernel, (field, jax.ShapeDtypeStruct((3, 3, 3, 3, 64), F32)))(
        fluid_state, rate, deposit, top, base, acc
    )


def solution(mesh):
    placed = (
        P(None, "gx", "gy", "gz"),
        P("gx", "gy", "gz", None, None),
        P("gx", "gy", "gz", None),
        P("gx", "gy", "gz"),
    )
    return jax.shard_map(
        local,
        mesh=mesh,
        in_specs=placed,
        out_specs=(P(None, "gx", "gy", "gz"), P("gx", "gy", "gz", None, None)),
        check_vma=False,
    )
```

```python
import jax
import jax.numpy as jnp
import numpy as np
from jax import lax
from jax.experimental import pallas as pl
from jax.experimental.pallas import tpu as pltpu
from jax.sharding import PartitionSpec as P

F32 = jnp.float32
BF16 = jnp.bfloat16
VMEM_BYTES = 24 * 1024 * 1024

NODES = np.array([-1.0, -1.0 / np.sqrt(5.0), 1.0 / np.sqrt(5.0), 1.0])
WEIGHTS = np.array([1.0 / 6.0, 5.0 / 6.0, 5.0 / 6.0, 1.0 / 6.0])


def derivative_table():
    factor = [np.prod([NODES[i] - NODES[j] for j in range(4) if j != i]) for i in range(4)]
    table = np.zeros((4, 4))
    for i in range(4):
        for j in range(4):
            if i != j:
                table[i, j] = factor[i] / (factor[j] * (NODES[i] - NODES[j]))
    return table


DERIV = derivative_table()
SCALE = [1.0 / np.prod([NODES[i] - NODES[j] for j in range(4) if j != i]) for i in range(4)]

FACE = 9


def by_pos(pos, values):
    out = jnp.full(pos.shape, float(values[3]), F32)
    for k in range(3):
        out = jnp.where(pos == k, float(values[k]), out)
    return out


def primitives(state):
    inverse = 1.0 / state[0]
    vel = [state[d + 1] * inverse for d in range(3)]
    square = vel[0] * vel[0] + vel[1] * vel[1] + vel[2] * vel[2]
    pressure = 0.4 * (state[4] - 0.5 * state[0] * square)
    sound = jnp.sqrt(1.4 * pressure * inverse)
    return vel, pressure, sound, square


def flux(state, vel, pressure, d):
    normal = vel[d]
    out = [state[d + 1]]
    for k in range(3):
        term = state[k + 1] * normal
        out.append(term + pressure if k == d else term)
    out.append((state[4] + pressure) * normal)
    return out


def side(state, d):
    vel, pressure, sound, _ = primitives(state)
    return flux(state, vel, pressure, d), jnp.abs(vel[d]) + sound


def tile_of(ref):
    return lambda tile: ref[tile]


def face_kernel(u_ref, up_ref, down_ref, face_ref, top_ref):
    top = None
    for i in range(4):
        _, _, sound, square = primitives([u_ref[v, i] for v in range(5)])
        speed = jnp.sqrt(square) + sound
        top = speed if top is None else jnp.maximum(top, speed)
    top = jnp.maximum(top[:, :128], top[:, 128:])
    top_ref[...] = jnp.broadcast_to(jnp.max(top, axis=0, keepdims=True), top_ref.shape)
    for v in range(5):
        for yh in range(2):
            for zh in range(2):
                tile = 4 * v + 2 * yh + zh
                ys, zs = slice(8 * yh, 8 * yh + 8), slice(128 * zh, 128 * zh + 128)
                up_ref[tile] = u_ref[v, 3, ys, zs]
                down_ref[tile] = u_ref[v, 0, ys, zs]
        for i in range(4):
            for zh in range(2):
                zs = slice(128 * zh, 128 * zh + 128)
                row = 4 * zh + i
                face_ref[v, row : row + 1, :] = u_ref[v, i, 15:16, zs]
                face_ref[5 + v, row : row + 1, :] = u_ref[v, i, 0:1, zs]
    lane = lax.broadcasted_iota(jnp.int32, (16, 128), 1)
    high = jnp.zeros((16, 128), F32)
    low = jnp.zeros((16, 128), F32)
    for v in range(5):
        for i in range(4):
            here = lane == 4 * v + i
            high = jnp.where(here, u_ref[v, i, :, 255:256], high)
            low = jnp.where(here, u_ref[v, i, :, 0:1], low)
    for yh in range(2):
        face_ref[10 + yh] = high[8 * yh : 8 * yh + 8]
        face_ref[12 + yh] = low[8 * yh : 8 * yh + 8]


def pack_kernel(data_ref, host_ref, count_ref, face_up_ref, face_down_ref, up_ref, down_ref, keep_ref):
    slot = lax.broadcasted_iota(jnp.int32, (1, 64), 1)
    for a, out in ((2, up_ref), (0, down_ref), (1, keep_ref)):
        for b in range(3):
            for c in range(3):
                count = count_ref[a, b : b + 1, c : c + 1]
                host = host_ref[a, b, c : c + 1, :]
                code = jnp.where(slot < count, host + 1, 0).astype(F32)
                out[3 * b + c, :, 0:64] = data_ref[a, b, c]
                out[3 * b + c, :, 64:128] = jnp.broadcast_to(code, (8, 64))
    for t in range(20):
        up_ref[FACE + t] = face_up_ref[t]
        down_ref[FACE + t] = face_down_ref[t]


def turn_y_kernel(low_ref, high_ref, own_ref, face_ref, tops_ref, up_ref, down_ref, keep_ref, top_ref):
    top_ref[...] = jnp.broadcast_to(jnp.max(tops_ref[...], axis=0, keepdims=True), top_ref.shape)
    for a, source in enumerate((low_ref, own_ref, high_ref)):
        for c in range(3):
            up_ref[3 * a + c] = source[6 + c]
            down_ref[3 * a + c] = source[c]
            keep_ref[3 * a + c] = source[3 + c]
    for v in range(5):
        up_ref[FACE + v] = face_ref[v]
        down_ref[FACE + v] = face_ref[5 + v]


def turn_z_kernel(low_ref, high_ref, own_ref, face_ref, up_ref, down_ref, keep_ref):
    for b, source in enumerate((low_ref, own_ref, high_ref)):
        for a in range(3):
            up_ref[3 * a + b] = source[3 * a + 2]
            down_ref[3 * a + b] = source[3 * a]
            keep_ref[3 * a + b] = source[3 * a + 1]
    for yh in range(2):
        up_ref[FACE + yh] = face_ref[10 + yh]
        down_ref[FACE + yh] = face_ref[12 + yh]


def wall(axis, last, own, received, sign_of):
    at = lax.axis_index(axis) == (lax.axis_size(axis) - 1 if last else 0)
    pick = jnp.full(received[0].shape, at.astype(jnp.int32), jnp.int32) == 1
    return [jnp.where(pick, sign_of(v) * own[v], received[v]) for v in range(5)]


def shift_rate(state, fluxes, speed, low, high, axis, pos, first, last, coef):
    count = state[0].shape[axis]
    low_state, low_flux, low_speed = low
    high_state, high_flux, high_speed = high
    at_low = pos == 0
    ends = at_low | (pos == 3)

    def beside(here, below, above):
        near = jnp.where(at_low, pltpu.roll(here, 1, axis), pltpu.roll(here, count - 1, axis))
        return jnp.where(first, below, jnp.where(last, above, near))

    spread = jnp.maximum(speed, beside(speed, low_speed, high_speed))
    spread = jnp.where(ends, 3.0 * spread, 0.0)
    out = []
    for v in range(5):
        value = fluxes[v]
        above = jnp.where(last, high_flux[v], pltpu.roll(value, count - 1, axis))
        below = jnp.where(first, low_flux[v], pltpu.roll(value, 1, axis))
        total = coef[1] * above + coef[-1] * below
        for d in (-3, -2, 2, 3):
            total = total + coef[d] * pltpu.roll(value, -d % count, axis)
        out.append(spread * (beside(state[v], low_state[v], high_state[v]) - state[v]) - total)
    return out


def rate_kernel(u_ref, x1_ref, x2_ref, y1_ref, y2_ref, z1_ref, z2_ref, face_ref, rate_ref, fx_ref, sx_ref):
    x_side = tile_of(x1_ref), tile_of(x2_ref)
    y_side = tile_of(y1_ref), tile_of(y2_ref)
    z_side = tile_of(z1_ref), tile_of(z2_ref)
    shape = (16, 256)
    row = lax.broadcasted_iota(jnp.int32, shape, 0)
    lane = lax.broadcasted_iota(jnp.int32, shape, 1)
    ypos, zpos = row & 3, lane & 3

    def coefs(pos):
        out = {}
        for d in (-3, -2, -1, 1, 2, 3):
            values = [DERIV[k, k + d] if 0 <= k + d < 4 else 0.0 for k in range(4)]
            if d == 1:
                values[3] = 3.0
            if d == -1:
                values[0] = -3.0
            out[d] = by_pos(pos, values)
        return out

    ycoef, zcoef = coefs(ypos), coefs(zpos)
    yfirst, ylast = row == 0, row == 15
    zfirst, zlast = lane == 0, lane == 255

    yflip = lambda v: -1.0 if v == 2 else 1.0
    ylow = wall("gy", False, [face_ref[5 + v] for v in range(5)], [y_side[0](FACE + v) for v in range(5)], yflip)
    yhigh = wall("gy", True, [face_ref[v] for v in range(5)], [y_side[1](FACE + v) for v in range(5)], yflip)
    ylow_flux, ylow_speed = side(ylow, 1)
    yhigh_flux, yhigh_speed = side(yhigh, 1)

    def columns(first_tile, source):
        both = jnp.concatenate([source(first_tile), source(first_tile + 1)], axis=0)
        return [both if v == 0 else pltpu.roll(both, 128 - 4 * v, 1) for v in range(5)]

    own = tile_of(face_ref)
    zflip = lambda v: -1.0 if v == 3 else 1.0
    zlow = wall("gz", False, columns(12, own), columns(FACE, z_side[0]), zflip)
    zhigh = wall("gz", True, columns(10, own), columns(FACE, z_side[1]), zflip)
    zlow_flux, zlow_speed = side(zlow, 2)
    zhigh_flux, zhigh_speed = side(zhigh, 2)

    def pick_row(tile, i):
        return jnp.concatenate([tile[i : i + 1], tile[4 + i : 5 + i]], axis=1)

    for i in range(4):
        state = [u_ref[v, i] for v in range(5)]
        vel, pressure, sound, _ = primitives(state)
        xflux = flux(state, vel, pressure, 0)
        for v in range(5):
            fx_ref[v, i] = xflux[v]
        if i in (0, 3):
            sx_ref[i // 3] = jnp.abs(vel[0]) + sound
        low = ([pick_row(t, i) for t in ylow], [pick_row(t, i) for t in ylow_flux], pick_row(ylow_speed, i))
        high = ([pick_row(t, i) for t in yhigh], [pick_row(t, i) for t in yhigh_flux], pick_row(yhigh_speed, i))
        yrate = shift_rate(
            state, flux(state, vel, pressure, 1), jnp.abs(vel[1]) + sound,
            low, high, 0, ypos, yfirst, ylast, ycoef,
        )
        pick = lambda t: t[:, i : i + 1]
        low = ([pick(t) for t in zlow], [pick(t) for t in zlow_flux], pick(zlow_speed))
        high = ([pick(t) for t in zhigh], [pick(t) for t in zhigh_flux], pick(zhigh_speed))
        zrate = shift_rate(
            state, flux(state, vel, pressure, 2), jnp.abs(vel[2]) + sound,
            low, high, 1, zpos, zfirst, zlast, zcoef,
        )
        for v in range(5):
            rate_ref[v, i] = yrate[v] + zrate[v]

    xflip = lambda v: -1.0 if v == 1 else 1.0
    for half in range(2):
        for part in range(2):
            ys, zs = slice(8 * half, 8 * half + 8), slice(128 * part, 128 * part + 128)
            tile = FACE + 2 * half + part
            ends = []
            for last, i, source in ((False, 0, x_side[0]), (True, 3, x_side[1])):
                mine = [u_ref[v, i, ys, zs] for v in range(5)]
                beyond = wall("gx", last, mine, [source(tile + 4 * v) for v in range(5)], xflip)
                far_flux, far_speed = side(beyond, 0)
                spread = 3.0 * jnp.maximum(sx_ref[i // 3, ys, zs], far_speed)
                sign = -3.0 if last else 3.0
                ends.append([sign * far_flux[v] + spread * (beyond[v] - mine[v]) for v in range(5)])
            for v in range(5):
                f = [fx_ref[v, i, ys, zs] for i in range(4)]
                for j in range(4):
                    total = rate_ref[v, j, ys, zs]
                    for i in range(4):
                        if i != j:
                            total = total - float(DERIV[j, i]) * f[i]
                    if j == 0:
                        total = total + ends[0][v]
                    if j == 3:
                        total = total + ends[1][v]
                    rate_ref[v, j, ys, zs] = total


def split(value):
    high = value.astype(BF16)
    return high, (value - high.astype(F32)).astype(BF16)


def parcel_kernel(u_ref, z1_ref, z2_ref, own_ref, dep_ref, base_ref, acc_ref, vel_hi, vel_lo, z_hi, z_lo, a_hi, a_lo):
    sides = (z1_ref, own_ref, z2_ref)
    tiles = [sides[g % 3][g // 3] for g in range(27)] + [jnp.zeros((8, 128), F32)]
    for i in range(4):
        inverse = 1.0 / u_ref[0, i]
        for d in range(3):
            hi, lo = split(u_ref[d + 1, i] * inverse)
            start = 16 * (4 * d + i)
            vel_hi[start : start + 16, :] = hi
            vel_lo[start : start + 16, :] = lo
    left = lax.broadcasted_iota(jnp.int32, (8, 128), 1) < 64
    sub8 = lax.broadcasted_iota(jnp.int32, (8, 128), 0)
    sub16 = lax.broadcasted_iota(jnp.int32, (16, 128), 0)
    pos, block = sub16 & 3, sub16 >> 2
    weight_y = by_pos(pos, 1.0 / WEIGHTS)
    weight_xy = [weight_y * float(1.0 / WEIGHTS[i]) for i in range(4)]
    inner = float(NODES[2])
    kept = []
    for p in range(14):
        first, second = tiles[2 * p], tiles[2 * p + 1]
        field = jnp.where(left, first, pltpu.roll(second, 64, 1))
        code = jnp.where(left, pltpu.roll(first, 64, 1), second)
        host = code.astype(jnp.int32) - 1
        host = jnp.concatenate([host, host], axis=0)
        outer = (field + 1.0) * (field - 1.0)
        middle = (field + inner) * (field - inner)
        basis = [
            float(SCALE[0]) * middle * (field - 1.0),
            float(SCALE[1]) * outer * (field - inner),
            float(SCALE[2]) * outer * (field + inner),
            float(SCALE[3]) * middle * (field + 1.0),
        ]

        def spread(r):
            rows = [jnp.broadcast_to(basis[k][r : r + 1], (16, 128)) for k in range(4)]
            return jnp.where(pos == 0, rows[0], jnp.where(pos == 1, rows[1], jnp.where(pos == 2, rows[2], rows[3])))

        in_y = jnp.where((host >> 6) == block, spread(1), 0.0)
        in_z = spread(2)
        in_z_hi = in_z.astype(BF16).astype(F32)
        in_z_lo = in_z - in_z_hi
        offset = (host & 63) - block
        cols = slice(128 * p, 128 * p + 128)
        for t in range(16):
            here = offset == 4 * t
            z_hi[16 * t : 16 * t + 16, cols] = jnp.where(here, in_z_hi, 0.0).astype(BF16)
            z_lo[16 * t : 16 * t + 16, cols] = jnp.where(here, in_z_lo, 0.0).astype(BF16)
        kept.append((field, code, [basis[i][0:1] for i in range(4)], in_y))
    wide = jnp.dot(vel_hi[...], z_hi[...], preferred_element_type=F32)
    wide += jnp.dot(vel_lo[...], z_hi[...], preferred_element_type=F32)
    wide += jnp.dot(vel_hi[...], z_lo[...], preferred_element_type=F32)
    for p in range(14):
        field, code, in_x, in_y = kept[p]
        cols = slice(128 * p, 128 * p + 128)
        live = code > 0.5
        in_xy = [in_x[i] * in_y for i in range(4)]
        seen = []
        for d in range(3):
            mixed = None
            for i in range(4):
                start = 16 * (4 * d + i)
                term = in_xy[i] * wide[start : start + 16, cols]
                mixed = term if mixed is None else mixed + term
            seen.append(jnp.sum(mixed, axis=0, keepdims=True))
        fluid = jnp.where(sub8 == 0, seen[0], jnp.where(sub8 == 1, seen[1], seen[2]))
        speed = pltpu.roll(field, 5, 0)
        keep = live & (sub8 < 3)
        relax = jnp.where(live[0:1], field[6:7], 1.0)
        force = jnp.where(keep, (fluid - speed) / relax, 0.0)
        base = jnp.where(keep, speed, 0.0)
        base_ref[p] = base
        acc_ref[p] = force
        mass = field[7:8]
        push = -mass * force
        work = -mass * jnp.sum(force * base, axis=0, keepdims=True)
        sources = [push[0:1], push[1:2], push[2:3], work]
        for i in range(4):
            scaled = in_xy[i] * weight_xy[i]
            for d in range(4):
                hi, lo = split(sources[d] * scaled)
                start = 16 * (4 * d + i)
                a_hi[start : start + 16, cols] = hi
                a_lo[start : start + 16, cols] = lo
    lanes = (((1,), (1,)), ((), ()))
    total = lax.dot_general(a_hi[...], z_hi[...], lanes, preferred_element_type=F32)
    total += lax.dot_general(a_lo[...], z_hi[...], lanes, preferred_element_type=F32)
    total += lax.dot_general(a_hi[...], z_lo[...], lanes, preferred_element_type=F32)
    zpos = lax.broadcasted_iota(jnp.int32, (16, 256), 1) & 3
    weight_z = by_pos(zpos, 1.0 / WEIGHTS)
    for d in range(4):
        for i in range(4):
            start = 16 * (4 * d + i)
            dep_ref[d, i] = total[start : start + 16, :] * weight_z


def finish_kernel(u_ref, rate_ref, dep_ref, top_ref, base_ref, acc_ref, next_ref, vel_ref):
    top = jnp.max(jnp.max(top_ref[...], axis=0, keepdims=True), axis=1, keepdims=True)
    step = 1.0 / (7.0 * jnp.broadcast_to(top, (8, 256)))
    step16 = jnp.concatenate([step, step], axis=0)
    for v in range(5):
        for i in range(4):
            rate = rate_ref[v, i]
            if v > 0:
                rate = rate + dep_ref[v - 1, i]
            next_ref[v, i] = u_ref[v, i] + step16 * rate
    small = step[:, :128]
    for pair in range(14):
        value = base_ref[pair] + small * acc_ref[pair]
        for h in range(2):
            g = 2 * pair + h
            if g < 27:
                vel_ref[g // 9, g // 3 % 3, g % 3] = value[0:3, 64 * h : 64 * h + 64]


def exchanged(up, down, axis, wrap):
    count = lax.axis_size(axis)
    pairs = [(i, (i + 1) % count) for i in range(count if wrap else count - 1)]
    return (
        lax.ppermute(up, axis, pairs),
        lax.ppermute(down, axis, [(j, i) for i, j in pairs]),
    )


def all_tops(top, axis):
    return lax.all_to_all(top, axis, 0, 0, tiled=True)


def call(kernel, outs, scratch=()):
    return pl.pallas_call(
        kernel,
        out_shape=outs,
        scratch_shapes=list(scratch),
        compiler_params=pltpu.CompilerParams(vmem_limit_bytes=VMEM_BYTES),
    )


def tiles_of(n):
    return jax.ShapeDtypeStruct((n, 8, 128), F32)


def local(fluid_state, parcel_data, host_element, slot_counts):
    planes = lax.axis_size("gx") * lax.axis_size("gy")
    row = jax.ShapeDtypeStruct((planes, 128), F32)
    face_up, face_down, faces, top = call(face_kernel, (tiles_of(20), tiles_of(20), tiles_of(14), row))(fluid_state)
    x_up, x_down, keep_x = call(pack_kernel, (tiles_of(29), tiles_of(29), tiles_of(9)))(
        parcel_data, host_element, slot_counts, face_up, face_down
    )
    x1, x2 = exchanged(x_up, x_down, "gx", False)
    tops = all_tops(top, ("gx", "gy"))
    row = jax.ShapeDtypeStruct((lax.axis_size("gz"), 128), F32)
    y_up, y_down, keep_y, top = call(turn_y_kernel, (tiles_of(14), tiles_of(14), tiles_of(9), row))(
        x1, x2, keep_x, faces, tops
    )
    y1, y2 = exchanged(y_up, y_down, "gy", False)
    z_up, z_down, keep_z = call(turn_z_kernel, (tiles_of(11), tiles_of(11), tiles_of(9)))(y1, y2, keep_y, faces)
    z1, z2 = exchanged(z_up, z_down, "gz", True)
    top = all_tops(top, "gz")
    field = jax.ShapeDtypeStruct((5, 4, 16, 256), F32)
    rate = call(
        rate_kernel, field, [pltpu.VMEM((5, 4, 16, 256), F32), pltpu.VMEM((2, 16, 256), F32)],
    )(fluid_state, x1, x2, y1, y2, z1, z2, faces)
    deposit, base, acc = call(
        parcel_kernel,
        (jax.ShapeDtypeStruct((4, 4, 16, 256), F32), tiles_of(14), tiles_of(14)),
        [
            pltpu.VMEM((192, 256), BF16),
            pltpu.VMEM((192, 256), BF16),
            pltpu.VMEM((256, 1792), BF16),
            pltpu.VMEM((256, 1792), BF16),
            pltpu.VMEM((256, 1792), BF16),
            pltpu.VMEM((256, 1792), BF16),
        ],
    )(fluid_state, z1, z2, keep_z)
    return call(finish_kernel, (field, jax.ShapeDtypeStruct((3, 3, 3, 3, 64), F32)))(
        fluid_state, rate, deposit, top, base, acc
    )


def solution(mesh):
    placed = (
        P(None, "gx", "gy", "gz"),
        P("gx", "gy", "gz", None, None),
        P("gx", "gy", "gz", None),
        P("gx", "gy", "gz"),
    )
    return jax.shard_map(
        local,
        mesh=mesh,
        in_specs=placed,
        out_specs=(P(None, "gx", "gy", "gz"), P("gx", "gy", "gz", None, None)),
        check_vma=False,
    )
```

```python
import jax
import jax.numpy as jnp
import numpy as np
from jax import lax
from jax.experimental import pallas as pl
from jax.experimental.pallas import tpu as pltpu
from jax.sharding import PartitionSpec as P

F32 = jnp.float32
BF16 = jnp.bfloat16
VMEM_BYTES = 24 * 1024 * 1024

NODES = np.array([-1.0, -1.0 / np.sqrt(5.0), 1.0 / np.sqrt(5.0), 1.0])
WEIGHTS = np.array([1.0 / 6.0, 5.0 / 6.0, 5.0 / 6.0, 1.0 / 6.0])


def derivative_table():
    factor = [np.prod([NODES[i] - NODES[j] for j in range(4) if j != i]) for i in range(4)]
    table = np.zeros((4, 4))
    for i in range(4):
        for j in range(4):
            if i != j:
                table[i, j] = factor[i] / (factor[j] * (NODES[i] - NODES[j]))
    return table


DERIV = derivative_table()
SCALE = [1.0 / np.prod([NODES[i] - NODES[j] for j in range(4) if j != i]) for i in range(4)]

FACE = 9


def by_pos(pos, values):
    out = jnp.full(pos.shape, float(values[3]), F32)
    for k in range(3):
        out = jnp.where(pos == k, float(values[k]), out)
    return out


def primitives(state):
    inverse = 1.0 / state[0]
    vel = [state[d + 1] * inverse for d in range(3)]
    square = vel[0] * vel[0] + vel[1] * vel[1] + vel[2] * vel[2]
    pressure = 0.4 * (state[4] - 0.5 * state[0] * square)
    sound = jnp.sqrt(1.4 * pressure * inverse)
    return vel, pressure, sound, square


def flux(state, vel, pressure, d):
    normal = vel[d]
    out = [state[d + 1]]
    for k in range(3):
        term = state[k + 1] * normal
        out.append(term + pressure if k == d else term)
    out.append((state[4] + pressure) * normal)
    return out


def side(state, d):
    vel, pressure, sound, _ = primitives(state)
    return flux(state, vel, pressure, d), jnp.abs(vel[d]) + sound


def tile_of(ref):
    return lambda tile: ref[tile]


def face_kernel(u_ref, up_ref, down_ref, face_ref, top_ref):
    top = None
    for i in range(4):
        _, _, sound, square = primitives([u_ref[v, i] for v in range(5)])
        speed = jnp.sqrt(square) + sound
        top = speed if top is None else jnp.maximum(top, speed)
    top = jnp.maximum(top[:, :128], top[:, 128:])
    top_ref[...] = jnp.broadcast_to(jnp.max(top, axis=0, keepdims=True), top_ref.shape)
    for v in range(5):
        for yh in range(2):
            for zh in range(2):
                tile = 4 * v + 2 * yh + zh
                ys, zs = slice(8 * yh, 8 * yh + 8), slice(128 * zh, 128 * zh + 128)
                up_ref[tile] = u_ref[v, 3, ys, zs]
                down_ref[tile] = u_ref[v, 0, ys, zs]
        for i in range(4):
            for zh in range(2):
                zs = slice(128 * zh, 128 * zh + 128)
                row = 4 * zh + i
                face_ref[v, row : row + 1, :] = u_ref[v, i, 15:16, zs]
                face_ref[5 + v, row : row + 1, :] = u_ref[v, i, 0:1, zs]
    lane = lax.broadcasted_iota(jnp.int32, (16, 128), 1)
    high = jnp.zeros((16, 128), F32)
    low = jnp.zeros((16, 128), F32)
    for v in range(5):
        for i in range(4):
            here = lane == 4 * v + i
            high = jnp.where(here, u_ref[v, i, :, 255:256], high)
            low = jnp.where(here, u_ref[v, i, :, 0:1], low)
    for yh in range(2):
        face_ref[10 + yh] = high[8 * yh : 8 * yh + 8]
        face_ref[12 + yh] = low[8 * yh : 8 * yh + 8]


def pack_kernel(data_ref, host_ref, count_ref, face_up_ref, face_down_ref, up_ref, down_ref, keep_ref):
    slot = lax.broadcasted_iota(jnp.int32, (1, 64), 1)
    for a, out in ((2, up_ref), (0, down_ref), (1, keep_ref)):
        for b in range(3):
            for c in range(3):
                count = count_ref[a, b : b + 1, c : c + 1]
                host = host_ref[a, b, c : c + 1, :]
                code = jnp.where(slot < count, host + 1, 0).astype(F32)
                out[3 * b + c, :, 0:64] = data_ref[a, b, c]
                out[3 * b + c, :, 64:128] = jnp.broadcast_to(code, (8, 64))
    for t in range(20):
        up_ref[FACE + t] = face_up_ref[t]
        down_ref[FACE + t] = face_down_ref[t]


def turn_y_kernel(low_ref, high_ref, own_ref, face_ref, tops_ref, up_ref, down_ref, keep_ref, top_ref):
    top_ref[...] = jnp.broadcast_to(jnp.max(tops_ref[...], axis=0, keepdims=True), top_ref.shape)
    for a, source in enumerate((low_ref, own_ref, high_ref)):
        for c in range(3):
            up_ref[3 * a + c] = source[6 + c]
            down_ref[3 * a + c] = source[c]
            keep_ref[3 * a + c] = source[3 + c]
    for v in range(5):
        up_ref[FACE + v] = face_ref[v]
        down_ref[FACE + v] = face_ref[5 + v]


def turn_z_kernel(low_ref, high_ref, own_ref, face_ref, tops_ref, up_ref, down_ref, keep_ref, top_ref):
    top_ref[...] = jnp.broadcast_to(jnp.max(tops_ref[...], axis=0, keepdims=True), top_ref.shape)
    for b, source in enumerate((low_ref, own_ref, high_ref)):
        for a in range(3):
            up_ref[3 * a + b] = source[3 * a + 2]
            down_ref[3 * a + b] = source[3 * a]
            keep_ref[3 * a + b] = source[3 * a + 1]
    for yh in range(2):
        up_ref[FACE + yh] = face_ref[10 + yh]
        down_ref[FACE + yh] = face_ref[12 + yh]


def wall(axis, last, own, received, sign_of):
    at = lax.axis_index(axis) == (lax.axis_size(axis) - 1 if last else 0)
    pick = jnp.full(received[0].shape, at.astype(jnp.int32), jnp.int32) == 1
    return [jnp.where(pick, sign_of(v) * own[v], received[v]) for v in range(5)]


def shift_rate(state, fluxes, speed, low, high, axis, pos, first, last, coef):
    count = state[0].shape[axis]
    low_state, low_flux, low_speed = low
    high_state, high_flux, high_speed = high
    at_low = pos == 0
    ends = at_low | (pos == 3)

    def beside(here, below, above):
        near = jnp.where(at_low, pltpu.roll(here, 1, axis), pltpu.roll(here, count - 1, axis))
        return jnp.where(first, below, jnp.where(last, above, near))

    spread = jnp.maximum(speed, beside(speed, low_speed, high_speed))
    spread = jnp.where(ends, 3.0 * spread, 0.0)
    out = []
    for v in range(5):
        value = fluxes[v]
        above = jnp.where(last, high_flux[v], pltpu.roll(value, count - 1, axis))
        below = jnp.where(first, low_flux[v], pltpu.roll(value, 1, axis))
        total = coef[1] * above + coef[-1] * below
        for d in (-3, -2, 2, 3):
            total = total + coef[d] * pltpu.roll(value, -d % count, axis)
        out.append(spread * (beside(state[v], low_state[v], high_state[v]) - state[v]) - total)
    return out


def rate_kernel(u_ref, x1_ref, x2_ref, y1_ref, y2_ref, z1_ref, z2_ref, face_ref, rate_ref, fx_ref, sx_ref):
    x_side = tile_of(x1_ref), tile_of(x2_ref)
    y_side = tile_of(y1_ref), tile_of(y2_ref)
    z_side = tile_of(z1_ref), tile_of(z2_ref)
    shape = (16, 256)
    row = lax.broadcasted_iota(jnp.int32, shape, 0)
    lane = lax.broadcasted_iota(jnp.int32, shape, 1)
    ypos, zpos = row & 3, lane & 3

    def coefs(pos):
        out = {}
        for d in (-3, -2, -1, 1, 2, 3):
            values = [DERIV[k, k + d] if 0 <= k + d < 4 else 0.0 for k in range(4)]
            if d == 1:
                values[3] = 3.0
            if d == -1:
                values[0] = -3.0
            out[d] = by_pos(pos, values)
        return out

    ycoef, zcoef = coefs(ypos), coefs(zpos)
    yfirst, ylast = row == 0, row == 15
    zfirst, zlast = lane == 0, lane == 255

    yflip = lambda v: -1.0 if v == 2 else 1.0
    ylow = wall("gy", False, [face_ref[5 + v] for v in range(5)], [y_side[0](FACE + v) for v in range(5)], yflip)
    yhigh = wall("gy", True, [face_ref[v] for v in range(5)], [y_side[1](FACE + v) for v in range(5)], yflip)
    ylow_flux, ylow_speed = side(ylow, 1)
    yhigh_flux, yhigh_speed = side(yhigh, 1)

    def columns(first_tile, source):
        both = jnp.concatenate([source(first_tile), source(first_tile + 1)], axis=0)
        return [both if v == 0 else pltpu.roll(both, 128 - 4 * v, 1) for v in range(5)]

    own = tile_of(face_ref)
    zflip = lambda v: -1.0 if v == 3 else 1.0
    zlow = wall("gz", False, columns(12, own), columns(FACE, z_side[0]), zflip)
    zhigh = wall("gz", True, columns(10, own), columns(FACE, z_side[1]), zflip)
    zlow_flux, zlow_speed = side(zlow, 2)
    zhigh_flux, zhigh_speed = side(zhigh, 2)

    def pick_row(tile, i):
        return jnp.concatenate([tile[i : i + 1], tile[4 + i : 5 + i]], axis=1)

    for i in range(4):
        state = [u_ref[v, i] for v in range(5)]
        vel, pressure, sound, _ = primitives(state)
        xflux = flux(state, vel, pressure, 0)
        for v in range(5):
            fx_ref[v, i] = xflux[v]
        if i in (0, 3):
            sx_ref[i // 3] = jnp.abs(vel[0]) + sound
        low = ([pick_row(t, i) for t in ylow], [pick_row(t, i) for t in ylow_flux], pick_row(ylow_speed, i))
        high = ([pick_row(t, i) for t in yhigh], [pick_row(t, i) for t in yhigh_flux], pick_row(yhigh_speed, i))
        yrate = shift_rate(
            state, flux(state, vel, pressure, 1), jnp.abs(vel[1]) + sound,
            low, high, 0, ypos, yfirst, ylast, ycoef,
        )
        pick = lambda t: t[:, i : i + 1]
        low = ([pick(t) for t in zlow], [pick(t) for t in zlow_flux], pick(zlow_speed))
        high = ([pick(t) for t in zhigh], [pick(t) for t in zhigh_flux], pick(zhigh_speed))
        zrate = shift_rate(
            state, flux(state, vel, pressure, 2), jnp.abs(vel[2]) + sound,
            low, high, 1, zpos, zfirst, zlast, zcoef,
        )
        for v in range(5):
            rate_ref[v, i] = yrate[v] + zrate[v]

    xflip = lambda v: -1.0 if v == 1 else 1.0
    for half in range(2):
        for part in range(2):
            ys, zs = slice(8 * half, 8 * half + 8), slice(128 * part, 128 * part + 128)
            tile = FACE + 2 * half + part
            ends = []
            for last, i, source in ((False, 0, x_side[0]), (True, 3, x_side[1])):
                mine = [u_ref[v, i, ys, zs] for v in range(5)]
                beyond = wall("gx", last, mine, [source(tile + 4 * v) for v in range(5)], xflip)
                far_flux, far_speed = side(beyond, 0)
                spread = 3.0 * jnp.maximum(sx_ref[i // 3, ys, zs], far_speed)
                sign = -3.0 if last else 3.0
                ends.append([sign * far_flux[v] + spread * (beyond[v] - mine[v]) for v in range(5)])
            for v in range(5):
                f = [fx_ref[v, i, ys, zs] for i in range(4)]
                for j in range(4):
                    total = rate_ref[v, j, ys, zs]
                    for i in range(4):
                        if i != j:
                            total = total - float(DERIV[j, i]) * f[i]
                    if j == 0:
                        total = total + ends[0][v]
                    if j == 3:
                        total = total + ends[1][v]
                    rate_ref[v, j, ys, zs] = total


def split(value):
    high = value.astype(BF16)
    return high, (value - high.astype(F32)).astype(BF16)


def parcel_kernel(u_ref, z1_ref, z2_ref, own_ref, dep_ref, base_ref, acc_ref, vel_hi, vel_lo, z_hi, z_lo, a_hi, a_lo):
    sides = (z1_ref, own_ref, z2_ref)
    tiles = [sides[g % 3][g // 3] for g in range(27)] + [jnp.zeros((8, 128), F32)]
    for i in range(4):
        inverse = 1.0 / u_ref[0, i]
        for d in range(3):
            hi, lo = split(u_ref[d + 1, i] * inverse)
            start = 16 * (4 * d + i)
            vel_hi[start : start + 16, :] = hi
            vel_lo[start : start + 16, :] = lo
    left = lax.broadcasted_iota(jnp.int32, (8, 128), 1) < 64
    sub8 = lax.broadcasted_iota(jnp.int32, (8, 128), 0)
    sub16 = lax.broadcasted_iota(jnp.int32, (16, 128), 0)
    pos, block = sub16 & 3, sub16 >> 2
    weight_y = by_pos(pos, 1.0 / WEIGHTS)
    weight_xy = [weight_y * float(1.0 / WEIGHTS[i]) for i in range(4)]
    inner = float(NODES[2])
    kept = []
    for p in range(14):
        first, second = tiles[2 * p], tiles[2 * p + 1]
        field = jnp.where(left, first, pltpu.roll(second, 64, 1))
        code = jnp.where(left, pltpu.roll(first, 64, 1), second)
        host = code.astype(jnp.int32) - 1
        host = jnp.concatenate([host, host], axis=0)
        outer = (field + 1.0) * (field - 1.0)
        middle = (field + inner) * (field - inner)
        basis = [
            float(SCALE[0]) * middle * (field - 1.0),
            float(SCALE[1]) * outer * (field - inner),
            float(SCALE[2]) * outer * (field + inner),
            float(SCALE[3]) * middle * (field + 1.0),
        ]

        def spread(r):
            rows = [jnp.broadcast_to(basis[k][r : r + 1], (16, 128)) for k in range(4)]
            return jnp.where(pos == 0, rows[0], jnp.where(pos == 1, rows[1], jnp.where(pos == 2, rows[2], rows[3])))

        in_y = jnp.where((host >> 6) == block, spread(1), 0.0)
        in_z = spread(2)
        in_z_hi = in_z.astype(BF16).astype(F32)
        in_z_lo = in_z - in_z_hi
        offset = (host & 63) - block
        cols = slice(128 * p, 128 * p + 128)
        for t in range(16):
            here = offset == 4 * t
            z_hi[16 * t : 16 * t + 16, cols] = jnp.where(here, in_z_hi, 0.0).astype(BF16)
            z_lo[16 * t : 16 * t + 16, cols] = jnp.where(here, in_z_lo, 0.0).astype(BF16)
        kept.append((field, code, [basis[i][0:1] for i in range(4)], in_y))
    wide = jnp.dot(vel_hi[...], z_hi[...], preferred_element_type=F32)
    wide += jnp.dot(vel_lo[...], z_hi[...], preferred_element_type=F32)
    wide += jnp.dot(vel_hi[...], z_lo[...], preferred_element_type=F32)
    for p in range(14):
        field, code, in_x, in_y = kept[p]
        cols = slice(128 * p, 128 * p + 128)
        live = code > 0.5
        in_xy = [in_x[i] * in_y for i in range(4)]
        seen = []
        for d in range(3):
            mixed = None
            for i in range(4):
                start = 16 * (4 * d + i)
                term = in_xy[i] * wide[start : start + 16, cols]
                mixed = term if mixed is None else mixed + term
            seen.append(jnp.sum(mixed, axis=0, keepdims=True))
        fluid = jnp.where(sub8 == 0, seen[0], jnp.where(sub8 == 1, seen[1], seen[2]))
        speed = pltpu.roll(field, 5, 0)
        keep = live & (sub8 < 3)
        relax = jnp.where(live[0:1], field[6:7], 1.0)
        force = jnp.where(keep, (fluid - speed) / relax, 0.0)
        base = jnp.where(keep, speed, 0.0)
        base_ref[p] = base
        acc_ref[p] = force
        mass = field[7:8]
        push = -mass * force
        work = -mass * jnp.sum(force * base, axis=0, keepdims=True)
        sources = [push[0:1], push[1:2], push[2:3], work]
        for i in range(4):
            scaled = in_xy[i] * weight_xy[i]
            for d in range(4):
                hi, lo = split(sources[d] * scaled)
                start = 16 * (4 * d + i)
                a_hi[start : start + 16, cols] = hi
                a_lo[start : start + 16, cols] = lo
    lanes = (((1,), (1,)), ((), ()))
    total = lax.dot_general(a_hi[...], z_hi[...], lanes, preferred_element_type=F32)
    total += lax.dot_general(a_lo[...], z_hi[...], lanes, preferred_element_type=F32)
    total += lax.dot_general(a_hi[...], z_lo[...], lanes, preferred_element_type=F32)
    zpos = lax.broadcasted_iota(jnp.int32, (16, 256), 1) & 3
    weight_z = by_pos(zpos, 1.0 / WEIGHTS)
    for d in range(4):
        for i in range(4):
            start = 16 * (4 * d + i)
            dep_ref[d, i] = total[start : start + 16, :] * weight_z


def finish_kernel(u_ref, rate_ref, dep_ref, top_ref, base_ref, acc_ref, next_ref, vel_ref):
    top = jnp.max(jnp.max(top_ref[...], axis=0, keepdims=True), axis=1, keepdims=True)
    step = 1.0 / (7.0 * jnp.broadcast_to(top, (8, 256)))
    step16 = jnp.concatenate([step, step], axis=0)
    for v in range(5):
        for i in range(4):
            rate = rate_ref[v, i]
            if v > 0:
                rate = rate + dep_ref[v - 1, i]
            next_ref[v, i] = u_ref[v, i] + step16 * rate
    small = step[:, :128]
    for pair in range(14):
        value = base_ref[pair] + small * acc_ref[pair]
        for h in range(2):
            g = 2 * pair + h
            if g < 27:
                vel_ref[g // 9, g // 3 % 3, g % 3] = value[0:3, 64 * h : 64 * h + 64]


def exchanged(up, down, axis, wrap):
    count = lax.axis_size(axis)
    pairs = [(i, (i + 1) % count) for i in range(count if wrap else count - 1)]
    return (
        lax.ppermute(up, axis, pairs),
        lax.ppermute(down, axis, [(j, i) for i, j in pairs]),
    )


def all_tops(top, axis):
    return lax.all_to_all(top, axis, 0, 0, tiled=True)


def call(kernel, outs, scratch=()):
    return pl.pallas_call(
        kernel,
        out_shape=outs,
        scratch_shapes=list(scratch),
        compiler_params=pltpu.CompilerParams(vmem_limit_bytes=VMEM_BYTES),
    )


def tiles_of(n):
    return jax.ShapeDtypeStruct((n, 8, 128), F32)


def local(fluid_state, parcel_data, host_element, slot_counts):
    rows = [jax.ShapeDtypeStruct((lax.axis_size(axis), 128), F32) for axis in ("gx", "gy", "gz")]
    face_up, face_down, faces, top = call(face_kernel, (tiles_of(20), tiles_of(20), tiles_of(14), rows[0]))(fluid_state)
    x_up, x_down, keep_x = call(pack_kernel, (tiles_of(29), tiles_of(29), tiles_of(9)))(
        parcel_data, host_element, slot_counts, face_up, face_down
    )
    x1, x2 = exchanged(x_up, x_down, "gx", False)
    tops = all_tops(top, "gx")
    y_up, y_down, keep_y, top = call(turn_y_kernel, (tiles_of(14), tiles_of(14), tiles_of(9), rows[1]))(
        x1, x2, keep_x, faces, tops
    )
    y1, y2 = exchanged(y_up, y_down, "gy", False)
    tops = all_tops(top, "gy")
    z_up, z_down, keep_z, top = call(turn_z_kernel, (tiles_of(11), tiles_of(11), tiles_of(9), rows[2]))(
        y1, y2, keep_y, faces, tops
    )
    z1, z2 = exchanged(z_up, z_down, "gz", True)
    top = all_tops(top, "gz")
    field = jax.ShapeDtypeStruct((5, 4, 16, 256), F32)
    rate = call(
        rate_kernel, field, [pltpu.VMEM((5, 4, 16, 256), F32), pltpu.VMEM((2, 16, 256), F32)],
    )(fluid_state, x1, x2, y1, y2, z1, z2, faces)
    deposit, base, acc = call(
        parcel_kernel,
        (jax.ShapeDtypeStruct((4, 4, 16, 256), F32), tiles_of(14), tiles_of(14)),
        [
            pltpu.VMEM((192, 256), BF16),
            pltpu.VMEM((192, 256), BF16),
            pltpu.VMEM((256, 1792), BF16),
            pltpu.VMEM((256, 1792), BF16),
            pltpu.VMEM((256, 1792), BF16),
            pltpu.VMEM((256, 1792), BF16),
        ],
    )(fluid_state, z1, z2, keep_z)
    return call(finish_kernel, (field, jax.ShapeDtypeStruct((3, 3, 3, 3, 64), F32)))(
        fluid_state, rate, deposit, top, base, acc
    )


def solution(mesh):
    placed = (
        P(None, "gx", "gy", "gz"),
        P("gx", "gy", "gz", None, None),
        P("gx", "gy", "gz", None),
        P("gx", "gy", "gz"),
    )
    return jax.shard_map(
        local,
        mesh=mesh,
        in_specs=placed,
        out_specs=(P(None, "gx", "gy", "gz"), P("gx", "gy", "gz", None, None)),
        check_vma=False,
    )
```

```python
import jax
import jax.numpy as jnp
import numpy as np
from jax import lax
from jax.experimental import pallas as pl
from jax.experimental.pallas import tpu as pltpu
from jax.sharding import PartitionSpec as P

F32 = jnp.float32
BF16 = jnp.bfloat16
VMEM_BYTES = 24 * 1024 * 1024

NODES = np.array([-1.0, -1.0 / np.sqrt(5.0), 1.0 / np.sqrt(5.0), 1.0])
WEIGHTS = np.array([1.0 / 6.0, 5.0 / 6.0, 5.0 / 6.0, 1.0 / 6.0])


def derivative_table():
    factor = [np.prod([NODES[i] - NODES[j] for j in range(4) if j != i]) for i in range(4)]
    table = np.zeros((4, 4))
    for i in range(4):
        for j in range(4):
            if i != j:
                table[i, j] = factor[i] / (factor[j] * (NODES[i] - NODES[j]))
    return table


DERIV = derivative_table()
SCALE = [1.0 / np.prod([NODES[i] - NODES[j] for j in range(4) if j != i]) for i in range(4)]

FACE = 9


def by_pos(pos, values):
    out = jnp.full(pos.shape, float(values[3]), F32)
    for k in range(3):
        out = jnp.where(pos == k, float(values[k]), out)
    return out


def primitives(state):
    inverse = 1.0 / state[0]
    vel = [state[d + 1] * inverse for d in range(3)]
    square = vel[0] * vel[0] + vel[1] * vel[1] + vel[2] * vel[2]
    pressure = 0.4 * (state[4] - 0.5 * state[0] * square)
    sound = jnp.sqrt(1.4 * pressure * inverse)
    return vel, pressure, sound, square


def flux(state, vel, pressure, d):
    normal = vel[d]
    out = [state[d + 1]]
    for k in range(3):
        term = state[k + 1] * normal
        out.append(term + pressure if k == d else term)
    out.append((state[4] + pressure) * normal)
    return out


def side(state, d):
    vel, pressure, sound, _ = primitives(state)
    return flux(state, vel, pressure, d), jnp.abs(vel[d]) + sound


def tile_of(ref):
    return lambda tile: ref[tile]


def face_kernel(u_ref, up_ref, down_ref, face_ref, top_ref):
    top = None
    for i in range(4):
        _, _, sound, square = primitives([u_ref[v, i] for v in range(5)])
        speed = jnp.sqrt(square) + sound
        top = speed if top is None else jnp.maximum(top, speed)
    top = jnp.maximum(top[:, :128], top[:, 128:])
    top_ref[...] = jnp.broadcast_to(jnp.max(top, axis=0, keepdims=True), top_ref.shape)
    for v in range(5):
        for yh in range(2):
            for zh in range(2):
                tile = 4 * v + 2 * yh + zh
                ys, zs = slice(8 * yh, 8 * yh + 8), slice(128 * zh, 128 * zh + 128)
                up_ref[tile] = u_ref[v, 3, ys, zs]
                down_ref[tile] = u_ref[v, 0, ys, zs]
        for i in range(4):
            for zh in range(2):
                zs = slice(128 * zh, 128 * zh + 128)
                row = 4 * zh + i
                face_ref[v, row : row + 1, :] = u_ref[v, i, 15:16, zs]
                face_ref[5 + v, row : row + 1, :] = u_ref[v, i, 0:1, zs]
    lane = lax.broadcasted_iota(jnp.int32, (16, 128), 1)
    high = jnp.zeros((16, 128), F32)
    low = jnp.zeros((16, 128), F32)
    for v in range(5):
        for i in range(4):
            here = lane == 4 * v + i
            high = jnp.where(here, u_ref[v, i, :, 255:256], high)
            low = jnp.where(here, u_ref[v, i, :, 0:1], low)
    for yh in range(2):
        face_ref[10 + yh] = high[8 * yh : 8 * yh + 8]
        face_ref[12 + yh] = low[8 * yh : 8 * yh + 8]


def pack_kernel(data_ref, host_ref, count_ref, face_up_ref, face_down_ref, up_ref, down_ref, keep_ref):
    slot = lax.broadcasted_iota(jnp.int32, (1, 64), 1)
    for a, out in ((2, up_ref), (0, down_ref), (1, keep_ref)):
        for b in range(3):
            for c in range(3):
                count = count_ref[a, b : b + 1, c : c + 1]
                host = host_ref[a, b, c : c + 1, :]
                code = jnp.where(slot < count, host + 1, 0).astype(F32)
                out[3 * b + c, :, 0:64] = data_ref[a, b, c]
                out[3 * b + c, :, 64:128] = jnp.broadcast_to(code, (8, 64))
    for t in range(20):
        up_ref[FACE + t] = face_up_ref[t]
        down_ref[FACE + t] = face_down_ref[t]


def turn_y_kernel(low_ref, high_ref, own_ref, face_ref, tops_ref, up_ref, down_ref, keep_ref, top_ref):
    top_ref[...] = jnp.broadcast_to(jnp.max(tops_ref[...], axis=0, keepdims=True), top_ref.shape)
    for a, source in enumerate((low_ref, own_ref, high_ref)):
        for c in range(3):
            up_ref[3 * a + c] = source[6 + c]
            down_ref[3 * a + c] = source[c]
            keep_ref[3 * a + c] = source[3 + c]
    for v in range(5):
        up_ref[FACE + v] = face_ref[v]
        down_ref[FACE + v] = face_ref[5 + v]


def turn_z_kernel(low_ref, high_ref, own_ref, face_ref, up_ref, down_ref, keep_ref):
    for b, source in enumerate((low_ref, own_ref, high_ref)):
        for a in range(3):
            up_ref[3 * a + b] = source[3 * a + 2]
            down_ref[3 * a + b] = source[3 * a]
            keep_ref[3 * a + b] = source[3 * a + 1]
    for yh in range(2):
        up_ref[FACE + yh] = face_ref[10 + yh]
        down_ref[FACE + yh] = face_ref[12 + yh]


def wall(axis, last, own, received, sign_of):
    at = lax.axis_index(axis) == (lax.axis_size(axis) - 1 if last else 0)
    pick = jnp.full(received[0].shape, at.astype(jnp.int32), jnp.int32) == 1
    return [jnp.where(pick, sign_of(v) * own[v], received[v]) for v in range(5)]


def shift_rate(state, fluxes, speed, low, high, axis, pos, first, last, coef):
    count = state[0].shape[axis]
    low_state, low_flux, low_speed = low
    high_state, high_flux, high_speed = high
    at_low = pos == 0
    ends = at_low | (pos == 3)

    def beside(here, below, above):
        near = jnp.where(at_low, pltpu.roll(here, 1, axis), pltpu.roll(here, count - 1, axis))
        return jnp.where(first, below, jnp.where(last, above, near))

    spread = jnp.maximum(speed, beside(speed, low_speed, high_speed))
    spread = jnp.where(ends, 3.0 * spread, 0.0)
    out = []
    for v in range(5):
        value = fluxes[v]
        above = jnp.where(last, high_flux[v], pltpu.roll(value, count - 1, axis))
        below = jnp.where(first, low_flux[v], pltpu.roll(value, 1, axis))
        total = coef[1] * above + coef[-1] * below
        for d in (-3, -2, 2, 3):
            total = total + coef[d] * pltpu.roll(value, -d % count, axis)
        out.append(spread * (beside(state[v], low_state[v], high_state[v]) - state[v]) - total)
    return out


def rate_kernel(u_ref, x1_ref, x2_ref, y1_ref, y2_ref, z1_ref, z2_ref, face_ref, rate_ref, fx_ref, sx_ref):
    x_side = tile_of(x1_ref), tile_of(x2_ref)
    y_side = tile_of(y1_ref), tile_of(y2_ref)
    z_side = tile_of(z1_ref), tile_of(z2_ref)
    shape = (16, 256)
    row = lax.broadcasted_iota(jnp.int32, shape, 0)
    lane = lax.broadcasted_iota(jnp.int32, shape, 1)
    ypos, zpos = row & 3, lane & 3

    def coefs(pos):
        out = {}
        for d in (-3, -2, -1, 1, 2, 3):
            values = [DERIV[k, k + d] if 0 <= k + d < 4 else 0.0 for k in range(4)]
            if d == 1:
                values[3] = 3.0
            if d == -1:
                values[0] = -3.0
            out[d] = by_pos(pos, values)
        return out

    ycoef, zcoef = coefs(ypos), coefs(zpos)
    yfirst, ylast = row == 0, row == 15
    zfirst, zlast = lane == 0, lane == 255

    yflip = lambda v: -1.0 if v == 2 else 1.0
    ylow = wall("gy", False, [face_ref[5 + v] for v in range(5)], [y_side[0](FACE + v) for v in range(5)], yflip)
    yhigh = wall("gy", True, [face_ref[v] for v in range(5)], [y_side[1](FACE + v) for v in range(5)], yflip)
    ylow_flux, ylow_speed = side(ylow, 1)
    yhigh_flux, yhigh_speed = side(yhigh, 1)

    def columns(first_tile, source):
        both = jnp.concatenate([source(first_tile), source(first_tile + 1)], axis=0)
        return [both if v == 0 else pltpu.roll(both, 128 - 4 * v, 1) for v in range(5)]

    own = tile_of(face_ref)
    zflip = lambda v: -1.0 if v == 3 else 1.0
    zlow = wall("gz", False, columns(12, own), columns(FACE, z_side[0]), zflip)
    zhigh = wall("gz", True, columns(10, own), columns(FACE, z_side[1]), zflip)
    zlow_flux, zlow_speed = side(zlow, 2)
    zhigh_flux, zhigh_speed = side(zhigh, 2)

    def pick_row(tile, i):
        return jnp.concatenate([tile[i : i + 1], tile[4 + i : 5 + i]], axis=1)

    for i in range(4):
        state = [u_ref[v, i] for v in range(5)]
        vel, pressure, sound, _ = primitives(state)
        xflux = flux(state, vel, pressure, 0)
        for v in range(5):
            fx_ref[v, i] = xflux[v]
        if i in (0, 3):
            sx_ref[i // 3] = jnp.abs(vel[0]) + sound
        low = ([pick_row(t, i) for t in ylow], [pick_row(t, i) for t in ylow_flux], pick_row(ylow_speed, i))
        high = ([pick_row(t, i) for t in yhigh], [pick_row(t, i) for t in yhigh_flux], pick_row(yhigh_speed, i))
        yrate = shift_rate(
            state, flux(state, vel, pressure, 1), jnp.abs(vel[1]) + sound,
            low, high, 0, ypos, yfirst, ylast, ycoef,
        )
        pick = lambda t: t[:, i : i + 1]
        low = ([pick(t) for t in zlow], [pick(t) for t in zlow_flux], pick(zlow_speed))
        high = ([pick(t) for t in zhigh], [pick(t) for t in zhigh_flux], pick(zhigh_speed))
        zrate = shift_rate(
            state, flux(state, vel, pressure, 2), jnp.abs(vel[2]) + sound,
            low, high, 1, zpos, zfirst, zlast, zcoef,
        )
        for v in range(5):
            rate_ref[v, i] = yrate[v] + zrate[v]

    xflip = lambda v: -1.0 if v == 1 else 1.0
    for half in range(2):
        for part in range(2):
            ys, zs = slice(8 * half, 8 * half + 8), slice(128 * part, 128 * part + 128)
            tile = FACE + 2 * half + part
            ends = []
            for last, i, source in ((False, 0, x_side[0]), (True, 3, x_side[1])):
                mine = [u_ref[v, i, ys, zs] for v in range(5)]
                beyond = wall("gx", last, mine, [source(tile + 4 * v) for v in range(5)], xflip)
                far_flux, far_speed = side(beyond, 0)
                spread = 3.0 * jnp.maximum(sx_ref[i // 3, ys, zs], far_speed)
                sign = -3.0 if last else 3.0
                ends.append([sign * far_flux[v] + spread * (beyond[v] - mine[v]) for v in range(5)])
            for v in range(5):
                f = [fx_ref[v, i, ys, zs] for i in range(4)]
                for j in range(4):
                    total = rate_ref[v, j, ys, zs]
                    for i in range(4):
                        if i != j:
                            total = total - float(DERIV[j, i]) * f[i]
                    if j == 0:
                        total = total + ends[0][v]
                    if j == 3:
                        total = total + ends[1][v]
                    rate_ref[v, j, ys, zs] = total


def split(value):
    high = value.astype(BF16)
    return high, (value - high.astype(F32)).astype(BF16)


def parcel_kernel(u_ref, z1_ref, z2_ref, own_ref, dep_ref, base_ref, acc_ref, vel_hi, vel_lo, z_hi, z_lo, a_hi, a_lo):
    sides = (z1_ref, own_ref, z2_ref)
    tiles = [sides[g % 3][g // 3] for g in range(27)] + [jnp.zeros((8, 128), F32)]
    for i in range(4):
        inverse = 1.0 / u_ref[0, i]
        for d in range(3):
            hi, lo = split(u_ref[d + 1, i] * inverse)
            start = 16 * (4 * d + i)
            vel_hi[start : start + 16, :] = hi
            vel_lo[start : start + 16, :] = lo
    left = lax.broadcasted_iota(jnp.int32, (8, 128), 1) < 64
    sub8 = lax.broadcasted_iota(jnp.int32, (8, 128), 0)
    sub16 = lax.broadcasted_iota(jnp.int32, (16, 128), 0)
    pos, block = sub16 & 3, sub16 >> 2
    weight_y = by_pos(pos, 1.0 / WEIGHTS)
    weight_xy = [weight_y * float(1.0 / WEIGHTS[i]) for i in range(4)]
    inner = float(NODES[2])
    kept = []
    for p in range(14):
        first, second = tiles[2 * p], tiles[2 * p + 1]
        field = jnp.where(left, first, pltpu.roll(second, 64, 1))
        code = jnp.where(left, pltpu.roll(first, 64, 1), second)
        host = code.astype(jnp.int32) - 1
        host = jnp.concatenate([host, host], axis=0)
        outer = (field + 1.0) * (field - 1.0)
        middle = (field + inner) * (field - inner)
        basis = [
            float(SCALE[0]) * middle * (field - 1.0),
            float(SCALE[1]) * outer * (field - inner),
            float(SCALE[2]) * outer * (field + inner),
            float(SCALE[3]) * middle * (field + 1.0),
        ]

        def spread(r):
            rows = [jnp.broadcast_to(basis[k][r : r + 1], (16, 128)) for k in range(4)]
            return jnp.where(pos == 0, rows[0], jnp.where(pos == 1, rows[1], jnp.where(pos == 2, rows[2], rows[3])))

        in_y = jnp.where((host >> 6) == block, spread(1), 0.0)
        in_z = spread(2)
        in_z_hi = in_z.astype(BF16).astype(F32)
        in_z_lo = in_z - in_z_hi
        offset = (host & 63) - block
        cols = slice(128 * p, 128 * p + 128)
        for t in range(16):
            here = offset == 4 * t
            z_hi[16 * t : 16 * t + 16, cols] = jnp.where(here, in_z_hi, 0.0).astype(BF16)
            z_lo[16 * t : 16 * t + 16, cols] = jnp.where(here, in_z_lo, 0.0).astype(BF16)
        kept.append((field, code, [basis[i][0:1] for i in range(4)], in_y))
    wide = jnp.dot(vel_hi[...], z_hi[...], preferred_element_type=F32)
    wide += jnp.dot(vel_lo[...], z_hi[...], preferred_element_type=F32)
    wide += jnp.dot(vel_hi[...], z_lo[...], preferred_element_type=F32)
    for p in range(14):
        field, code, in_x, in_y = kept[p]
        cols = slice(128 * p, 128 * p + 128)
        live = code > 0.5
        in_xy = [in_x[i] * in_y for i in range(4)]
        seen = []
        for d in range(3):
            mixed = None
            for i in range(4):
                start = 16 * (4 * d + i)
                term = in_xy[i] * wide[start : start + 16, cols]
                mixed = term if mixed is None else mixed + term
            seen.append(jnp.sum(mixed, axis=0, keepdims=True))
        fluid = jnp.where(sub8 == 0, seen[0], jnp.where(sub8 == 1, seen[1], seen[2]))
        speed = pltpu.roll(field, 5, 0)
        keep = live & (sub8 < 3)
        relax = jnp.where(live[0:1], field[6:7], 1.0)
        force = jnp.where(keep, (fluid - speed) / relax, 0.0)
        base = jnp.where(keep, speed, 0.0)
        base_ref[p] = base
        acc_ref[p] = force
        mass = field[7:8]
        push = -mass * force
        work = -mass * jnp.sum(force * base, axis=0, keepdims=True)
        sources = [push[0:1], push[1:2], push[2:3], work]
        for i in range(4):
            scaled = in_xy[i] * weight_xy[i]
            for d in range(4):
                hi, lo = split(sources[d] * scaled)
                start = 16 * (4 * d + i)
                a_hi[start : start + 16, cols] = hi
                a_lo[start : start + 16, cols] = lo
    lanes = (((1,), (1,)), ((), ()))
    total = lax.dot_general(a_hi[...], z_hi[...], lanes, preferred_element_type=F32)
    total += lax.dot_general(a_lo[...], z_hi[...], lanes, preferred_element_type=F32)
    total += lax.dot_general(a_hi[...], z_lo[...], lanes, preferred_element_type=F32)
    zpos = lax.broadcasted_iota(jnp.int32, (16, 256), 1) & 3
    weight_z = by_pos(zpos, 1.0 / WEIGHTS)
    for d in range(4):
        for i in range(4):
            start = 16 * (4 * d + i)
            dep_ref[d, i] = total[start : start + 16, :] * weight_z


def finish_kernel(u_ref, rate_ref, dep_ref, top_ref, base_ref, acc_ref, next_ref, vel_ref):
    top = jnp.max(jnp.max(top_ref[...], axis=0, keepdims=True), axis=1, keepdims=True)
    step = 1.0 / (7.0 * jnp.broadcast_to(top, (8, 256)))
    step16 = jnp.concatenate([step, step], axis=0)
    for v in range(5):
        for i in range(4):
            rate = rate_ref[v, i]
            if v > 0:
                rate = rate + dep_ref[v - 1, i]
            next_ref[v, i] = u_ref[v, i] + step16 * rate
    small = step[:, :128]
    for pair in range(14):
        value = base_ref[pair] + small * acc_ref[pair]
        for h in range(2):
            g = 2 * pair + h
            if g < 27:
                vel_ref[g // 9, g // 3 % 3, g % 3] = value[0:3, 64 * h : 64 * h + 64]


def exchanged(up, down, axis, wrap):
    count = lax.axis_size(axis)
    pairs = [(i, (i + 1) % count) for i in range(count if wrap else count - 1)]
    return (
        lax.ppermute(up, axis, pairs),
        lax.ppermute(down, axis, [(j, i) for i, j in pairs]),
    )


def all_tops(top, axes, groups):
    return lax.all_to_all(top, axes, 0, 0, axis_index_groups=groups, tiled=True)


def call(kernel, outs, scratch=()):
    return pl.pallas_call(
        kernel,
        out_shape=outs,
        scratch_shapes=list(scratch),
        compiler_params=pltpu.CompilerParams(vmem_limit_bytes=VMEM_BYTES),
    )


def tiles_of(n):
    return jax.ShapeDtypeStruct((n, 8, 128), F32)


def local(fluid_state, parcel_data, host_element, slot_counts):
    nx, ny, nz = (lax.axis_size(axis) for axis in ("gx", "gy", "gz"))
    spaced = [[x * nz + z for x in range(p, nx, 2) for z in range(nz)] for p in range(2)]
    paired = [[x * ny + y for x in (2 * k, 2 * k + 1) for y in range(ny)] for k in range(nx // 2)]
    row = jax.ShapeDtypeStruct((len(spaced[0]), 128), F32)
    face_up, face_down, faces, top = call(face_kernel, (tiles_of(20), tiles_of(20), tiles_of(14), row))(fluid_state)
    x_up, x_down, keep_x = call(pack_kernel, (tiles_of(29), tiles_of(29), tiles_of(9)))(
        parcel_data, host_element, slot_counts, face_up, face_down
    )
    x1, x2 = exchanged(x_up, x_down, "gx", False)
    tops = all_tops(top, ("gx", "gz"), spaced)
    row = jax.ShapeDtypeStruct((len(paired[0]), 128), F32)
    y_up, y_down, keep_y, top = call(turn_y_kernel, (tiles_of(14), tiles_of(14), tiles_of(9), row))(
        x1, x2, keep_x, faces, tops
    )
    y1, y2 = exchanged(y_up, y_down, "gy", False)
    z_up, z_down, keep_z = call(turn_z_kernel, (tiles_of(11), tiles_of(11), tiles_of(9)))(y1, y2, keep_y, faces)
    z1, z2 = exchanged(z_up, z_down, "gz", True)
    top = all_tops(top, ("gx", "gy"), paired)
    field = jax.ShapeDtypeStruct((5, 4, 16, 256), F32)
    rate = call(
        rate_kernel, field, [pltpu.VMEM((5, 4, 16, 256), F32), pltpu.VMEM((2, 16, 256), F32)],
    )(fluid_state, x1, x2, y1, y2, z1, z2, faces)
    deposit, base, acc = call(
        parcel_kernel,
        (jax.ShapeDtypeStruct((4, 4, 16, 256), F32), tiles_of(14), tiles_of(14)),
        [
            pltpu.VMEM((192, 256), BF16),
            pltpu.VMEM((192, 256), BF16),
            pltpu.VMEM((256, 1792), BF16),
            pltpu.VMEM((256, 1792), BF16),
            pltpu.VMEM((256, 1792), BF16),
            pltpu.VMEM((256, 1792), BF16),
        ],
    )(fluid_state, z1, z2, keep_z)
    return call(finish_kernel, (field, jax.ShapeDtypeStruct((3, 3, 3, 3, 64), F32)))(
        fluid_state, rate, deposit, top, base, acc
    )


def solution(mesh):
    placed = (
        P(None, "gx", "gy", "gz"),
        P("gx", "gy", "gz", None, None),
        P("gx", "gy", "gz", None),
        P("gx", "gy", "gz"),
    )
    return jax.shard_map(
        local,
        mesh=mesh,
        in_specs=placed,
        out_specs=(P(None, "gx", "gy", "gz"), P("gx", "gy", "gz", None, None)),
        check_vma=False,
    )
```

```python
import jax
import jax.numpy as jnp
import numpy as np
from jax import lax
from jax.experimental import pallas as pl
from jax.experimental.pallas import tpu as pltpu
from jax.sharding import PartitionSpec as P

F32 = jnp.float32
BF16 = jnp.bfloat16
VMEM_BYTES = 24 * 1024 * 1024

NODES = np.array([-1.0, -1.0 / np.sqrt(5.0), 1.0 / np.sqrt(5.0), 1.0])
WEIGHTS = np.array([1.0 / 6.0, 5.0 / 6.0, 5.0 / 6.0, 1.0 / 6.0])


def derivative_table():
    factor = [np.prod([NODES[i] - NODES[j] for j in range(4) if j != i]) for i in range(4)]
    table = np.zeros((4, 4))
    for i in range(4):
        for j in range(4):
            if i != j:
                table[i, j] = factor[i] / (factor[j] * (NODES[i] - NODES[j]))
    return table


DERIV = derivative_table()
SCALE = [1.0 / np.prod([NODES[i] - NODES[j] for j in range(4) if j != i]) for i in range(4)]

FACE = 9


def by_pos(pos, values):
    out = jnp.full(pos.shape, float(values[3]), F32)
    for k in range(3):
        out = jnp.where(pos == k, float(values[k]), out)
    return out


def primitives(state):
    inverse = 1.0 / state[0]
    vel = [state[d + 1] * inverse for d in range(3)]
    square = vel[0] * vel[0] + vel[1] * vel[1] + vel[2] * vel[2]
    pressure = 0.4 * (state[4] - 0.5 * state[0] * square)
    sound = jnp.sqrt(1.4 * pressure * inverse)
    return vel, pressure, sound, square


def flux(state, vel, pressure, d):
    normal = vel[d]
    out = [state[d + 1]]
    for k in range(3):
        term = state[k + 1] * normal
        out.append(term + pressure if k == d else term)
    out.append((state[4] + pressure) * normal)
    return out


def side(state, d):
    vel, pressure, sound, _ = primitives(state)
    return flux(state, vel, pressure, d), jnp.abs(vel[d]) + sound


def tile_of(ref):
    return lambda tile: ref[tile]


def face_kernel(u_ref, up_ref, down_ref, face_ref, top_ref):
    top = None
    for i in range(4):
        _, _, sound, square = primitives([u_ref[v, i] for v in range(5)])
        speed = jnp.sqrt(square) + sound
        top = speed if top is None else jnp.maximum(top, speed)
    top = jnp.maximum(top[:, :128], top[:, 128:])
    top_ref[...] = jnp.broadcast_to(jnp.max(top, axis=0, keepdims=True), top_ref.shape)
    for v in range(5):
        for yh in range(2):
            for zh in range(2):
                tile = 4 * v + 2 * yh + zh
                ys, zs = slice(8 * yh, 8 * yh + 8), slice(128 * zh, 128 * zh + 128)
                up_ref[tile] = u_ref[v, 3, ys, zs]
                down_ref[tile] = u_ref[v, 0, ys, zs]
        for i in range(4):
            for zh in range(2):
                zs = slice(128 * zh, 128 * zh + 128)
                row = 4 * zh + i
                face_ref[v, row : row + 1, :] = u_ref[v, i, 15:16, zs]
                face_ref[5 + v, row : row + 1, :] = u_ref[v, i, 0:1, zs]
    lane = lax.broadcasted_iota(jnp.int32, (16, 128), 1)
    high = jnp.zeros((16, 128), F32)
    low = jnp.zeros((16, 128), F32)
    for v in range(5):
        for i in range(4):
            here = lane == 4 * v + i
            high = jnp.where(here, u_ref[v, i, :, 255:256], high)
            low = jnp.where(here, u_ref[v, i, :, 0:1], low)
    for yh in range(2):
        face_ref[10 + yh] = high[8 * yh : 8 * yh + 8]
        face_ref[12 + yh] = low[8 * yh : 8 * yh + 8]


def pack_kernel(data_ref, host_ref, count_ref, face_up_ref, face_down_ref, up_ref, down_ref, keep_ref):
    slot = lax.broadcasted_iota(jnp.int32, (1, 64), 1)
    for a, out in ((2, up_ref), (0, down_ref), (1, keep_ref)):
        for b in range(3):
            for c in range(3):
                count = count_ref[a, b : b + 1, c : c + 1]
                host = host_ref[a, b, c : c + 1, :]
                code = jnp.where(slot < count, host + 1, 0).astype(F32)
                out[3 * b + c, :, 0:64] = data_ref[a, b, c]
                out[3 * b + c, :, 64:128] = jnp.broadcast_to(code, (8, 64))
    for t in range(20):
        up_ref[FACE + t] = face_up_ref[t]
        down_ref[FACE + t] = face_down_ref[t]


def turn_y_kernel(low_ref, high_ref, own_ref, face_ref, tops_ref, up_ref, down_ref, keep_ref, top_ref):
    top_ref[...] = jnp.broadcast_to(jnp.max(tops_ref[...], axis=0, keepdims=True), top_ref.shape)
    for a, source in enumerate((low_ref, own_ref, high_ref)):
        for c in range(3):
            up_ref[3 * a + c] = source[6 + c]
            down_ref[3 * a + c] = source[c]
            keep_ref[3 * a + c] = source[3 + c]
    for v in range(5):
        up_ref[FACE + v] = face_ref[v]
        down_ref[FACE + v] = face_ref[5 + v]


def turn_z_kernel(low_ref, high_ref, own_ref, face_ref, up_ref, down_ref, keep_ref):
    for b, source in enumerate((low_ref, own_ref, high_ref)):
        for a in range(3):
            up_ref[3 * a + b] = source[3 * a + 2]
            down_ref[3 * a + b] = source[3 * a]
            keep_ref[3 * a + b] = source[3 * a + 1]
    for yh in range(2):
        up_ref[FACE + yh] = face_ref[10 + yh]
        down_ref[FACE + yh] = face_ref[12 + yh]


def wall(axis, last, own, received, sign_of):
    at = lax.axis_index(axis) == (lax.axis_size(axis) - 1 if last else 0)
    pick = jnp.full(received[0].shape, at.astype(jnp.int32), jnp.int32) == 1
    return [jnp.where(pick, sign_of(v) * own[v], received[v]) for v in range(5)]


def shift_rate(state, fluxes, speed, low, high, axis, pos, first, last, coef):
    count = state[0].shape[axis]
    low_state, low_flux, low_speed = low
    high_state, high_flux, high_speed = high
    at_low = pos == 0
    ends = at_low | (pos == 3)

    def beside(here, below, above):
        near = jnp.where(at_low, pltpu.roll(here, 1, axis), pltpu.roll(here, count - 1, axis))
        return jnp.where(first, below, jnp.where(last, above, near))

    spread = jnp.maximum(speed, beside(speed, low_speed, high_speed))
    spread = jnp.where(ends, 3.0 * spread, 0.0)
    out = []
    for v in range(5):
        value = fluxes[v]
        above = jnp.where(last, high_flux[v], pltpu.roll(value, count - 1, axis))
        below = jnp.where(first, low_flux[v], pltpu.roll(value, 1, axis))
        total = coef[1] * above + coef[-1] * below
        for d in (-3, -2, 2, 3):
            total = total + coef[d] * pltpu.roll(value, -d % count, axis)
        out.append(spread * (beside(state[v], low_state[v], high_state[v]) - state[v]) - total)
    return out


def rate_kernel(u_ref, x1_ref, x2_ref, y1_ref, y2_ref, z1_ref, z2_ref, face_ref, rate_ref, fx_ref, sx_ref):
    x_side = tile_of(x1_ref), tile_of(x2_ref)
    y_side = tile_of(y1_ref), tile_of(y2_ref)
    z_side = tile_of(z1_ref), tile_of(z2_ref)
    shape = (16, 256)
    row = lax.broadcasted_iota(jnp.int32, shape, 0)
    lane = lax.broadcasted_iota(jnp.int32, shape, 1)
    ypos, zpos = row & 3, lane & 3

    def coefs(pos):
        out = {}
        for d in (-3, -2, -1, 1, 2, 3):
            values = [DERIV[k, k + d] if 0 <= k + d < 4 else 0.0 for k in range(4)]
            if d == 1:
                values[3] = 3.0
            if d == -1:
                values[0] = -3.0
            out[d] = by_pos(pos, values)
        return out

    ycoef, zcoef = coefs(ypos), coefs(zpos)
    yfirst, ylast = row == 0, row == 15
    zfirst, zlast = lane == 0, lane == 255

    yflip = lambda v: -1.0 if v == 2 else 1.0
    ylow = wall("gy", False, [face_ref[5 + v] for v in range(5)], [y_side[0](FACE + v) for v in range(5)], yflip)
    yhigh = wall("gy", True, [face_ref[v] for v in range(5)], [y_side[1](FACE + v) for v in range(5)], yflip)
    ylow_flux, ylow_speed = side(ylow, 1)
    yhigh_flux, yhigh_speed = side(yhigh, 1)

    def columns(first_tile, source):
        both = jnp.concatenate([source(first_tile), source(first_tile + 1)], axis=0)
        return [both if v == 0 else pltpu.roll(both, 128 - 4 * v, 1) for v in range(5)]

    own = tile_of(face_ref)
    zflip = lambda v: -1.0 if v == 3 else 1.0
    zlow = wall("gz", False, columns(12, own), columns(FACE, z_side[0]), zflip)
    zhigh = wall("gz", True, columns(10, own), columns(FACE, z_side[1]), zflip)
    zlow_flux, zlow_speed = side(zlow, 2)
    zhigh_flux, zhigh_speed = side(zhigh, 2)

    def pick_row(tile, i):
        return jnp.concatenate([tile[i : i + 1], tile[4 + i : 5 + i]], axis=1)

    for i in range(4):
        state = [u_ref[v, i] for v in range(5)]
        vel, pressure, sound, _ = primitives(state)
        xflux = flux(state, vel, pressure, 0)
        for v in range(5):
            fx_ref[v, i] = xflux[v]
        if i in (0, 3):
            sx_ref[i // 3] = jnp.abs(vel[0]) + sound
        low = ([pick_row(t, i) for t in ylow], [pick_row(t, i) for t in ylow_flux], pick_row(ylow_speed, i))
        high = ([pick_row(t, i) for t in yhigh], [pick_row(t, i) for t in yhigh_flux], pick_row(yhigh_speed, i))
        yrate = shift_rate(
            state, flux(state, vel, pressure, 1), jnp.abs(vel[1]) + sound,
            low, high, 0, ypos, yfirst, ylast, ycoef,
        )
        pick = lambda t: t[:, i : i + 1]
        low = ([pick(t) for t in zlow], [pick(t) for t in zlow_flux], pick(zlow_speed))
        high = ([pick(t) for t in zhigh], [pick(t) for t in zhigh_flux], pick(zhigh_speed))
        zrate = shift_rate(
            state, flux(state, vel, pressure, 2), jnp.abs(vel[2]) + sound,
            low, high, 1, zpos, zfirst, zlast, zcoef,
        )
        for v in range(5):
            rate_ref[v, i] = yrate[v] + zrate[v]

    xflip = lambda v: -1.0 if v == 1 else 1.0
    for half in range(2):
        for part in range(2):
            ys, zs = slice(8 * half, 8 * half + 8), slice(128 * part, 128 * part + 128)
            tile = FACE + 2 * half + part
            ends = []
            for last, i, source in ((False, 0, x_side[0]), (True, 3, x_side[1])):
                mine = [u_ref[v, i, ys, zs] for v in range(5)]
                beyond = wall("gx", last, mine, [source(tile + 4 * v) for v in range(5)], xflip)
                far_flux, far_speed = side(beyond, 0)
                spread = 3.0 * jnp.maximum(sx_ref[i // 3, ys, zs], far_speed)
                sign = -3.0 if last else 3.0
                ends.append([sign * far_flux[v] + spread * (beyond[v] - mine[v]) for v in range(5)])
            for v in range(5):
                f = [fx_ref[v, i, ys, zs] for i in range(4)]
                for j in range(4):
                    total = rate_ref[v, j, ys, zs]
                    for i in range(4):
                        if i != j:
                            total = total - float(DERIV[j, i]) * f[i]
                    if j == 0:
                        total = total + ends[0][v]
                    if j == 3:
                        total = total + ends[1][v]
                    rate_ref[v, j, ys, zs] = total


def split(value):
    high = value.astype(BF16)
    return high, (value - high.astype(F32)).astype(BF16)


def parcel_kernel(u_ref, z1_ref, z2_ref, own_ref, dep_ref, base_ref, acc_ref, vel_hi, vel_lo, z_hi, z_lo, a_hi, a_lo):
    sides = (z1_ref, own_ref, z2_ref)
    tiles = [sides[g % 3][g // 3] for g in range(27)] + [jnp.zeros((8, 128), F32)]
    for i in range(4):
        inverse = 1.0 / u_ref[0, i]
        for d in range(3):
            hi, lo = split(u_ref[d + 1, i] * inverse)
            start = 16 * (4 * d + i)
            vel_hi[start : start + 16, :] = hi
            vel_lo[start : start + 16, :] = lo
    left = lax.broadcasted_iota(jnp.int32, (8, 128), 1) < 64
    sub8 = lax.broadcasted_iota(jnp.int32, (8, 128), 0)
    sub16 = lax.broadcasted_iota(jnp.int32, (16, 128), 0)
    pos, block = sub16 & 3, sub16 >> 2
    weight_y = by_pos(pos, 1.0 / WEIGHTS)
    weight_xy = [weight_y * float(1.0 / WEIGHTS[i]) for i in range(4)]
    inner = float(NODES[2])
    kept = []
    for p in range(14):
        first, second = tiles[2 * p], tiles[2 * p + 1]
        field = jnp.where(left, first, pltpu.roll(second, 64, 1))
        code = jnp.where(left, pltpu.roll(first, 64, 1), second)
        host = code.astype(jnp.int32) - 1
        host = jnp.concatenate([host, host], axis=0)
        outer = (field + 1.0) * (field - 1.0)
        middle = (field + inner) * (field - inner)
        basis = [
            float(SCALE[0]) * middle * (field - 1.0),
            float(SCALE[1]) * outer * (field - inner),
            float(SCALE[2]) * outer * (field + inner),
            float(SCALE[3]) * middle * (field + 1.0),
        ]

        def spread(r):
            rows = [jnp.broadcast_to(basis[k][r : r + 1], (16, 128)) for k in range(4)]
            return jnp.where(pos == 0, rows[0], jnp.where(pos == 1, rows[1], jnp.where(pos == 2, rows[2], rows[3])))

        in_y = jnp.where((host >> 6) == block, spread(1), 0.0)
        in_z = spread(2)
        in_z_hi = in_z.astype(BF16).astype(F32)
        in_z_lo = in_z - in_z_hi
        offset = (host & 63) - block
        cols = slice(128 * p, 128 * p + 128)
        for t in range(16):
            here = offset == 4 * t
            z_hi[16 * t : 16 * t + 16, cols] = jnp.where(here, in_z_hi, 0.0).astype(BF16)
            z_lo[16 * t : 16 * t + 16, cols] = jnp.where(here, in_z_lo, 0.0).astype(BF16)
        kept.append((field, code, [basis[i][0:1] for i in range(4)], in_y))
    wide = jnp.dot(vel_hi[...], z_hi[...], preferred_element_type=F32)
    wide += jnp.dot(vel_lo[...], z_hi[...], preferred_element_type=F32)
    wide += jnp.dot(vel_hi[...], z_lo[...], preferred_element_type=F32)
    for p in range(14):
        field, code, in_x, in_y = kept[p]
        cols = slice(128 * p, 128 * p + 128)
        live = code > 0.5
        in_xy = [in_x[i] * in_y for i in range(4)]
        seen = []
        for d in range(3):
            mixed = None
            for i in range(4):
                start = 16 * (4 * d + i)
                term = in_xy[i] * wide[start : start + 16, cols]
                mixed = term if mixed is None else mixed + term
            seen.append(jnp.sum(mixed, axis=0, keepdims=True))
        fluid = jnp.where(sub8 == 0, seen[0], jnp.where(sub8 == 1, seen[1], seen[2]))
        speed = pltpu.roll(field, 5, 0)
        keep = live & (sub8 < 3)
        relax = jnp.where(live[0:1], field[6:7], 1.0)
        force = jnp.where(keep, (fluid - speed) / relax, 0.0)
        base = jnp.where(keep, speed, 0.0)
        base_ref[p] = base
        acc_ref[p] = force
        mass = field[7:8]
        push = -mass * force
        work = -mass * jnp.sum(force * base, axis=0, keepdims=True)
        sources = [push[0:1], push[1:2], push[2:3], work]
        for i in range(4):
            scaled = in_xy[i] * weight_xy[i]
            for d in range(4):
                hi, lo = split(sources[d] * scaled)
                start = 16 * (4 * d + i)
                a_hi[start : start + 16, cols] = hi
                a_lo[start : start + 16, cols] = lo
    lanes = (((1,), (1,)), ((), ()))
    total = lax.dot_general(a_hi[...], z_hi[...], lanes, preferred_element_type=F32)
    total += lax.dot_general(a_lo[...], z_hi[...], lanes, preferred_element_type=F32)
    total += lax.dot_general(a_hi[...], z_lo[...], lanes, preferred_element_type=F32)
    zpos = lax.broadcasted_iota(jnp.int32, (16, 256), 1) & 3
    weight_z = by_pos(zpos, 1.0 / WEIGHTS)
    for d in range(4):
        for i in range(4):
            start = 16 * (4 * d + i)
            dep_ref[d, i] = total[start : start + 16, :] * weight_z


def finish_kernel(u_ref, rate_ref, dep_ref, top_ref, base_ref, acc_ref, next_ref, vel_ref):
    top = jnp.max(jnp.max(top_ref[...], axis=0, keepdims=True), axis=1, keepdims=True)
    step = 1.0 / (7.0 * jnp.broadcast_to(top, (8, 256)))
    step16 = jnp.concatenate([step, step], axis=0)
    for v in range(5):
        for i in range(4):
            rate = rate_ref[v, i]
            if v > 0:
                rate = rate + dep_ref[v - 1, i]
            next_ref[v, i] = u_ref[v, i] + step16 * rate
    small = step[:, :128]
    for pair in range(14):
        value = base_ref[pair] + small * acc_ref[pair]
        for h in range(2):
            g = 2 * pair + h
            if g < 27:
                vel_ref[g // 9, g // 3 % 3, g % 3] = value[0:3, 64 * h : 64 * h + 64]


def exchanged(up, down, axis, wrap):
    count = lax.axis_size(axis)
    pairs = [(i, (i + 1) % count) for i in range(count if wrap else count - 1)]
    return (
        lax.ppermute(up, axis, pairs),
        lax.ppermute(down, axis, [(j, i) for i, j in pairs]),
    )


def all_tops(top, axes, groups):
    return lax.all_to_all(top, axes, 0, 0, axis_index_groups=groups, tiled=True)


def call(kernel, outs, scratch=()):
    return pl.pallas_call(
        kernel,
        out_shape=outs,
        scratch_shapes=list(scratch),
        compiler_params=pltpu.CompilerParams(vmem_limit_bytes=VMEM_BYTES),
    )


def tiles_of(n):
    return jax.ShapeDtypeStruct((n, 8, 128), F32)


def local(fluid_state, parcel_data, host_element, slot_counts):
    nx, ny, nz = (lax.axis_size(axis) for axis in ("gx", "gy", "gz"))
    spaced = [[x * ny + y for x in range(p, nx, 2) for y in range(ny)] for p in range(2)]
    paired = [[x * nz + z for x in (2 * k, 2 * k + 1) for z in range(nz)] for k in range(nx // 2)]
    row = jax.ShapeDtypeStruct((len(spaced[0]), 128), F32)
    face_up, face_down, faces, top = call(face_kernel, (tiles_of(20), tiles_of(20), tiles_of(14), row))(fluid_state)
    x_up, x_down, keep_x = call(pack_kernel, (tiles_of(29), tiles_of(29), tiles_of(9)))(
        parcel_data, host_element, slot_counts, face_up, face_down
    )
    x1, x2 = exchanged(x_up, x_down, "gx", False)
    tops = all_tops(top, ("gx", "gy"), spaced)
    row = jax.ShapeDtypeStruct((len(paired[0]), 128), F32)
    y_up, y_down, keep_y, top = call(turn_y_kernel, (tiles_of(14), tiles_of(14), tiles_of(9), row))(
        x1, x2, keep_x, faces, tops
    )
    y1, y2 = exchanged(y_up, y_down, "gy", False)
    z_up, z_down, keep_z = call(turn_z_kernel, (tiles_of(11), tiles_of(11), tiles_of(9)))(y1, y2, keep_y, faces)
    z1, z2 = exchanged(z_up, z_down, "gz", True)
    top = all_tops(top, ("gx", "gz"), paired)
    field = jax.ShapeDtypeStruct((5, 4, 16, 256), F32)
    rate = call(
        rate_kernel, field, [pltpu.VMEM((5, 4, 16, 256), F32), pltpu.VMEM((2, 16, 256), F32)],
    )(fluid_state, x1, x2, y1, y2, z1, z2, faces)
    deposit, base, acc = call(
        parcel_kernel,
        (jax.ShapeDtypeStruct((4, 4, 16, 256), F32), tiles_of(14), tiles_of(14)),
        [
            pltpu.VMEM((192, 256), BF16),
            pltpu.VMEM((192, 256), BF16),
            pltpu.VMEM((256, 1792), BF16),
            pltpu.VMEM((256, 1792), BF16),
            pltpu.VMEM((256, 1792), BF16),
            pltpu.VMEM((256, 1792), BF16),
        ],
    )(fluid_state, z1, z2, keep_z)
    return call(finish_kernel, (field, jax.ShapeDtypeStruct((3, 3, 3, 3, 64), F32)))(
        fluid_state, rate, deposit, top, base, acc
    )


def solution(mesh):
    placed = (
        P(None, "gx", "gy", "gz"),
        P("gx", "gy", "gz", None, None),
        P("gx", "gy", "gz", None),
        P("gx", "gy", "gz"),
    )
    return jax.shard_map(
        local,
        mesh=mesh,
        in_specs=placed,
        out_specs=(P(None, "gx", "gy", "gz"), P("gx", "gy", "gz", None, None)),
        check_vma=False,
    )
```

```python
import jax
import jax.numpy as jnp
import numpy as np
from jax import lax
from jax.experimental import pallas as pl
from jax.experimental.pallas import tpu as pltpu
from jax.sharding import PartitionSpec as P

F32 = jnp.float32
BF16 = jnp.bfloat16
VMEM_BYTES = 24 * 1024 * 1024

NODES = np.array([-1.0, -1.0 / np.sqrt(5.0), 1.0 / np.sqrt(5.0), 1.0])
WEIGHTS = np.array([1.0 / 6.0, 5.0 / 6.0, 5.0 / 6.0, 1.0 / 6.0])


def derivative_table():
    factor = [np.prod([NODES[i] - NODES[j] for j in range(4) if j != i]) for i in range(4)]
    table = np.zeros((4, 4))
    for i in range(4):
        for j in range(4):
            if i != j:
                table[i, j] = factor[i] / (factor[j] * (NODES[i] - NODES[j]))
    return table


DERIV = derivative_table()
SCALE = [1.0 / np.prod([NODES[i] - NODES[j] for j in range(4) if j != i]) for i in range(4)]

FACE = 9


def by_pos(pos, values):
    out = jnp.full(pos.shape, float(values[3]), F32)
    for k in range(3):
        out = jnp.where(pos == k, float(values[k]), out)
    return out


def primitives(state):
    inverse = 1.0 / state[0]
    vel = [state[d + 1] * inverse for d in range(3)]
    square = vel[0] * vel[0] + vel[1] * vel[1] + vel[2] * vel[2]
    pressure = 0.4 * (state[4] - 0.5 * state[0] * square)
    sound = jnp.sqrt(1.4 * pressure * inverse)
    return vel, pressure, sound, square


def flux(state, vel, pressure, d):
    normal = vel[d]
    out = [state[d + 1]]
    for k in range(3):
        term = state[k + 1] * normal
        out.append(term + pressure if k == d else term)
    out.append((state[4] + pressure) * normal)
    return out


def side(state, d):
    vel, pressure, sound, _ = primitives(state)
    return flux(state, vel, pressure, d), jnp.abs(vel[d]) + sound


def tile_of(ref):
    return lambda tile: ref[tile]


def face_kernel(u_ref, up_ref, down_ref, face_ref, top_ref):
    top = None
    for i in range(4):
        _, _, sound, square = primitives([u_ref[v, i] for v in range(5)])
        speed = jnp.sqrt(square) + sound
        top = speed if top is None else jnp.maximum(top, speed)
    top = jnp.maximum(top[:, :128], top[:, 128:])
    top_ref[...] = jnp.broadcast_to(jnp.max(top, axis=0, keepdims=True), top_ref.shape)
    for v in range(5):
        for yh in range(2):
            for zh in range(2):
                tile = 4 * v + 2 * yh + zh
                ys, zs = slice(8 * yh, 8 * yh + 8), slice(128 * zh, 128 * zh + 128)
                up_ref[tile] = u_ref[v, 3, ys, zs]
                down_ref[tile] = u_ref[v, 0, ys, zs]
        for i in range(4):
            for zh in range(2):
                zs = slice(128 * zh, 128 * zh + 128)
                row = 4 * zh + i
                face_ref[v, row : row + 1, :] = u_ref[v, i, 15:16, zs]
                face_ref[5 + v, row : row + 1, :] = u_ref[v, i, 0:1, zs]
    lane = lax.broadcasted_iota(jnp.int32, (16, 128), 1)
    high = jnp.zeros((16, 128), F32)
    low = jnp.zeros((16, 128), F32)
    for v in range(5):
        for i in range(4):
            here = lane == 4 * v + i
            high = jnp.where(here, u_ref[v, i, :, 255:256], high)
            low = jnp.where(here, u_ref[v, i, :, 0:1], low)
    for yh in range(2):
        face_ref[10 + yh] = high[8 * yh : 8 * yh + 8]
        face_ref[12 + yh] = low[8 * yh : 8 * yh + 8]


def pack_kernel(data_ref, host_ref, count_ref, face_up_ref, face_down_ref, up_ref, down_ref, keep_ref):
    slot = lax.broadcasted_iota(jnp.int32, (1, 64), 1)
    for a, out in ((2, up_ref), (0, down_ref), (1, keep_ref)):
        for b in range(3):
            for c in range(3):
                count = count_ref[a, b : b + 1, c : c + 1]
                host = host_ref[a, b, c : c + 1, :]
                code = jnp.where(slot < count, host + 1, 0).astype(F32)
                out[3 * b + c, :, 0:64] = data_ref[a, b, c]
                out[3 * b + c, :, 64:128] = jnp.broadcast_to(code, (8, 64))
    for t in range(20):
        up_ref[FACE + t] = face_up_ref[t]
        down_ref[FACE + t] = face_down_ref[t]


def turn_z_kernel(low_ref, high_ref, own_ref, face_ref, tops_ref, up_ref, down_ref, keep_ref, top_ref):
    top_ref[...] = jnp.broadcast_to(jnp.max(tops_ref[...], axis=0, keepdims=True), top_ref.shape)
    for a, source in enumerate((low_ref, own_ref, high_ref)):
        for b in range(3):
            up_ref[3 * a + b] = source[3 * b + 2]
            down_ref[3 * a + b] = source[3 * b]
            keep_ref[3 * a + b] = source[3 * b + 1]
    for yh in range(2):
        up_ref[FACE + yh] = face_ref[10 + yh]
        down_ref[FACE + yh] = face_ref[12 + yh]


def turn_y_kernel(low_ref, high_ref, own_ref, face_ref, up_ref, down_ref, keep_ref):
    for c, source in enumerate((low_ref, own_ref, high_ref)):
        for a in range(3):
            up_ref[3 * a + c] = source[3 * a + 2]
            down_ref[3 * a + c] = source[3 * a]
            keep_ref[3 * a + c] = source[3 * a + 1]
    for v in range(5):
        up_ref[FACE + v] = face_ref[v]
        down_ref[FACE + v] = face_ref[5 + v]


def wall(axis, last, own, received, sign_of):
    at = lax.axis_index(axis) == (lax.axis_size(axis) - 1 if last else 0)
    pick = jnp.full(received[0].shape, at.astype(jnp.int32), jnp.int32) == 1
    return [jnp.where(pick, sign_of(v) * own[v], received[v]) for v in range(5)]


def shift_rate(state, fluxes, speed, low, high, axis, pos, first, last, coef):
    count = state[0].shape[axis]
    low_state, low_flux, low_speed = low
    high_state, high_flux, high_speed = high
    at_low = pos == 0
    ends = at_low | (pos == 3)

    def beside(here, below, above):
        near = jnp.where(at_low, pltpu.roll(here, 1, axis), pltpu.roll(here, count - 1, axis))
        return jnp.where(first, below, jnp.where(last, above, near))

    spread = jnp.maximum(speed, beside(speed, low_speed, high_speed))
    spread = jnp.where(ends, 3.0 * spread, 0.0)
    out = []
    for v in range(5):
        value = fluxes[v]
        above = jnp.where(last, high_flux[v], pltpu.roll(value, count - 1, axis))
        below = jnp.where(first, low_flux[v], pltpu.roll(value, 1, axis))
        total = coef[1] * above + coef[-1] * below
        for d in (-3, -2, 2, 3):
            total = total + coef[d] * pltpu.roll(value, -d % count, axis)
        out.append(spread * (beside(state[v], low_state[v], high_state[v]) - state[v]) - total)
    return out


def rate_kernel(u_ref, x1_ref, x2_ref, y1_ref, y2_ref, z1_ref, z2_ref, face_ref, rate_ref, fx_ref, sx_ref):
    x_side = tile_of(x1_ref), tile_of(x2_ref)
    y_side = tile_of(y1_ref), tile_of(y2_ref)
    z_side = tile_of(z1_ref), tile_of(z2_ref)
    shape = (16, 256)
    row = lax.broadcasted_iota(jnp.int32, shape, 0)
    lane = lax.broadcasted_iota(jnp.int32, shape, 1)
    ypos, zpos = row & 3, lane & 3

    def coefs(pos):
        out = {}
        for d in (-3, -2, -1, 1, 2, 3):
            values = [DERIV[k, k + d] if 0 <= k + d < 4 else 0.0 for k in range(4)]
            if d == 1:
                values[3] = 3.0
            if d == -1:
                values[0] = -3.0
            out[d] = by_pos(pos, values)
        return out

    ycoef, zcoef = coefs(ypos), coefs(zpos)
    yfirst, ylast = row == 0, row == 15
    zfirst, zlast = lane == 0, lane == 255

    yflip = lambda v: -1.0 if v == 2 else 1.0
    ylow = wall("gy", False, [face_ref[5 + v] for v in range(5)], [y_side[0](FACE + v) for v in range(5)], yflip)
    yhigh = wall("gy", True, [face_ref[v] for v in range(5)], [y_side[1](FACE + v) for v in range(5)], yflip)
    ylow_flux, ylow_speed = side(ylow, 1)
    yhigh_flux, yhigh_speed = side(yhigh, 1)

    def columns(first_tile, source):
        both = jnp.concatenate([source(first_tile), source(first_tile + 1)], axis=0)
        return [both if v == 0 else pltpu.roll(both, 128 - 4 * v, 1) for v in range(5)]

    own = tile_of(face_ref)
    zflip = lambda v: -1.0 if v == 3 else 1.0
    zlow = wall("gz", False, columns(12, own), columns(FACE, z_side[0]), zflip)
    zhigh = wall("gz", True, columns(10, own), columns(FACE, z_side[1]), zflip)
    zlow_flux, zlow_speed = side(zlow, 2)
    zhigh_flux, zhigh_speed = side(zhigh, 2)

    def pick_row(tile, i):
        return jnp.concatenate([tile[i : i + 1], tile[4 + i : 5 + i]], axis=1)

    for i in range(4):
        state = [u_ref[v, i] for v in range(5)]
        vel, pressure, sound, _ = primitives(state)
        xflux = flux(state, vel, pressure, 0)
        for v in range(5):
            fx_ref[v, i] = xflux[v]
        if i in (0, 3):
            sx_ref[i // 3] = jnp.abs(vel[0]) + sound
        low = ([pick_row(t, i) for t in ylow], [pick_row(t, i) for t in ylow_flux], pick_row(ylow_speed, i))
        high = ([pick_row(t, i) for t in yhigh], [pick_row(t, i) for t in yhigh_flux], pick_row(yhigh_speed, i))
        yrate = shift_rate(
            state, flux(state, vel, pressure, 1), jnp.abs(vel[1]) + sound,
            low, high, 0, ypos, yfirst, ylast, ycoef,
        )
        pick = lambda t: t[:, i : i + 1]
        low = ([pick(t) for t in zlow], [pick(t) for t in zlow_flux], pick(zlow_speed))
        high = ([pick(t) for t in zhigh], [pick(t) for t in zhigh_flux], pick(zhigh_speed))
        zrate = shift_rate(
            state, flux(state, vel, pressure, 2), jnp.abs(vel[2]) + sound,
            low, high, 1, zpos, zfirst, zlast, zcoef,
        )
        for v in range(5):
            rate_ref[v, i] = yrate[v] + zrate[v]

    xflip = lambda v: -1.0 if v == 1 else 1.0
    for half in range(2):
        for part in range(2):
            ys, zs = slice(8 * half, 8 * half + 8), slice(128 * part, 128 * part + 128)
            tile = FACE + 2 * half + part
            ends = []
            for last, i, source in ((False, 0, x_side[0]), (True, 3, x_side[1])):
                mine = [u_ref[v, i, ys, zs] for v in range(5)]
                beyond = wall("gx", last, mine, [source(tile + 4 * v) for v in range(5)], xflip)
                far_flux, far_speed = side(beyond, 0)
                spread = 3.0 * jnp.maximum(sx_ref[i // 3, ys, zs], far_speed)
                sign = -3.0 if last else 3.0
                ends.append([sign * far_flux[v] + spread * (beyond[v] - mine[v]) for v in range(5)])
            for v in range(5):
                f = [fx_ref[v, i, ys, zs] for i in range(4)]
                for j in range(4):
                    total = rate_ref[v, j, ys, zs]
                    for i in range(4):
                        if i != j:
                            total = total - float(DERIV[j, i]) * f[i]
                    if j == 0:
                        total = total + ends[0][v]
                    if j == 3:
                        total = total + ends[1][v]
                    rate_ref[v, j, ys, zs] = total


def split(value):
    high = value.astype(BF16)
    return high, (value - high.astype(F32)).astype(BF16)


def parcel_kernel(u_ref, y1_ref, y2_ref, own_ref, dep_ref, base_ref, acc_ref, vel_hi, vel_lo, z_hi, z_lo, a_hi, a_lo):
    sides = (y1_ref, own_ref, y2_ref)
    tiles = [sides[g // 3 % 3][3 * (g // 9) + g % 3] for g in range(27)] + [jnp.zeros((8, 128), F32)]
    for i in range(4):
        inverse = 1.0 / u_ref[0, i]
        for d in range(3):
            hi, lo = split(u_ref[d + 1, i] * inverse)
            start = 16 * (4 * d + i)
            vel_hi[start : start + 16, :] = hi
            vel_lo[start : start + 16, :] = lo
    left = lax.broadcasted_iota(jnp.int32, (8, 128), 1) < 64
    sub8 = lax.broadcasted_iota(jnp.int32, (8, 128), 0)
    sub16 = lax.broadcasted_iota(jnp.int32, (16, 128), 0)
    pos, block = sub16 & 3, sub16 >> 2
    weight_y = by_pos(pos, 1.0 / WEIGHTS)
    weight_xy = [weight_y * float(1.0 / WEIGHTS[i]) for i in range(4)]
    inner = float(NODES[2])
    kept = []
    for p in range(14):
        first, second = tiles[2 * p], tiles[2 * p + 1]
        field = jnp.where(left, first, pltpu.roll(second, 64, 1))
        code = jnp.where(left, pltpu.roll(first, 64, 1), second)
        host = code.astype(jnp.int32) - 1
        host = jnp.concatenate([host, host], axis=0)
        outer = (field + 1.0) * (field - 1.0)
        middle = (field + inner) * (field - inner)
        basis = [
            float(SCALE[0]) * middle * (field - 1.0),
            float(SCALE[1]) * outer * (field - inner),
            float(SCALE[2]) * outer * (field + inner),
            float(SCALE[3]) * middle * (field + 1.0),
        ]

        def spread(r):
            rows = [jnp.broadcast_to(basis[k][r : r + 1], (16, 128)) for k in range(4)]
            return jnp.where(pos == 0, rows[0], jnp.where(pos == 1, rows[1], jnp.where(pos == 2, rows[2], rows[3])))

        in_y = jnp.where((host >> 6) == block, spread(1), 0.0)
        in_z = spread(2)
        in_z_hi = in_z.astype(BF16).astype(F32)
        in_z_lo = in_z - in_z_hi
        offset = (host & 63) - block
        cols = slice(128 * p, 128 * p + 128)
        for t in range(16):
            here = offset == 4 * t
            z_hi[16 * t : 16 * t + 16, cols] = jnp.where(here, in_z_hi, 0.0).astype(BF16)
            z_lo[16 * t : 16 * t + 16, cols] = jnp.where(here, in_z_lo, 0.0).astype(BF16)
        kept.append((field, code, [basis[i][0:1] for i in range(4)], in_y))
    wide = jnp.dot(vel_hi[...], z_hi[...], preferred_element_type=F32)
    wide += jnp.dot(vel_lo[...], z_hi[...], preferred_element_type=F32)
    wide += jnp.dot(vel_hi[...], z_lo[...], preferred_element_type=F32)
    for p in range(14):
        field, code, in_x, in_y = kept[p]
        cols = slice(128 * p, 128 * p + 128)
        live = code > 0.5
        in_xy = [in_x[i] * in_y for i in range(4)]
        seen = []
        for d in range(3):
            mixed = None
            for i in range(4):
                start = 16 * (4 * d + i)
                term = in_xy[i] * wide[start : start + 16, cols]
                mixed = term if mixed is None else mixed + term
            seen.append(jnp.sum(mixed, axis=0, keepdims=True))
        fluid = jnp.where(sub8 == 0, seen[0], jnp.where(sub8 == 1, seen[1], seen[2]))
        speed = pltpu.roll(field, 5, 0)
        keep = live & (sub8 < 3)
        relax = jnp.where(live[0:1], field[6:7], 1.0)
        force = jnp.where(keep, (fluid - speed) / relax, 0.0)
        base = jnp.where(keep, speed, 0.0)
        base_ref[p] = base
        acc_ref[p] = force
        mass = field[7:8]
        push = -mass * force
        work = -mass * jnp.sum(force * base, axis=0, keepdims=True)
        sources = [push[0:1], push[1:2], push[2:3], work]
        for i in range(4):
            scaled = in_xy[i] * weight_xy[i]
            for d in range(4):
                hi, lo = split(sources[d] * scaled)
                start = 16 * (4 * d + i)
                a_hi[start : start + 16, cols] = hi
                a_lo[start : start + 16, cols] = lo
    lanes = (((1,), (1,)), ((), ()))
    total = lax.dot_general(a_hi[...], z_hi[...], lanes, preferred_element_type=F32)
    total += lax.dot_general(a_lo[...], z_hi[...], lanes, preferred_element_type=F32)
    total += lax.dot_general(a_hi[...], z_lo[...], lanes, preferred_element_type=F32)
    zpos = lax.broadcasted_iota(jnp.int32, (16, 256), 1) & 3
    weight_z = by_pos(zpos, 1.0 / WEIGHTS)
    for d in range(4):
        for i in range(4):
            start = 16 * (4 * d + i)
            dep_ref[d, i] = total[start : start + 16, :] * weight_z


def finish_kernel(u_ref, rate_ref, dep_ref, top_ref, base_ref, acc_ref, next_ref, vel_ref):
    top = jnp.max(jnp.max(top_ref[...], axis=0, keepdims=True), axis=1, keepdims=True)
    step = 1.0 / (7.0 * jnp.broadcast_to(top, (8, 256)))
    step16 = jnp.concatenate([step, step], axis=0)
    for v in range(5):
        for i in range(4):
            rate = rate_ref[v, i]
            if v > 0:
                rate = rate + dep_ref[v - 1, i]
            next_ref[v, i] = u_ref[v, i] + step16 * rate
    small = step[:, :128]
    for pair in range(14):
        value = base_ref[pair] + small * acc_ref[pair]
        for h in range(2):
            g = 2 * pair + h
            if g < 27:
                vel_ref[g // 9, g // 3 % 3, g % 3] = value[0:3, 64 * h : 64 * h + 64]


def exchanged(up, down, axis, wrap):
    count = lax.axis_size(axis)
    pairs = [(i, (i + 1) % count) for i in range(count if wrap else count - 1)]
    return (
        lax.ppermute(up, axis, pairs),
        lax.ppermute(down, axis, [(j, i) for i, j in pairs]),
    )


def all_tops(top, axis):
    return lax.all_to_all(top, axis, 0, 0, tiled=True)


def call(kernel, outs, scratch=()):
    return pl.pallas_call(
        kernel,
        out_shape=outs,
        scratch_shapes=list(scratch),
        compiler_params=pltpu.CompilerParams(vmem_limit_bytes=VMEM_BYTES),
    )


def tiles_of(n):
    return jax.ShapeDtypeStruct((n, 8, 128), F32)


def local(fluid_state, parcel_data, host_element, slot_counts):
    planes = lax.axis_size("gx") * lax.axis_size("gy")
    row = jax.ShapeDtypeStruct((planes, 128), F32)
    face_up, face_down, faces, top = call(face_kernel, (tiles_of(20), tiles_of(20), tiles_of(14), row))(fluid_state)
    x_up, x_down, keep_x = call(pack_kernel, (tiles_of(29), tiles_of(29), tiles_of(9)))(
        parcel_data, host_element, slot_counts, face_up, face_down
    )
    x1, x2 = exchanged(x_up, x_down, "gx", False)
    tops = all_tops(top, ("gx", "gy"))
    row = jax.ShapeDtypeStruct((lax.axis_size("gz"), 128), F32)
    z_up, z_down, keep_z, top = call(turn_z_kernel, (tiles_of(11), tiles_of(11), tiles_of(9), row))(
        x1, x2, keep_x, faces, tops
    )
    z1, z2 = exchanged(z_up, z_down, "gz", True)
    y_up, y_down, keep_y = call(turn_y_kernel, (tiles_of(14), tiles_of(14), tiles_of(9)))(z1, z2, keep_z, faces)
    y1, y2 = exchanged(y_up, y_down, "gy", False)
    top = all_tops(top, "gz")
    field = jax.ShapeDtypeStruct((5, 4, 16, 256), F32)
    rate = call(
        rate_kernel, field, [pltpu.VMEM((5, 4, 16, 256), F32), pltpu.VMEM((2, 16, 256), F32)],
    )(fluid_state, x1, x2, y1, y2, z1, z2, faces)
    deposit, base, acc = call(
        parcel_kernel,
        (jax.ShapeDtypeStruct((4, 4, 16, 256), F32), tiles_of(14), tiles_of(14)),
        [
            pltpu.VMEM((192, 256), BF16),
            pltpu.VMEM((192, 256), BF16),
            pltpu.VMEM((256, 1792), BF16),
            pltpu.VMEM((256, 1792), BF16),
            pltpu.VMEM((256, 1792), BF16),
            pltpu.VMEM((256, 1792), BF16),
        ],
    )(fluid_state, y1, y2, keep_y)
    return call(finish_kernel, (field, jax.ShapeDtypeStruct((3, 3, 3, 3, 64), F32)))(
        fluid_state, rate, deposit, top, base, acc
    )


def solution(mesh):
    placed = (
        P(None, "gx", "gy", "gz"),
        P("gx", "gy", "gz", None, None),
        P("gx", "gy", "gz", None),
        P("gx", "gy", "gz"),
    )
    return jax.shard_map(
        local,
        mesh=mesh,
        in_specs=placed,
        out_specs=(P(None, "gx", "gy", "gz"), P("gx", "gy", "gz", None, None)),
        check_vma=False,
    )
```
